256 devices in a mesh: flop: 64 (over z, x, core), turn: 4 (over y).
Axes of the slice: x: 4, y: 4, z: 8, core: 2. Of those that a mesh axis runs over, the one named last changes fastest.
Arguments:
- ranges: float32 [2, 1326], replicated, may hold values from 0.05 to 1
- flop_regret: float32 [64, 4, 1326], P('flop'), may hold values from 0.01 to 1
- flop_cards: int32 [64, 3], P('flop'), may hold values from 0 to 51, as said below
- live_turns: int32 [64, 4], P('flop'), may hold values from 1 to 24, as said below
- turn_card: int32 [64, 96], P('flop', 'turn'), may hold values from 0 to 51, as said below
- river_cards: int32 [64, 96, 2], P('flop', 'turn'), may hold values from 0 to 51, as said below
- strength: float32 [64, 96, 2, 1326], P('flop', 'turn'), may hold values from 0 to 1
- turn_regret: float32 [64, 96, 4, 4, 1326], P('flop', 'turn'), may hold values from 0.01 to 1
Outputs:
- new_flop_regret: float32 [64, 4, 1326], P('flop')
- new_turn_regret: float32 [64, 96, 4, 4, 1326], P('flop', 'turn')
- root_value: float32 [2, 1326], replicated
The draws below stay inside these ranges and needn't reach their ends.
Inputs may be any that keep to these rules, and one draw needn't show every extreme that they name: `live_turns`: for each flop the 4 counts add up to 49, one device holds exactly 24, and the counts of the other devices differ from one another by at most one. `flop_cards`: three different cards. `turn_card`: the live slots of one flop hold its 49 turn cards, all different and none on the flop. `river_cards`: the rivers of a slot differ from one another, from the flop and from the slot's turn card.
All inputs are finite; a program needn't handle non-finite values.
Results may differ from the reference program's by a relative error of at most 0.0003.
Values sent between devices are 32-bit elements; how exact they have to be, the bound alone decides.
No kernel may reach another device: no remote copies, remote signals or barrier semaphores. Data moves between devices by JAX's collectives and lax.ppermute only.
A program may use at most 64 MiB of HBM per device.

```python
import math
import jax
import jax.numpy as jnp
import numpy as np
from jax import lax

CARDS = 52
H = 1326
A = 4
TURNS = 49
TS = 24
RIV = 2
FLOPS = 64
N_TURN = 4


def deal(key):
    first_key, second_key, third_key = jax.random.split(key, 3)
    offset = jax.random.randint(first_key, (), 0, N_TURN)
    heavy = ((offset + jnp.arange(FLOPS, dtype=jnp.int32)) % N_TURN)[:, None]
    rotation = jax.random.randint(second_key, (FLOPS, 1), 0, N_TURN - 1)
    remain = TURNS - TS
    base = remain // (N_TURN - 1)
    spare = remain % (N_TURN - 1)
    device = jnp.arange(N_TURN, dtype=jnp.int32)[None, :]
    order = (device - heavy - 1) % N_TURN
    lighter = base + ((order - rotation) % (N_TURN - 1) < spare).astype(jnp.int32)
    counts = jnp.where(order == N_TURN - 1, TS, lighter).astype(jnp.int32)
    decks = jax.vmap(lambda subkey: jax.random.permutation(subkey, CARDS))(jax.random.split(third_key, FLOPS)).astype(jnp.int32)
    starts = jnp.cumsum(counts, axis=1) - counts
    slot = jnp.arange(N_TURN * TS, dtype=jnp.int32)
    holder = slot // TS
    within = slot % TS
    number = (starts[:, holder] + within[None, :]) % TURNS
    return (counts, decks, number)


def draw_live_turns(key, part):
    return deal(key)[0]


def draw_flop_cards(key, part):
    return deal(key)[1][:, :3]


def draw_turn_card(key, part):
    counts, decks, number = deal(key)
    return jnp.take_along_axis(decks, 3 + number, axis=1).astype(jnp.int32)


def draw_river_cards(key, part):
    counts, decks, number = deal(key)
    places = 3 + (number[:, :, None] + jnp.arange(1, RIV + 1, dtype=jnp.int32)[None, None, :]) % (CARDS - 3)
    return jax.vmap(lambda deck_row, spots: deck_row[spots])(decks, places).astype(jnp.int32)


def shard_levels(key, dims, cuts, smallest, high):
    factor_of, own = 1.0, jax.random.fold_in(key, 6)
    for dim, parts in cuts:
        heights = jnp.exp(jax.random.uniform(jax.random.fold_in(own, dim), (parts,), jnp.float32, smallest / len(cuts), high / len(cuts)))
        factor_of = factor_of * jnp.repeat(heights, dims[dim] // parts).reshape([-1 if axis == dim else 1 for axis in range(len(dims))])
    return factor_of


def setup_inputs(seed: int = 0) -> dict:
    splits = jax.random.split(jax.random.key(seed), 9)
    ranges = jnp.clip(jnp.exp(jax.random.uniform(splits[0], (2, H), jnp.float32, math.log(0.05), math.log(1.0))), 0.05, 1.0)
    flop_regret = jnp.clip(jnp.exp(math.log(1.0) - 4.6051702 * jax.random.uniform(splits[1], (FLOPS, A, H), jnp.float32) ** shard_levels(splits[1], (FLOPS, A, H), ((0, 64),), -0.2, 0.2)), 0.01, 1.0)
    flop_cards = draw_flop_cards(jax.random.fold_in(splits[8], 71), 0)
    live_turns = draw_live_turns(jax.random.fold_in(splits[8], 71), 0)
    turn_card = draw_turn_card(jax.random.fold_in(splits[8], 71), 0)
    river_cards = draw_river_cards(jax.random.fold_in(splits[8], 71), 0)
    strength = jnp.clip(1.0 * jax.random.uniform(splits[6], (FLOPS, N_TURN * TS, RIV, H), jnp.float32) ** shard_levels(splits[6], (FLOPS, N_TURN * TS, RIV, H), ((0, 64), (1, 4)), -0.2, 0.2), 0.0, 1.0)
    turn_regret = jnp.clip(jnp.exp(math.log(1.0) - 4.6051702 * jax.random.uniform(splits[7], (FLOPS, N_TURN * TS, A, A, H), jnp.float32) ** shard_levels(splits[7], (FLOPS, N_TURN * TS, A, A, H), ((0, 64), (1, 4)), -0.2, 0.2)), 0.01, 1.0)
    return dict(ranges=ranges, flop_regret=flop_regret, flop_cards=flop_cards, live_turns=live_turns, turn_card=turn_card, river_cards=river_cards, strength=strength, turn_regret=turn_regret)


bet_sizes = (0.25, 0.5, 1.0, 2.0)


def hand_table():
    card_low, card_high = np.triu_indices(CARDS, 1)
    return jnp.asarray(card_low, jnp.int32), jnp.asarray(card_high, jnp.int32)


def pot_table():
    growth = 1.0 + 2.0 * np.asarray(bet_sizes)
    return jnp.asarray(np.outer(growth, growth) / (2.0 * H * RIV), jnp.float32)


def unblocked(card_low, card_high, board):
    struck = (card_low[None, :] == board[:, None]) | (card_high[None, :] == board[:, None])
    return jnp.where(jnp.any(struck, axis=0), 0.0, 1.0).astype(jnp.float32)


def slot_terms(reach_one, reach_zero, pot_gain, flop_board, card_low, card_high, turn_id, river_ids, strengths, regrets):
    actions = regrets.shape[0]
    hands = regrets.shape[2]
    sigma_turn = regrets / jnp.sum(regrets, axis=1, keepdims=True)
    reach_other = (reach_one[None, None, :] * sigma_turn).astype(jnp.bfloat16).reshape(actions * actions, hands)
    early = jnp.concatenate([flop_board.astype(jnp.int32), turn_id.astype(jnp.int32)[None]])
    disjoint = ((card_low[:, None] != card_low[None, :]) & (card_low[:, None] != card_high[None, :])
                & (card_high[:, None] != card_low[None, :]) & (card_high[:, None] != card_high[None, :]))

    def river_step(totals, inputs):
        river_id, strength_row = inputs
        alive = unblocked(card_low, card_high, jnp.concatenate([early, river_id.astype(jnp.int32)[None]]))
        outcome = jnp.sign(strength_row[:, None] - strength_row[None, :]) * jnp.where(disjoint, alive[:, None] * alive[None, :], 0.0)
        outcome = outcome.astype(jnp.bfloat16)
        toward = lax.dot_general(reach_other, outcome, (((1,), (1,)), ((), ())), preferred_element_type=jnp.float32)
        against = jnp.dot(reach_zero, outcome, preferred_element_type=jnp.float32)
        return (totals[0] + toward, totals[1] + against), None

    start = (jnp.zeros((actions * actions, hands), jnp.float32), jnp.zeros((actions, hands), jnp.float32))
    (toward, against), _ = lax.scan(river_step, start, (river_ids, strengths))
    value_zero = jnp.sum(pot_gain[:, :, None] * toward.reshape(actions, actions, hands), axis=1)
    action_one = -pot_gain[:, :, None] * against[:, None, :]
    value_one = jnp.sum(sigma_turn * action_one, axis=1)
    new_turn = jnp.maximum(regrets + action_one - value_one[:, None, :], 0.0)
    return value_zero, value_one, new_turn


def reference(ranges, flop_regret, flop_cards, live_turns, turn_card, river_cards, strength, turn_regret):
    card_low, card_high = hand_table()
    pot_gain = pot_table()
    reach_first = ranges[0]
    reach_second = ranges[1]

    def one_flop(inputs):
        regrets_flop, flop_board, counts, turn_ids, river_ids, strengths, regrets_turn = inputs
        sigma_flop = regrets_flop / jnp.sum(regrets_flop, axis=0, keepdims=True)
        reach_zero = (reach_first[None, :] * sigma_flop).astype(jnp.bfloat16)
        starts = jnp.cumsum(counts) - counts
        number = jnp.arange(TURNS, dtype=jnp.int32)
        inside = (number[:, None] >= starts[None, :]) & (number[:, None] < (starts + counts)[None, :])
        device_base = jnp.arange(N_TURN, dtype=jnp.int32)[None, :] * TS
        slot_list = jnp.sum(jnp.where(inside, device_base + number[:, None] - starts[None, :], 0), axis=1).astype(jnp.int32)

        def one_turn(slot_at):
            return slot_terms(reach_second, reach_zero, pot_gain, flop_board, card_low, card_high,
                              turn_ids[slot_at], river_ids[slot_at], strengths[slot_at], regrets_turn[slot_at])

        value_zero, value_one, new_turn = lax.map(one_turn, slot_list)
        action_value = jnp.sum(value_zero, axis=0) / TURNS
        node_zero = jnp.sum(sigma_flop * action_value, axis=0)
        node_one = jnp.sum(value_one, axis=(0, 1)) / TURNS
        new_flop = jnp.maximum(regrets_flop + action_value - node_zero[None, :], 0.0)
        placed = jnp.zeros_like(regrets_turn).at[slot_list].set(new_turn)
        return new_flop, placed, jnp.stack([node_zero, node_one])

    new_flop, placed, nodes = lax.map(one_flop, (flop_regret, flop_cards, live_turns, turn_card, river_cards, strength, turn_regret))
    root_value = jnp.sum(nodes, axis=0) / FLOPS
    return new_flop, placed, root_value
```

```python
import jax
import jax.numpy as jnp
import numpy as np
from jax import lax
from jax.experimental import pallas as pl
from jax.experimental.pallas import tpu as pltpu
from jax.sharding import PartitionSpec as P

CARDS = 52
H = 1326
HP = 1408
A = 4
TURNS = 49
TS = 24
RIV = 2
FLOPS = 64
BLOCK = 256
BIG = 2.0**126

bet_sizes = (0.25, 0.5, 1.0, 2.0)
card_low, card_high = np.triu_indices(CARDS, 1)
growth = 1.0 + 2.0 * np.asarray(bet_sizes)
pot = (np.outer(growth, growth) / (2.0 * H * RIV)).astype(np.float32)


def tables():
    alive = np.ones((56, HP), np.float32)
    for card in range(CARDS):
        alive[card, :H] = (card_low != card) & (card_high != card)
    alive[:, H:] = 0.0
    disjoint = np.zeros((HP, HP), np.float32)
    disjoint[:H, :H] = (
        (card_low[:, None] != card_low[None, :])
        & (card_low[:, None] != card_high[None, :])
        & (card_high[:, None] != card_low[None, :])
        & (card_high[:, None] != card_high[None, :])
    )
    return alive, disjoint.astype(jnp.bfloat16)


BLOCKS = [(start, min(BLOCK, 1328 - start)) for start in range(0, HP, BLOCK)]


def swap_halves(x):
    return jnp.concatenate([x[4:8], x[0:4]], axis=0)


def rounded(x):
    return x.astype(jnp.bfloat16).astype(jnp.float32)


def kernel(
    flop_cards, live_turns, turn_card, river_cards,
    ranges_in, flop_regret_in, strength_in, turn_regret, alive_in, keep_in,
    new_turn, sums, root,
    ranges, flop_regret, strength, alive_table, keep, lose,
    regrets, reach, strong_in, strong_out, found, total, one_total, spread, blank,
    small_sems, keep_sems, in_sems, out_sems,
):
    me = lax.axis_index("turn")
    count = live_turns[0, me]

    def regret_copy(slot, b):
        return pltpu.make_async_copy(
            turn_regret.at[0, slot, :, b],
            regrets.at[slot, b // 2, pl.ds((b % 2) * 4, 4)],
            in_sems.at[slot, b],
        )

    def result_copy(slot, b):
        return pltpu.make_async_copy(
            regrets.at[slot, b // 2, pl.ds((b % 2) * 4, 4)],
            new_turn.at[0, slot, :, b],
            out_sems.at[slot, b],
        )

    def blank_copy(slot):
        return pltpu.make_async_copy(blank, new_turn.at[0, slot], out_sems.at[slot, 0])

    small = [
        pltpu.make_async_copy(source, target, small_sems.at[n])
        for n, (source, target) in enumerate(
            [
                (ranges_in, ranges),
                (flop_regret_in, flop_regret),
                (alive_in, alive_table),
                (strength_in, strength),
            ]
        )
    ]
    masks = [
        pltpu.make_async_copy(
            keep_in.at[pl.ds(start, BLOCK if start + BLOCK <= HP else 128)],
            keep.at[pl.ds(start, BLOCK if start + BLOCK <= HP else 128)],
            keep_sems.at[n],
        )
        for n, (start, rows) in enumerate(BLOCKS)
    ]
    for copy in small:
        copy.start()
    for b in range(A):
        regret_copy(0, b).start()
    for copy in masks:
        copy.start()

    def fetch(slot, carry):
        for b in range(A):
            regret_copy(slot, b).start()
        return carry

    lax.fori_loop(1, count, fetch, 0)
    blank[...] = jnp.zeros_like(blank)

    def clear(slot, carry):
        blank_copy(slot).start()
        return carry

    lax.fori_loop(count, TS, clear, 0)
    reach[...] = jnp.zeros_like(reach)
    strong_in[...] = jnp.zeros_like(strong_in)
    total[...] = jnp.zeros_like(total)
    one_total[...] = jnp.zeros_like(one_total)
    for copy in small:
        copy.wait()

    regrets_flop = flop_regret[0]
    sigma_flop = regrets_flop / jnp.sum(regrets_flop, axis=0, keepdims=True)
    reach_zero = rounded(ranges[0:1, :] * sigma_flop)
    reach[8:16, :H] = jnp.concatenate([reach_zero, reach_zero], axis=0)
    flop_alive = (
        alive_table[pl.ds(flop_cards[0, 0], 1), :]
        * alive_table[pl.ds(flop_cards[0, 1], 1), :]
        * alive_table[pl.ds(flop_cards[0, 2], 1), :]
    )
    row = lax.broadcasted_iota(jnp.int32, (8, 1), 0)
    upper = row < 4
    pots = []
    for k in range(2):
        column = jnp.zeros((8, 1), jnp.float32)
        for n in range(8):
            column = jnp.where(row == n, float(pot[n % 4, 2 * k + n // 4]), column)
        pots.append(column)
    for n, (start, rows) in enumerate(BLOCKS):
        masks[n].wait()
        lose[start : start + rows, :] = -keep[start : start + rows, :]

    def slot_step(slot, carry):
        for b in range(A):
            regret_copy(slot, b).wait()
        first, second = regrets[slot, 0], regrets[slot, 1]
        summed = first + second
        inverse = 1.0 / (summed + swap_halves(summed))
        sigma_first, sigma_second = first * inverse, second * inverse
        second_range = ranges[1:2, :]
        weight = (
            rounded(second_range * sigma_first) * pots[0]
            + rounded(second_range * sigma_second) * pots[1]
        )
        weight = weight + swap_halves(weight)
        reach[0:8, :H] = jnp.where(upper, weight, weight - rounded(weight))
        spreading = sigma_first * pots[0] + sigma_second * pots[1]
        spread[...] = spreading + swap_halves(spreading)
        strong_in[0:RIV, :H] = strength[0, slot] * BIG
        strong_out[...] = strong_in[...].T
        turn_alive = flop_alive * alive_table[pl.ds(turn_card[0, slot], 1), :]
        for r in range(RIV):
            alive = turn_alive * alive_table[pl.ds(river_cards[0, r, slot], 1), :]
            given = (reach[...] * alive).astype(jnp.bfloat16)
            for start, rows in BLOCKS:
                own = jnp.broadcast_to(strong_out[start : start + rows, r : r + 1], (rows, 128))
                for other in range(0, HP, BLOCK):
                    stop = min(other + BLOCK, HP)
                    gap = jnp.concatenate(
                        [
                            own - strong_in[r : r + 1, lane : lane + 128]
                            for lane in range(other, stop, 128)
                        ],
                        axis=1,
                    ).astype(jnp.bfloat16)
                    outcome = jnp.maximum(
                        jnp.minimum(gap, keep[start : start + rows, other:stop]),
                        lose[start : start + rows, other:stop],
                    )
                    gave = jnp.dot(
                        given[:, start : start + rows], outcome,
                        preferred_element_type=jnp.float32,
                    )
                    if start == 0:
                        found[r, :, other:stop] = gave
                    else:
                        found[r, :, other:stop] += gave
            if r == 0:
                values = found[r] * -alive
            else:
                values = values + found[r] * -alive
        total[...] += values[0:8, :]
        against = values[8:16, :H]
        spreading = spread[...]
        one_total[...] += against * spreading
        for k in range(2):
            regrets[slot, k] = jnp.maximum(
                regrets[slot, k] + against * (pots[k] - spreading), 0.0
            )
        for b in range(A):
            result_copy(slot, b).start()
        return carry

    lax.fori_loop(0, count, slot_step, 0)
    whole = total[0:4, :H] + total[4:8, :H]
    sums[0:4, :] = whole
    scale = 1.0 / (TURNS * FLOPS)
    sums[4:5, :] = jnp.sum(sigma_flop * whole, axis=0, keepdims=True) * scale
    sums[5:6, :] = jnp.sum(one_total[0:4, :], axis=0, keepdims=True) * scale
    root[...] = sigma_flop

    def settle(slot, carry):
        for b in range(A):
            result_copy(slot, b).wait()
        return carry

    lax.fori_loop(0, count, settle, 0)

    def settle_blank(slot, carry):
        blank_copy(slot).wait()
        return carry

    lax.fori_loop(count, TS, settle_blank, 0)


def exchange(x, axis, flips):
    size = lax.axis_size(axis)
    for flip in flips:
        if flip < size:
            x = x + lax.ppermute(x, axis, [(n, n ^ flip) for n in range(size)])
    return x


def on_device(
    ranges, flop_regret, flop_cards, live_turns, turn_card, river_cards, strength, turn_regret
):
    alive, disjoint = tables()
    smem = pl.BlockSpec(memory_space=pltpu.SMEM)
    vmem = pl.BlockSpec(memory_space=pltpu.VMEM)
    hbm = pl.BlockSpec(memory_space=pltpu.HBM)
    new_turn, sums, sigma_flop = pl.pallas_call(
        kernel,
        out_shape=(
            jax.ShapeDtypeStruct(turn_regret.shape, jnp.float32),
            jax.ShapeDtypeStruct((6, H), jnp.float32),
            jax.ShapeDtypeStruct((A, H), jnp.float32),
        ),
        in_specs=[smem] * 4 + [hbm] * 6,
        out_specs=(hbm, vmem, vmem),
        scratch_shapes=[
            pltpu.VMEM((2, H), jnp.float32),
            pltpu.VMEM((1, A, H), jnp.float32),
            pltpu.VMEM((1, TS, RIV, H), jnp.float32),
            pltpu.VMEM((56, HP), jnp.float32),
            pltpu.VMEM((HP, HP), jnp.bfloat16),
            pltpu.VMEM((HP, HP), jnp.bfloat16),
            pltpu.VMEM((TS, 2, 8, H), jnp.float32),
            pltpu.VMEM((16, HP), jnp.float32),
            pltpu.VMEM((8, HP), jnp.float32),
            pltpu.VMEM((HP, 8), jnp.float32),
            pltpu.VMEM((RIV, 16, HP), jnp.float32),
            pltpu.VMEM((8, HP), jnp.float32),
            pltpu.VMEM((8, H), jnp.float32),
            pltpu.VMEM((8, H), jnp.float32),
            pltpu.VMEM((A, A, H), jnp.float32),
            pltpu.SemaphoreType.DMA((4,)),
            pltpu.SemaphoreType.DMA((len(BLOCKS),)),
            pltpu.SemaphoreType.DMA((TS, A)),
            pltpu.SemaphoreType.DMA((TS, A)),
        ],
        compiler_params=pltpu.CompilerParams(vmem_limit_bytes=60 * 1024 * 1024),
        name="subtrees",
    )(
        flop_cards, live_turns, turn_card, jnp.swapaxes(river_cards, 1, 2),
        ranges, flop_regret, strength, turn_regret, jnp.asarray(alive), jnp.asarray(disjoint),
    )
    regrets_flop = flop_regret[0]
    turns = exchange(sums, "turn", (1, 2))
    action_value = turns[0:4] / TURNS
    node_zero = jnp.sum(sigma_flop * action_value, axis=0)
    new_flop = jnp.maximum(regrets_flop + action_value - node_zero[None, :], 0.0)
    root_value = exchange(turns[4:6], "flop", (1, 2, 4, 8, 16, 32))
    return (new_flop[None], new_turn, root_value)


def solution(mesh):
    placed = (
        P(),
        P("flop", None, None),
        P("flop", None),
        P("flop", None),
        P("flop", "turn"),
        P("flop", "turn", None),
        P("flop", "turn", None, None),
        P("flop", "turn", None, None, None),
    )
    return jax.shard_map(
        on_device,
        mesh=mesh,
        in_specs=placed,
        out_specs=(P("flop", None, None), P("flop", "turn", None, None, None), P()),
        check_vma=False,
    )
```

```python
import jax
import jax.numpy as jnp
import numpy as np
from jax import lax
from jax.experimental import pallas as pl
from jax.experimental.pallas import tpu as pltpu
from jax.sharding import PartitionSpec as P

CARDS = 52
H = 1326
HP = 1408
LEFT = 48
C = 1128
CP = 1152
A = 4
TURNS = 49
TS = 24
RIV = 2
FLOPS = 64
BLOCK = 256
BIG = 2.0**126

bet_sizes = (0.25, 0.5, 1.0, 2.0)
card_low, card_high = np.triu_indices(CARDS, 1)
growth = 1.0 + 2.0 * np.asarray(bet_sizes)
pot = (np.outer(growth, growth) / (2.0 * H * RIV)).astype(np.float32)


def spread_rows(values, rows, fill):
    out = np.full((rows * 128,), fill, np.int32)
    out[: len(values)] = values
    return out.reshape(rows, 128)


def tables():
    low, high = np.triu_indices(LEFT, 1)
    index = np.stack(
        [
            spread_rows(low, 16, 0),
            spread_rows(high, 16, 1),
            spread_rows(card_low, 16, 0),
            spread_rows(card_high, 16, 1),
        ]
    )
    disjoint = np.zeros((CP, CP), np.float32)
    disjoint[:C, :C] = (
        (low[:, None] != low[None, :])
        & (low[:, None] != high[None, :])
        & (high[:, None] != low[None, :])
        & (high[:, None] != high[None, :])
    )
    return index, disjoint.astype(jnp.bfloat16)


BLOCKS = [(start, min(BLOCK, 1136 - start)) for start in range(0, CP, BLOCK)]


def swap_halves(x):
    return jnp.concatenate([x[4:8], x[0:4]], axis=0)


def rounded(x):
    return x.astype(jnp.bfloat16).astype(jnp.float32)


def kernel(
    flop_cards, live_turns, turn_card, river_cards,
    ranges_in, flop_regret_in, strength_in, turn_regret, index_in, keep_in,
    new_turn, sums, root,
    ranges, flop_regret, strength, index, keep,
    regrets, wide, lane, alive, columns, found, back, total, one_total, spread, blank,
    small_sems, keep_sems, in_sems, out_sems,
):
    me = lax.axis_index("turn")
    count = live_turns[0, me]

    def regret_copy(slot, b):
        return pltpu.make_async_copy(
            turn_regret.at[0, slot, :, b],
            regrets.at[slot, b // 2, pl.ds((b % 2) * 4, 4)],
            in_sems.at[slot, b],
        )

    def result_copy(slot, b):
        return pltpu.make_async_copy(
            regrets.at[slot, b // 2, pl.ds((b % 2) * 4, 4)],
            new_turn.at[0, slot, :, b],
            out_sems.at[slot, b],
        )

    def blank_copy(slot):
        return pltpu.make_async_copy(blank, new_turn.at[0, slot], out_sems.at[slot, 0])

    small = [
        pltpu.make_async_copy(source, target, small_sems.at[n])
        for n, (source, target) in enumerate(
            [
                (ranges_in, ranges),
                (flop_regret_in, flop_regret),
                (index_in, index),
                (strength_in, strength),
            ]
        )
    ]
    masks = [
        pltpu.make_async_copy(
            keep_in.at[pl.ds(start, BLOCK if start + BLOCK <= CP else 128)],
            keep.at[pl.ds(start, BLOCK if start + BLOCK <= CP else 128)],
            keep_sems.at[n],
        )
        for n, (start, rows) in enumerate(BLOCKS)
    ]
    for copy in small:
        copy.start()
    for b in range(A):
        regret_copy(0, b).start()
    for copy in masks:
        copy.start()

    def fetch(slot, carry):
        for b in range(A):
            regret_copy(slot, b).start()
        return carry

    lax.fori_loop(1, count, fetch, 0)
    blank[...] = jnp.zeros_like(blank)

    def clear(slot, carry):
        blank_copy(slot).start()
        return carry

    lax.fori_loop(count, TS, clear, 0)
    wide[...] = jnp.zeros_like(wide)
    back[...] = jnp.zeros_like(back)
    total[...] = jnp.zeros_like(total)
    one_total[...] = jnp.zeros_like(one_total)
    for copy in small:
        copy.wait()

    regrets_flop = flop_regret[0]
    sigma_flop = regrets_flop / jnp.sum(regrets_flop, axis=0, keepdims=True)
    reach_zero = rounded(ranges[0:1, :] * sigma_flop)
    wide[1, 0:4, :H] = reach_zero
    first_card, second_card, third_card = (flop_cards[0, n] for n in range(3))
    first_card, second_card = jnp.minimum(first_card, second_card), jnp.maximum(first_card, second_card)
    second_card, third_card = jnp.minimum(second_card, third_card), jnp.maximum(second_card, third_card)
    first_card, second_card = jnp.minimum(first_card, second_card), jnp.maximum(first_card, second_card)
    row = lax.broadcasted_iota(jnp.int32, (8, 1), 0)
    upper = row < 4
    pots = []
    for k in range(2):
        column = jnp.zeros((8, 1), jnp.float32)
        for n in range(8):
            column = jnp.where(row == n, float(pot[n % 4, 2 * k + n // 4]), column)
        pots.append(column)
    for copy in masks:
        copy.wait()

    def slot_step(slot, carry):
        for b in range(A):
            regret_copy(slot, b).wait()
        first, second = regrets[slot, 0], regrets[slot, 1]
        summed = first + second
        inverse = 1.0 / (summed + swap_halves(summed))
        sigma_first, sigma_second = first * inverse, second * inverse
        second_range = ranges[1:2, :]
        weight = (
            rounded(second_range * sigma_first) * pots[0]
            + rounded(second_range * sigma_second) * pots[1]
        )
        weight = weight + swap_halves(weight)
        wide[0, :, :H] = jnp.where(upper, weight, weight - rounded(weight))
        spreading = sigma_first * pots[0] + sigma_second * pots[1]
        spread[...] = spreading + swap_halves(spreading)
        wide[1, 4:6, :H] = strength[0, slot] * BIG

        dead, card = [], turn_card[0, slot]
        for flop_card in (first_card, second_card, third_card):
            dead.append(jnp.minimum(flop_card, card))
            card = jnp.maximum(flop_card, card)
        dead.append(card)
        low, high = index[0], index[1]
        for card in dead:
            low = low + (low >= card).astype(jnp.int32)
            high = high + (high >= card).astype(jnp.int32)
        lane[0] = ((low * (2 * CARDS - 1 - low)) >> 1) + high - low - 1
        for r in range(RIV):
            river = river_cards[0, r, slot]
            alive[r] = jnp.where((low == river) | (high == river), 0.0, -1.0)
        low, high = index[2], index[3]
        lost = (low == dead[0]) | (high == dead[0])
        for card in dead[1:]:
            lost = lost | (low == card) | (high == card)
        less_low, less_high = jnp.zeros_like(low), jnp.zeros_like(high)
        for card in dead:
            less_low = less_low + (low > card).astype(jnp.int32)
            less_high = less_high + (high > card).astype(jnp.int32)
        low, high = low - less_low, high - less_high
        place = ((low * (2 * LEFT - 1 - low)) >> 1) + high - low - 1
        lane[1] = jnp.where(lost, -1, place)

        packed = [[], []]
        for k in range(CP // 128):
            offset = jnp.broadcast_to(lane[0, k : k + 1, :], (8, 128)) - 128 * k
            spot = offset & 127
            for group in range(2):
                parts = [
                    jnp.take_along_axis(
                        wide[group, :, 128 * (k + m) : 128 * (k + m + 1)], spot, axis=1
                    )
                    for m in range(3)
                ]
                packed[group].append(
                    jnp.where(offset < 128, parts[0], jnp.where(offset < 256, parts[1], parts[2]))
                )
        columns[...] = jnp.concatenate(packed[1], axis=1).T
        given = []
        for r in range(RIV):
            pieces = []
            for k in range(CP // 128):
                mask = -alive[r, k : k + 1, :]
                zeros = jnp.where(upper, packed[1][k], swap_halves(packed[1][k]))
                pieces.append(
                    jnp.concatenate([packed[0][k] * mask, zeros * mask], axis=0).astype(jnp.bfloat16)
                )
            given.append(jnp.concatenate(pieces, axis=1))
        for start, rows in BLOCKS:
            own = [
                jnp.broadcast_to(columns[start : start + rows, 4 + r : 5 + r], (rows, 128))
                for r in range(RIV)
            ]
            for other in range(0, CP, BLOCK):
                stop = min(other + BLOCK, CP)
                most = keep[start : start + rows, other:stop]
                least = -most
                for r in range(RIV):
                    gap = jnp.concatenate(
                        [
                            own[r] - packed[1][k][4 + r : 5 + r, :]
                            for k in range(other // 128, stop // 128)
                        ],
                        axis=1,
                    ).astype(jnp.bfloat16)
                    outcome = jnp.maximum(jnp.minimum(gap, most), least)
                    gave = jnp.dot(
                        given[r][:, start : start + rows], outcome,
                        preferred_element_type=jnp.float32,
                    )
                    if start == 0:
                        found[r, :, other:stop] = gave
                    else:
                        found[r, :, other:stop] += gave
        merged = []
        for k in range(CP // 128):
            values = [
                found[r, :, 128 * k : 128 * (k + 1)] * alive[r, k : k + 1, :] for r in range(RIV)
            ]
            values = values[0] + values[1]
            merged.append(
                jnp.where(upper, values[0:8] + swap_halves(values[0:8]), values[8:16])
            )
        for k in range(HP // 128):
            place = jnp.broadcast_to(lane[1, k : k + 1, :], (8, 128))
            spot = place & 127
            result = jnp.zeros((8, 128), jnp.float32)
            for m in range(max(0, k - 2), min(k + 1, CP // 128)):
                part = jnp.take_along_axis(merged[m], spot, axis=1)
                result = jnp.where((place >> 7) == m, part, result)
            total[:, 128 * k : 128 * (k + 1)] += result
            back[:, 128 * k : 128 * (k + 1)] = jnp.where(upper, swap_halves(result), result)
        against = back[:, :H]
        spreading = spread[...]
        one_total[...] += against * spreading
        for k in range(2):
            regrets[slot, k] = jnp.maximum(
                regrets[slot, k] + against * (pots[k] - spreading), 0.0
            )
        for b in range(A):
            result_copy(slot, b).start()
        return carry

    lax.fori_loop(0, count, slot_step, 0)
    whole = total[0:4, :H]
    sums[0:4, :] = whole
    scale = 1.0 / (TURNS * FLOPS)
    sums[4:5, :] = jnp.sum(sigma_flop * whole, axis=0, keepdims=True) * scale
    sums[5:6, :] = jnp.sum(one_total[0:4, :], axis=0, keepdims=True) * scale
    root[...] = sigma_flop

    def settle(slot, carry):
        for b in range(A):
            result_copy(slot, b).wait()
        return carry

    lax.fori_loop(0, count, settle, 0)

    def settle_blank(slot, carry):
        blank_copy(slot).wait()
        return carry

    lax.fori_loop(count, TS, settle_blank, 0)


def exchange(x, axis, flips):
    size = lax.axis_size(axis)
    for flip in flips:
        if flip < size:
            x = x + lax.ppermute(x, axis, [(n, n ^ flip) for n in range(size)])
    return x


def spread_sum(x, axis):
    size = lax.axis_size(axis)
    share = -(-x.size // size)
    flat = jnp.pad(x.reshape(-1), (0, share * size - x.size)).reshape(size, share)
    mine = jnp.sum(lax.all_to_all(flat, axis, 0, 0, tiled=True), axis=0)
    whole = lax.all_to_all(jnp.broadcast_to(mine, (size, share)), axis, 0, 0, tiled=True)
    return whole.reshape(-1)[: x.size].reshape(x.shape)


def on_device(
    ranges, flop_regret, flop_cards, live_turns, turn_card, river_cards, strength, turn_regret
):
    index, disjoint = tables()
    smem = pl.BlockSpec(memory_space=pltpu.SMEM)
    vmem = pl.BlockSpec(memory_space=pltpu.VMEM)
    hbm = pl.BlockSpec(memory_space=pltpu.HBM)
    new_turn, sums, sigma_flop = pl.pallas_call(
        kernel,
        out_shape=(
            jax.ShapeDtypeStruct(turn_regret.shape, jnp.float32),
            jax.ShapeDtypeStruct((6, H), jnp.float32),
            jax.ShapeDtypeStruct((A, H), jnp.float32),
        ),
        in_specs=[smem] * 4 + [hbm] * 6,
        out_specs=(hbm, vmem, vmem),
        scratch_shapes=[
            pltpu.VMEM((2, H), jnp.float32),
            pltpu.VMEM((1, A, H), jnp.float32),
            pltpu.VMEM((1, TS, RIV, H), jnp.float32),
            pltpu.VMEM((4, 16, 128), jnp.int32),
            pltpu.VMEM((CP, CP), jnp.bfloat16),
            pltpu.VMEM((TS, 2, 8, H), jnp.float32),
            pltpu.VMEM((2, 8, HP), jnp.float32),
            pltpu.VMEM((2, 16, 128), jnp.int32),
            pltpu.VMEM((RIV, 16, 128), jnp.float32),
            pltpu.VMEM((CP, 8), jnp.float32),
            pltpu.VMEM((RIV, 16, CP), jnp.float32),
            pltpu.VMEM((8, HP), jnp.float32),
            pltpu.VMEM((8, HP), jnp.float32),
            pltpu.VMEM((8, H), jnp.float32),
            pltpu.VMEM((8, H), jnp.float32),
            pltpu.VMEM((A, A, H), jnp.float32),
            pltpu.SemaphoreType.DMA((4,)),
            pltpu.SemaphoreType.DMA((len(BLOCKS),)),
            pltpu.SemaphoreType.DMA((TS, A)),
            pltpu.SemaphoreType.DMA((TS, A)),
        ],
        compiler_params=pltpu.CompilerParams(vmem_limit_bytes=60 * 1024 * 1024),
        name="subtrees",
    )(
        flop_cards, live_turns, turn_card, jnp.swapaxes(river_cards, 1, 2),
        ranges, flop_regret, strength, turn_regret, jnp.asarray(index), jnp.asarray(disjoint),
    )
    regrets_flop = flop_regret[0]
    turns = exchange(sums, "turn", (1, 2))
    action_value = turns[0:4] / TURNS
    node_zero = jnp.sum(sigma_flop * action_value, axis=0)
    new_flop = jnp.maximum(regrets_flop + action_value - node_zero[None, :], 0.0)
    root_value = spread_sum(turns[4:6], "flop")
    return (new_flop[None], new_turn, root_value)


def solution(mesh):
    placed = (
        P(),
        P("flop", None, None),
        P("flop", None),
        P("flop", None),
        P("flop", "turn"),
        P("flop", "turn", None),
        P("flop", "turn", None, None),
        P("flop", "turn", None, None, None),
    )
    return jax.shard_map(
        on_device,
        mesh=mesh,
        in_specs=placed,
        out_specs=(P("flop", None, None), P("flop", "turn", None, None, None), P()),
        check_vma=False,
    )
```

```python
import jax
import jax.numpy as jnp
import numpy as np
from jax import lax
from jax.experimental import pallas as pl
from jax.experimental.pallas import tpu as pltpu
from jax.sharding import PartitionSpec as P

CARDS = 52
H = 1326
HP = 1408
LEFT = 48
C = 1128
CP = 1152
A = 4
TURNS = 49
TS = 24
RIV = 2
FLOPS = 64
BLOCK = 256
BIG = 2.0**126

bet_sizes = (0.25, 0.5, 1.0, 2.0)
card_low, card_high = np.triu_indices(CARDS, 1)
growth = 1.0 + 2.0 * np.asarray(bet_sizes)
pot = (np.outer(growth, growth) / (2.0 * H * RIV)).astype(np.float32)


def spread_rows(values, rows, fill):
    out = np.full((rows * 128,), fill, np.int32)
    out[: len(values)] = values
    return out.reshape(rows, 128)


def tables():
    low, high = np.triu_indices(LEFT, 1)
    index = np.stack(
        [
            spread_rows(low, 16, 0),
            spread_rows(high, 16, 1),
            spread_rows(card_low, 16, 0),
            spread_rows(card_high, 16, 1),
        ]
    )
    disjoint = np.zeros((CP, CP), np.float32)
    disjoint[:C, :C] = (
        (low[:, None] != low[None, :])
        & (low[:, None] != high[None, :])
        & (high[:, None] != low[None, :])
        & (high[:, None] != high[None, :])
    )
    return index, disjoint.astype(jnp.bfloat16)


BLOCKS = [(start, min(BLOCK, 1136 - start)) for start in range(0, CP, BLOCK)]


def swap_halves(x):
    return jnp.concatenate([x[4:8], x[0:4]], axis=0)


def rounded(x):
    return x.astype(jnp.bfloat16).astype(jnp.float32)


def kernel(
    flop_cards, live_turns, turn_card, river_cards,
    ranges_in, flop_regret_in, strength_in, turn_regret, index_in, keep_in,
    new_turn, sums, root,
    ranges, flop_regret, strength, index, keep,
    regrets, wide_a, wide_b, lane_a, lane_b, alive_a, alive_b, columns_a, columns_b,
    found_a, found_b, back_a, back_b, spread_a, spread_b, total, one_total, blank,
    small_sems, keep_sems, in_sems, out_sems,
):
    wides, lanes, alives = (wide_a, wide_b), (lane_a, lane_b), (alive_a, alive_b)
    columnses, founds, backs = (columns_a, columns_b), (found_a, found_b), (back_a, back_b)
    spreads = (spread_a, spread_b)
    me = lax.axis_index("turn")
    count = live_turns[0, me]
    pairs = (count + 1) // 2
    used = 2 * pairs

    def regret_copy(slot, b):
        return pltpu.make_async_copy(
            turn_regret.at[0, slot, :, b],
            regrets.at[slot, b // 2, pl.ds((b % 2) * 4, 4)],
            in_sems.at[slot, b],
        )

    def result_copy(slot, b):
        return pltpu.make_async_copy(
            regrets.at[slot, b // 2, pl.ds((b % 2) * 4, 4)],
            new_turn.at[0, slot, :, b],
            out_sems.at[slot, b],
        )

    def blank_copy(slot):
        return pltpu.make_async_copy(blank, new_turn.at[0, slot], out_sems.at[slot, 0])

    small = [
        pltpu.make_async_copy(source, target, small_sems.at[n])
        for n, (source, target) in enumerate(
            [
                (ranges_in, ranges),
                (flop_regret_in, flop_regret),
                (index_in, index),
                (strength_in, strength),
            ]
        )
    ]
    masks = [
        pltpu.make_async_copy(
            keep_in.at[pl.ds(start, BLOCK if start + BLOCK <= CP else 128)],
            keep.at[pl.ds(start, BLOCK if start + BLOCK <= CP else 128)],
            keep_sems.at[n],
        )
        for n, (start, rows) in enumerate(BLOCKS)
    ]
    for copy in small:
        copy.start()
    for b in range(A):
        regret_copy(0, b).start()
    for copy in masks:
        copy.start()

    def fetch(slot, carry):
        for b in range(A):
            regret_copy(slot, b).start()
        return carry

    lax.fori_loop(1, used, fetch, 0)
    blank[...] = jnp.zeros_like(blank)

    def clear(slot, carry):
        blank_copy(slot).start()
        return carry

    lax.fori_loop(used, TS, clear, 0)
    for ref in wides + backs:
        ref[...] = jnp.zeros_like(ref)
    total[...] = jnp.zeros_like(total)
    one_total[...] = jnp.zeros_like(one_total)
    for copy in small:
        copy.wait()

    regrets_flop = flop_regret[0]
    sigma_flop = regrets_flop / jnp.sum(regrets_flop, axis=0, keepdims=True)
    reach_zero = rounded(ranges[0:1, :] * sigma_flop)
    for wide in wides:
        wide[1, 0:4, :H] = reach_zero
    first_card, second_card, third_card = (flop_cards[0, n] for n in range(3))
    first_card, second_card = jnp.minimum(first_card, second_card), jnp.maximum(first_card, second_card)
    second_card, third_card = jnp.minimum(second_card, third_card), jnp.maximum(second_card, third_card)
    first_card, second_card = jnp.minimum(first_card, second_card), jnp.maximum(first_card, second_card)
    row = lax.broadcasted_iota(jnp.int32, (8, 1), 0)
    upper = row < 4
    pots = []
    for k in range(2):
        column = jnp.zeros((8, 1), jnp.float32)
        for n in range(8):
            column = jnp.where(row == n, float(pot[n % 4, 2 * k + n // 4]), column)
        pots.append(column)
    for copy in masks:
        copy.wait()

    def prepare(slot, side):
        wide, lane, alive, columns, spread = wides[side], lanes[side], alives[side], columnses[side], spreads[side]
        for b in range(A):
            regret_copy(slot, b).wait()
        first, second = regrets[slot, 0], regrets[slot, 1]
        summed = first + second
        inverse = 1.0 / (summed + swap_halves(summed))
        sigma_first, sigma_second = first * inverse, second * inverse
        second_range = ranges[1:2, :]
        weight = (
            rounded(second_range * sigma_first) * pots[0]
            + rounded(second_range * sigma_second) * pots[1]
        )
        weight = weight + swap_halves(weight)
        wide[0, :, :H] = jnp.where(upper, weight, weight - rounded(weight))
        spreading = sigma_first * pots[0] + sigma_second * pots[1]
        spread[...] = spreading + swap_halves(spreading)
        wide[1, 4:6, :H] = strength[0, slot] * BIG

        dead, card = [], turn_card[0, slot]
        for flop_card in (first_card, second_card, third_card):
            dead.append(jnp.minimum(flop_card, card))
            card = jnp.maximum(flop_card, card)
        dead.append(card)
        low, high = index[0], index[1]
        for card in dead:
            low = low + (low >= card).astype(jnp.int32)
            high = high + (high >= card).astype(jnp.int32)
        lane[0] = ((low * (2 * CARDS - 1 - low)) >> 1) + high - low - 1
        for r in range(RIV):
            river = river_cards[0, r, slot]
            alive[r] = jnp.where((low == river) | (high == river), 0.0, -1.0)
        low, high = index[2], index[3]
        lost = (low == dead[0]) | (high == dead[0])
        for card in dead[1:]:
            lost = lost | (low == card) | (high == card)
        less_low, less_high = jnp.zeros_like(low), jnp.zeros_like(high)
        for card in dead:
            less_low = less_low + (low > card).astype(jnp.int32)
            less_high = less_high + (high > card).astype(jnp.int32)
        low, high = low - less_low, high - less_high
        place = ((low * (2 * LEFT - 1 - low)) >> 1) + high - low - 1
        lane[1] = jnp.where(lost, -1, place)

        packed = [[], []]
        for k in range(CP // 128):
            offset = jnp.broadcast_to(lane[0, k : k + 1, :], (8, 128)) - 128 * k
            spot = offset & 127
            for group in range(2):
                parts = [
                    jnp.take_along_axis(
                        wide[group, :, 128 * (k + m) : 128 * (k + m + 1)], spot, axis=1
                    )
                    for m in range(3)
                ]
                packed[group].append(
                    jnp.where(offset < 128, parts[0], jnp.where(offset < 256, parts[1], parts[2]))
                )
        columns[...] = jnp.concatenate(packed[1], axis=1).T
        given = []
        for r in range(RIV):
            pieces = []
            for k in range(CP // 128):
                mask = -alive[r, k : k + 1, :]
                zeros = jnp.where(upper, packed[1][k], swap_halves(packed[1][k]))
                pieces.append(
                    jnp.concatenate([packed[0][k] * mask, zeros * mask], axis=0).astype(jnp.bfloat16)
                )
            given.append(jnp.concatenate(pieces, axis=1))
        return packed, given

    def multiply(side, packed, given):
        columns, found = columnses[side], founds[side]
        for start, rows in BLOCKS:
            own = [
                jnp.broadcast_to(columns[start : start + rows, 4 + r : 5 + r], (rows, 128))
                for r in range(RIV)
            ]
            for other in range(0, CP, BLOCK):
                stop = min(other + BLOCK, CP)
                most = keep[start : start + rows, other:stop]
                least = -most
                for r in range(RIV):
                    gap = jnp.concatenate(
                        [
                            own[r] - packed[1][k][4 + r : 5 + r, :]
                            for k in range(other // 128, stop // 128)
                        ],
                        axis=1,
                    ).astype(jnp.bfloat16)
                    outcome = jnp.maximum(jnp.minimum(gap, most), least)
                    gave = jnp.dot(
                        given[r][:, start : start + rows], outcome,
                        preferred_element_type=jnp.float32,
                    )
                    if start == 0:
                        found[r, :, other:stop] = gave
                    else:
                        found[r, :, other:stop] += gave

    def finish(slot, side, live):
        lane, alive, found = lanes[side], alives[side], founds[side]
        back, spread = backs[side], spreads[side]
        merged = []
        for k in range(CP // 128):
            values = [
                found[r, :, 128 * k : 128 * (k + 1)] * alive[r, k : k + 1, :] for r in range(RIV)
            ]
            values = values[0] + values[1]
            merged.append(
                jnp.where(upper, values[0:8] + swap_halves(values[0:8]), values[8:16])
            )
        for k in range(HP // 128):
            place = jnp.broadcast_to(lane[1, k : k + 1, :], (8, 128))
            spot = place & 127
            result = jnp.zeros((8, 128), jnp.float32)
            for m in range(max(0, k - 2), min(k + 1, CP // 128)):
                part = jnp.take_along_axis(merged[m], spot, axis=1)
                result = jnp.where((place >> 7) == m, part, result)
            if live is not None:
                result = result * live
            total[:, 128 * k : 128 * (k + 1)] += result
            back[:, 128 * k : 128 * (k + 1)] = jnp.where(upper, swap_halves(result), result)
        against = back[:, :H]
        spreading = spread[...]
        one_total[...] += against * spreading
        for k in range(2):
            updated = jnp.maximum(regrets[slot, k] + against * (pots[k] - spreading), 0.0)
            regrets[slot, k] = updated if live is None else updated * live
        for b in range(A):
            result_copy(slot, b).start()


    def pair_step(pair, carry):
        slots = (2 * pair, 2 * pair + 1)
        live = (None, (slots[1] < count).astype(jnp.float32))
        ready = [prepare(slots[side], side) for side in range(2)]
        for side in range(2):
            multiply(side, *ready[side])
            finish(slots[side], side, live[side])
        return carry

    lax.fori_loop(0, pairs, pair_step, 0)
    whole = total[0:4, :H]
    sums[0:4, :] = whole
    scale = 1.0 / (TURNS * FLOPS)
    sums[4:5, :] = jnp.sum(sigma_flop * whole, axis=0, keepdims=True) * scale
    sums[5:6, :] = jnp.sum(one_total[0:4, :], axis=0, keepdims=True) * scale
    root[...] = sigma_flop

    def settle(slot, carry):
        for b in range(A):
            result_copy(slot, b).wait()
        return carry

    lax.fori_loop(0, used, settle, 0)

    def settle_blank(slot, carry):
        blank_copy(slot).wait()
        return carry

    lax.fori_loop(used, TS, settle_blank, 0)


def group_sum(x, axis, groups=None):
    size = lax.axis_size(axis) if groups is None else len(groups[0])
    copies = jnp.broadcast_to(x, (size, *x.shape))
    return jnp.sum(lax.all_to_all(copies, axis, 0, 0, axis_index_groups=groups, tiled=True), axis=0)


def on_device(
    ranges, flop_regret, flop_cards, live_turns, turn_card, river_cards, strength, turn_regret
):
    index, disjoint = tables()
    smem = pl.BlockSpec(memory_space=pltpu.SMEM)
    vmem = pl.BlockSpec(memory_space=pltpu.VMEM)
    hbm = pl.BlockSpec(memory_space=pltpu.HBM)
    new_turn, sums, sigma_flop = pl.pallas_call(
        kernel,
        out_shape=(
            jax.ShapeDtypeStruct(turn_regret.shape, jnp.float32),
            jax.ShapeDtypeStruct((6, H), jnp.float32),
            jax.ShapeDtypeStruct((A, H), jnp.float32),
        ),
        in_specs=[smem] * 4 + [hbm] * 6,
        out_specs=(hbm, vmem, vmem),
        scratch_shapes=[
            pltpu.VMEM((2, H), jnp.float32),
            pltpu.VMEM((1, A, H), jnp.float32),
            pltpu.VMEM((1, TS, RIV, H), jnp.float32),
            pltpu.VMEM((4, 16, 128), jnp.int32),
            pltpu.VMEM((CP, CP), jnp.bfloat16),
            pltpu.VMEM((TS, 2, 8, H), jnp.float32),
            *[pltpu.VMEM((2, 8, HP), jnp.float32)] * 2,
            *[pltpu.VMEM((2, 16, 128), jnp.int32)] * 2,
            *[pltpu.VMEM((RIV, 16, 128), jnp.float32)] * 2,
            *[pltpu.VMEM((CP, 8), jnp.float32)] * 2,
            *[pltpu.VMEM((RIV, 16, CP), jnp.float32)] * 2,
            *[pltpu.VMEM((8, HP), jnp.float32)] * 2,
            *[pltpu.VMEM((8, H), jnp.float32)] * 2,
            pltpu.VMEM((8, HP), jnp.float32),
            pltpu.VMEM((8, H), jnp.float32),
            pltpu.VMEM((A, A, H), jnp.float32),
            pltpu.SemaphoreType.DMA((4,)),
            pltpu.SemaphoreType.DMA((len(BLOCKS),)),
            pltpu.SemaphoreType.DMA((TS, A)),
            pltpu.SemaphoreType.DMA((TS, A)),
        ],
        compiler_params=pltpu.CompilerParams(vmem_limit_bytes=60 * 1024 * 1024),
        name="subtrees",
    )(
        flop_cards, live_turns, turn_card, jnp.swapaxes(river_cards, 1, 2),
        ranges, flop_regret, strength, turn_regret, jnp.asarray(index), jnp.asarray(disjoint),
    )
    regrets_flop = flop_regret[0]
    turns = group_sum(sums, "turn")
    action_value = turns[0:4] / TURNS
    node_zero = jnp.sum(sigma_flop * action_value, axis=0)
    new_flop = jnp.maximum(regrets_flop + action_value - node_zero[None, :], 0.0)
    near = [[8 * z + k for k in range(8)] for z in range(8)]
    far = [[8 * z + k for z in range(8)] for k in range(8)]
    root_value = turns[4:6]
    if lax.axis_size("flop") == FLOPS:
        root_value = group_sum(group_sum(root_value, "flop", near), "flop", far)
    return (new_flop[None], new_turn, root_value)


def solution(mesh):
    placed = (
        P(),
        P("flop", None, None),
        P("flop", None),
        P("flop", None),
        P("flop", "turn"),
        P("flop", "turn", None),
        P("flop", "turn", None, None),
        P("flop", "turn", None, None, None),
    )
    return jax.shard_map(
        on_device,
        mesh=mesh,
        in_specs=placed,
        out_specs=(P("flop", None, None), P("flop", "turn", None, None, None), P()),
        check_vma=False,
    )
```

```python
import jax
import jax.numpy as jnp
import numpy as np
from jax import lax
from jax.experimental import pallas as pl
from jax.experimental.pallas import tpu as pltpu
from jax.sharding import PartitionSpec as P

CARDS = 52
H = 1326
HP = 1408
LEFT = 48
C = 1128
CP = 1152
A = 4
TURNS = 49
TS = 24
RIV = 2
FLOPS = 64
BLOCK = 256
PIECE = 32
BIG = 2.0**126

bet_sizes = (0.25, 0.5, 1.0, 2.0)
card_low, card_high = np.triu_indices(CARDS, 1)
growth = 1.0 + 2.0 * np.asarray(bet_sizes)
pot = (np.outer(growth, growth) / (2.0 * H * RIV)).astype(np.float32)


def spread_rows(values, rows, fill):
    out = np.full((rows * 128,), fill, np.int32)
    out[: len(values)] = values
    return out.reshape(rows, 128)


def tables():
    low, high = np.triu_indices(LEFT, 1)
    index = np.stack(
        [
            spread_rows(low, 16, 0),
            spread_rows(high, 16, 1),
            spread_rows(card_low, 16, 0),
            spread_rows(card_high, 16, 1),
        ]
    )
    disjoint = np.zeros((CP, CP), np.float32)
    disjoint[:C, :C] = (
        (low[:, None] != low[None, :])
        & (low[:, None] != high[None, :])
        & (high[:, None] != low[None, :])
        & (high[:, None] != high[None, :])
    )
    return index, disjoint.astype(jnp.bfloat16)


BLOCKS = [(start, min(BLOCK, 1136 - start)) for start in range(0, CP, BLOCK)]


def swap_halves(x):
    return jnp.concatenate([x[4:8], x[0:4]], axis=0)


def rounded(x):
    return x.astype(jnp.bfloat16).astype(jnp.float32)


def kernel(
    flop_cards, live_turns, turn_card, river_cards,
    ranges_in, flop_regret_in, strength_in, turn_regret, index_in, keep_in,
    new_turn, sums, root,
    ranges, flop_regret, strength, index, keep,
    regrets, wide_a, wide_b, lane_a, lane_b, alive_a, alive_b, bands_a, bands_b,
    found_a, found_b, back_a, back_b, spread_a, spread_b, total, one_total, blank,
    small_sems, keep_sems, in_sems, out_sems,
):
    wides, lanes, alives = (wide_a, wide_b), (lane_a, lane_b), (alive_a, alive_b)
    bandses, founds, backs = (bands_a, bands_b), (found_a, found_b), (back_a, back_b)
    spreads = (spread_a, spread_b)
    me = lax.axis_index("turn")
    count = live_turns[0, me]
    pairs = (count + 1) // 2
    used = 2 * pairs

    def regret_copy(slot, b):
        return pltpu.make_async_copy(
            turn_regret.at[0, slot, :, b],
            regrets.at[slot, b // 2, pl.ds((b % 2) * 4, 4)],
            in_sems.at[slot, b],
        )

    def result_copy(slot, b):
        return pltpu.make_async_copy(
            regrets.at[slot, b // 2, pl.ds((b % 2) * 4, 4)],
            new_turn.at[0, slot, :, b],
            out_sems.at[slot, b],
        )

    def blank_copy(slot):
        return pltpu.make_async_copy(blank, new_turn.at[0, slot], out_sems.at[slot, 0])

    small = [
        pltpu.make_async_copy(source, target, small_sems.at[n])
        for n, (source, target) in enumerate(
            [
                (ranges_in, ranges),
                (flop_regret_in, flop_regret),
                (index_in, index),
                (strength_in, strength),
            ]
        )
    ]
    masks = [
        pltpu.make_async_copy(
            keep_in.at[pl.ds(start, BLOCK if start + BLOCK <= CP else 128)],
            keep.at[pl.ds(start, BLOCK if start + BLOCK <= CP else 128)],
            keep_sems.at[n],
        )
        for n, (start, rows) in enumerate(BLOCKS)
    ]
    for copy in small:
        copy.start()
    for b in range(A):
        regret_copy(0, b).start()
    for copy in masks:
        copy.start()

    def fetch(slot, carry):
        for b in range(A):
            regret_copy(slot, b).start()
        return carry

    lax.fori_loop(1, used, fetch, 0)
    blank[...] = jnp.zeros_like(blank)

    def clear(slot, carry):
        blank_copy(slot).start()
        return carry

    lax.fori_loop(used, TS, clear, 0)
    for ref in wides + backs:
        ref[...] = jnp.zeros_like(ref)
    total[...] = jnp.zeros_like(total)
    one_total[...] = jnp.zeros_like(one_total)
    for copy in small:
        copy.wait()

    regrets_flop = flop_regret[0]
    sigma_flop = regrets_flop / jnp.sum(regrets_flop, axis=0, keepdims=True)
    reach_zero = rounded(ranges[0:1, :] * sigma_flop)
    for wide in wides:
        wide[1, 0:4, :H] = reach_zero
    first_card, second_card, third_card = (flop_cards[0, n] for n in range(3))
    first_card, second_card = jnp.minimum(first_card, second_card), jnp.maximum(first_card, second_card)
    second_card, third_card = jnp.minimum(second_card, third_card), jnp.maximum(second_card, third_card)
    first_card, second_card = jnp.minimum(first_card, second_card), jnp.maximum(first_card, second_card)
    row = lax.broadcasted_iota(jnp.int32, (8, 1), 0)
    upper = row < 4
    pots = []
    for k in range(2):
        column = jnp.zeros((8, 1), jnp.float32)
        for n in range(8):
            column = jnp.where(row == n, float(pot[n % 4, 2 * k + n // 4]), column)
        pots.append(column)
    for copy in masks:
        copy.wait()

    def prepare(slot, side):
        wide, lane, alive, bands, spread = wides[side], lanes[side], alives[side], bandses[side], spreads[side]
        for b in range(A):
            regret_copy(slot, b).wait()
        first, second = regrets[slot, 0], regrets[slot, 1]
        summed = first + second
        inverse = 1.0 / (summed + swap_halves(summed))
        sigma_first, sigma_second = first * inverse, second * inverse
        second_range = ranges[1:2, :]
        weight = (
            rounded(second_range * sigma_first) * pots[0]
            + rounded(second_range * sigma_second) * pots[1]
        )
        weight = weight + swap_halves(weight)
        wide[0, :, :H] = jnp.where(upper, weight, weight - rounded(weight))
        spreading = sigma_first * pots[0] + sigma_second * pots[1]
        spread[...] = spreading + swap_halves(spreading)
        wide[1, 4:6, :H] = strength[0, slot] * BIG

        dead, card = [], turn_card[0, slot]
        for flop_card in (first_card, second_card, third_card):
            dead.append(jnp.minimum(flop_card, card))
            card = jnp.maximum(flop_card, card)
        dead.append(card)
        low, high = index[0], index[1]
        for card in dead:
            low = low + (low >= card).astype(jnp.int32)
            high = high + (high >= card).astype(jnp.int32)
        lane[0] = ((low * (2 * CARDS - 1 - low)) >> 1) + high - low - 1
        for r in range(RIV):
            river = river_cards[0, r, slot]
            alive[r] = jnp.where((low == river) | (high == river), 0.0, -1.0)
        low, high = index[2], index[3]
        lost = (low == dead[0]) | (high == dead[0])
        for card in dead[1:]:
            lost = lost | (low == card) | (high == card)
        less_low, less_high = jnp.zeros_like(low), jnp.zeros_like(high)
        for card in dead:
            less_low = less_low + (low > card).astype(jnp.int32)
            less_high = less_high + (high > card).astype(jnp.int32)
        low, high = low - less_low, high - less_high
        place = ((low * (2 * LEFT - 1 - low)) >> 1) + high - low - 1
        lane[1] = jnp.where(lost, -1, place)

        packed = [[], []]
        for k in range(CP // 128):
            offset = jnp.broadcast_to(lane[0, k : k + 1, :], (8, 128)) - 128 * k
            spot = offset & 127
            for group in range(2):
                parts = [
                    jnp.take_along_axis(
                        wide[group, :, 128 * (k + m) : 128 * (k + m + 1)], spot, axis=1
                    )
                    for m in range(3)
                ]
                packed[group].append(
                    jnp.where(offset < 128, parts[0], jnp.where(offset < 256, parts[1], parts[2]))
                )
        turned = jnp.concatenate(packed[1], axis=1).T
        for r in range(RIV):
            bands[r] = jnp.broadcast_to(turned[:, 4 + r : 5 + r], (CP, 128))
        given = []
        for r in range(RIV):
            pieces = []
            for k in range(CP // 128):
                mask = -alive[r, k : k + 1, :]
                zeros = jnp.where(upper, packed[1][k], swap_halves(packed[1][k]))
                pieces.append(
                    jnp.concatenate([packed[0][k] * mask, zeros * mask], axis=0).astype(jnp.bfloat16)
                )
            given.append(jnp.concatenate(pieces, axis=1))
        return packed, given

    def multiply(side, packed, given):
        found, bands = founds[side], bandses[side]
        for other in range(0, CP, BLOCK):
            stop = min(other + BLOCK, CP)
            tiles = range(other // 128, stop // 128)
            gave = [None] * RIV
            for start, rows in BLOCKS:
                pieces = [[] for _ in range(RIV)]
                for top in range(start, start + rows, PIECE):
                    end = min(top + PIECE, start + rows)
                    most = keep[top:end, other:stop]
                    least = -most
                    for r in range(RIV):
                        own = bands[r, top:end, :]
                        gap = jnp.concatenate(
                            [own - packed[1][k][4 + r : 5 + r, :] for k in tiles], axis=1
                        ).astype(jnp.bfloat16)
                        pieces[r].append(jnp.maximum(jnp.minimum(gap, most), least))
                for r in range(RIV):
                    part = jnp.dot(
                        given[r][:, start : start + rows], jnp.concatenate(pieces[r], axis=0),
                        preferred_element_type=jnp.float32,
                    )
                    gave[r] = part if gave[r] is None else gave[r] + part
            for r in range(RIV):
                found[r, :, other:stop] = gave[r]

    def finish(slot, side, live):
        lane, alive, found = lanes[side], alives[side], founds[side]
        back, spread = backs[side], spreads[side]
        merged = []
        for k in range(CP // 128):
            values = [
                found[r, :, 128 * k : 128 * (k + 1)] * alive[r, k : k + 1, :] for r in range(RIV)
            ]
            values = values[0] + values[1]
            merged.append(
                jnp.where(upper, values[0:8] + swap_halves(values[0:8]), values[8:16])
            )
        for k in range(HP // 128):
            place = jnp.broadcast_to(lane[1, k : k + 1, :], (8, 128))
            spot = place & 127
            result = jnp.zeros((8, 128), jnp.float32)
            for m in range(max(0, k - 2), min(k + 1, CP // 128)):
                part = jnp.take_along_axis(merged[m], spot, axis=1)
                result = jnp.where((place >> 7) == m, part, result)
            if live is not None:
                result = result * live
            total[:, 128 * k : 128 * (k + 1)] += result
            back[:, 128 * k : 128 * (k + 1)] = jnp.where(upper, swap_halves(result), result)
        against = back[:, :H]
        spreading = spread[...]
        one_total[...] += against * spreading
        for k in range(2):
            updated = jnp.maximum(regrets[slot, k] + against * (pots[k] - spreading), 0.0)
            regrets[slot, k] = updated if live is None else updated * live
        for b in range(A):
            result_copy(slot, b).start()


    def pair_step(pair, carry):
        slots = (2 * pair, 2 * pair + 1)
        live = (None, (slots[1] < count).astype(jnp.float32))
        ready = [prepare(slots[side], side) for side in range(2)]
        for side in range(2):
            multiply(side, *ready[side])
            finish(slots[side], side, live[side])
        return carry

    lax.fori_loop(0, pairs, pair_step, 0)
    whole = total[0:4, :H]
    sums[0:4, :] = whole
    scale = 1.0 / (TURNS * FLOPS)
    sums[4:5, :] = jnp.sum(sigma_flop * whole, axis=0, keepdims=True) * scale
    sums[5:6, :] = jnp.sum(one_total[0:4, :], axis=0, keepdims=True) * scale
    root[...] = sigma_flop

    def settle(slot, carry):
        for b in range(A):
            result_copy(slot, b).wait()
        return carry

    lax.fori_loop(0, used, settle, 0)

    def settle_blank(slot, carry):
        blank_copy(slot).wait()
        return carry

    lax.fori_loop(used, TS, settle_blank, 0)


def group_sum(x, axis, groups=None):
    size = lax.axis_size(axis) if groups is None else len(groups[0])
    copies = jnp.broadcast_to(x, (size, *x.shape))
    return jnp.sum(lax.all_to_all(copies, axis, 0, 0, axis_index_groups=groups, tiled=True), axis=0)


def on_device(
    ranges, flop_regret, flop_cards, live_turns, turn_card, river_cards, strength, turn_regret
):
    index, disjoint = tables()
    smem = pl.BlockSpec(memory_space=pltpu.SMEM)
    vmem = pl.BlockSpec(memory_space=pltpu.VMEM)
    hbm = pl.BlockSpec(memory_space=pltpu.HBM)
    new_turn, sums, sigma_flop = pl.pallas_call(
        kernel,
        out_shape=(
            jax.ShapeDtypeStruct(turn_regret.shape, jnp.float32),
            jax.ShapeDtypeStruct((6, H), jnp.float32),
            jax.ShapeDtypeStruct((A, H), jnp.float32),
        ),
        in_specs=[smem] * 4 + [hbm] * 6,
        out_specs=(hbm, vmem, vmem),
        scratch_shapes=[
            pltpu.VMEM((2, H), jnp.float32),
            pltpu.VMEM((1, A, H), jnp.float32),
            pltpu.VMEM((1, TS, RIV, H), jnp.float32),
            pltpu.VMEM((4, 16, 128), jnp.int32),
            pltpu.VMEM((CP, CP), jnp.bfloat16),
            pltpu.VMEM((TS, 2, 8, H), jnp.float32),
            *[pltpu.VMEM((2, 8, HP), jnp.float32)] * 2,
            *[pltpu.VMEM((2, 16, 128), jnp.int32)] * 2,
            *[pltpu.VMEM((RIV, 16, 128), jnp.float32)] * 2,
            *[pltpu.VMEM((RIV, CP, 128), jnp.float32)] * 2,
            *[pltpu.VMEM((RIV, 16, CP), jnp.float32)] * 2,
            *[pltpu.VMEM((8, HP), jnp.float32)] * 2,
            *[pltpu.VMEM((8, H), jnp.float32)] * 2,
            pltpu.VMEM((8, HP), jnp.float32),
            pltpu.VMEM((8, H), jnp.float32),
            pltpu.VMEM((A, A, H), jnp.float32),
            pltpu.SemaphoreType.DMA((4,)),
            pltpu.SemaphoreType.DMA((len(BLOCKS),)),
            pltpu.SemaphoreType.DMA((TS, A)),
            pltpu.SemaphoreType.DMA((TS, A)),
        ],
        compiler_params=pltpu.CompilerParams(vmem_limit_bytes=60 * 1024 * 1024),
        name="subtrees",
    )(
        flop_cards, live_turns, turn_card, jnp.swapaxes(river_cards, 1, 2),
        ranges, flop_regret, strength, turn_regret, jnp.asarray(index), jnp.asarray(disjoint),
    )
    regrets_flop = flop_regret[0]
    turns = sums[0:4]
    for flip in (1, 2):
        turns = turns + lax.ppermute(turns, "turn", [(n, n ^ flip) for n in range(4)])
    action_value = turns / TURNS
    node_zero = jnp.sum(sigma_flop * action_value, axis=0)
    new_flop = jnp.maximum(regrets_flop + action_value - node_zero[None, :], 0.0)
    root_value = sums[4:6]
    if lax.axis_size("flop") == FLOPS:
        everyone = np.arange(4 * FLOPS).reshape(8, 4, 2, 4)
        near = everyone.transpose(0, 2, 1, 3).reshape(16, 16).tolist()
        far = everyone.transpose(1, 3, 0, 2).reshape(16, 16).tolist()
        for groups in (near, far):
            root_value = group_sum(root_value, ("flop", "turn"), groups)
    else:
        root_value = lax.psum(root_value, "turn")
    return (new_flop[None], new_turn, root_value)


def solution(mesh):
    placed = (
        P(),
        P("flop", None, None),
        P("flop", None),
        P("flop", None),
        P("flop", "turn"),
        P("flop", "turn", None),
        P("flop", "turn", None, None),
        P("flop", "turn", None, None, None),
    )
    return jax.shard_map(
        on_device,
        mesh=mesh,
        in_specs=placed,
        out_specs=(P("flop", None, None), P("flop", "turn", None, None, None), P()),
        check_vma=False,
    )
```

```python
import jax
import jax.numpy as jnp
import numpy as np
from jax import lax
from jax.experimental import pallas as pl
from jax.experimental.pallas import tpu as pltpu
from jax.sharding import PartitionSpec as P

CARDS = 52
H = 1326
HP = 1408
LEFT = 48
C = 1128
CP = 1152
A = 4
TURNS = 49
TS = 24
RIV = 2
FLOPS = 64
NEAR = 16
BLOCK = 256
BIG = 2.0**125
FAR = 2.0**126

bet_sizes = (0.25, 0.5, 1.0, 2.0)
card_low, card_high = np.triu_indices(CARDS, 1)
growth = 1.0 + 2.0 * np.asarray(bet_sizes)
pot = (np.outer(growth, growth) / (2.0 * H * RIV)).astype(np.float32)


def spread_rows(values, rows, fill):
    out = np.full((rows * 128,), fill, np.int32)
    out[: len(values)] = values
    return out.reshape(rows, 128)


def tables():
    low, high = np.triu_indices(LEFT, 1)
    index = np.stack(
        [
            spread_rows(low, 16, 0),
            spread_rows(high, 16, 1),
            spread_rows(card_low, 16, 0),
            spread_rows(card_high, 16, 1),
        ]
    )
    disjoint = np.zeros((CP, CP), np.float32)
    disjoint[:C, :C] = (
        (low[:, None] != low[None, :])
        & (low[:, None] != high[None, :])
        & (high[:, None] != low[None, :])
        & (high[:, None] != high[None, :])
    )
    holds = np.zeros((CP, 128), np.float32)
    holds[np.arange(C), low] = 1.0
    holds[np.arange(C), high] = 1.0
    holds[:C, LEFT] = 1.0
    return index, disjoint.astype(jnp.bfloat16), holds.astype(jnp.bfloat16)


BLOCKS = [(start, min(BLOCK, 1136 - start)) for start in range(0, CP, BLOCK)]


def swap_halves(x):
    return jnp.concatenate([x[4:8], x[0:4]], axis=0)


def rounded(x):
    return x.astype(jnp.bfloat16).astype(jnp.float32)


def kernel(
    flop_cards, live_turns, turn_card, river_cards,
    ranges_in, flop_regret_in, strength_in, turn_regret, index_in, keep_in, holds_in,
    new_turn, sums, copies, root,
    ranges, flop_regret, strength, index, keep, holds,
    regrets, wide_a, wide_b, lane_a, lane_b, struck_a, struck_b, columns_a, columns_b,
    surplus_a, surplus_b, found_a, found_b, back_a, back_b, spread_a, spread_b, total, one_total, blank,
    small_sems, keep_sems, in_sems, out_sems,
):
    wides, lanes, strucks = (wide_a, wide_b), (lane_a, lane_b), (struck_a, struck_b)
    columnses, founds, backs = (columns_a, columns_b), (found_a, found_b), (back_a, back_b)
    spreads, surpluses = (spread_a, spread_b), (surplus_a, surplus_b)
    me = lax.axis_index("turn")
    count = live_turns[0, me]
    pairs = (count + 1) // 2
    used = 2 * pairs

    def regret_copy(slot, b):
        return pltpu.make_async_copy(
            turn_regret.at[0, slot, :, b],
            regrets.at[slot, b // 2, pl.ds((b % 2) * 4, 4)],
            in_sems.at[slot, b],
        )

    def result_copy(slot, b):
        return pltpu.make_async_copy(
            regrets.at[slot, b // 2, pl.ds((b % 2) * 4, 4)],
            new_turn.at[0, slot, :, b],
            out_sems.at[slot, b],
        )

    def blank_copy(slot):
        return pltpu.make_async_copy(blank, new_turn.at[0, slot], out_sems.at[slot, 0])

    small = [
        pltpu.make_async_copy(source, target, small_sems.at[n])
        for n, (source, target) in enumerate(
            [
                (ranges_in, ranges),
                (flop_regret_in, flop_regret),
                (index_in, index),
                (strength_in, strength),
                (holds_in, holds),
            ]
        )
    ]
    masks = [
        pltpu.make_async_copy(
            keep_in.at[pl.ds(start, BLOCK if start + BLOCK <= CP else 128)],
            keep.at[pl.ds(start, BLOCK if start + BLOCK <= CP else 128)],
            keep_sems.at[n],
        )
        for n, (start, rows) in enumerate(BLOCKS)
    ]
    for copy in small:
        copy.start()
    for b in range(A):
        regret_copy(0, b).start()
    for copy in masks:
        copy.start()

    def fetch(slot, carry):
        for b in range(A):
            regret_copy(slot, b).start()
        return carry

    lax.fori_loop(1, used, fetch, 0)
    blank[...] = jnp.zeros_like(blank)

    def clear(slot, carry):
        blank_copy(slot).start()
        return carry

    lax.fori_loop(used, TS, clear, 0)
    for ref in wides + backs:
        ref[...] = jnp.zeros_like(ref)
    total[...] = jnp.zeros_like(total)
    one_total[...] = jnp.zeros_like(one_total)
    for copy in small:
        copy.wait()

    regrets_flop = flop_regret[0]
    sigma_flop = regrets_flop / jnp.sum(regrets_flop, axis=0, keepdims=True)
    reach_zero = rounded(ranges[0:1, :] * sigma_flop)
    for wide in wides:
        wide[1, 0:4, :H] = reach_zero
    first_card, second_card, third_card = (flop_cards[0, n] for n in range(3))
    first_card, second_card = jnp.minimum(first_card, second_card), jnp.maximum(first_card, second_card)
    second_card, third_card = jnp.minimum(second_card, third_card), jnp.maximum(second_card, third_card)
    first_card, second_card = jnp.minimum(first_card, second_card), jnp.maximum(first_card, second_card)
    row = lax.broadcasted_iota(jnp.int32, (8, 1), 0)
    upper = row < 4
    pots = []
    for k in range(2):
        column = jnp.zeros((8, 1), jnp.float32)
        for n in range(8):
            column = jnp.where(row == n, float(pot[n % 4, 2 * k + n // 4]), column)
        pots.append(column)
    for copy in masks:
        copy.wait()

    def prepare(slot, side):
        wide, lane, struck, columns, spread = wides[side], lanes[side], strucks[side], columnses[side], spreads[side]
        surplus = surpluses[side]
        for b in range(A):
            regret_copy(slot, b).wait()
        first, second = regrets[slot, 0], regrets[slot, 1]
        summed = first + second
        inverse = 1.0 / (summed + swap_halves(summed))
        sigma_first, sigma_second = first * inverse, second * inverse
        second_range = ranges[1:2, :]
        weight = (
            rounded(second_range * sigma_first) * pots[0]
            + rounded(second_range * sigma_second) * pots[1]
        )
        weight = weight + swap_halves(weight)
        wide[0, :, :H] = rounded(
            jnp.where(upper, weight, weight - rounded(weight))
        )
        spreading = sigma_first * pots[0] + sigma_second * pots[1]
        spread[...] = spreading + swap_halves(spreading)
        wide[1, 4:6, :H] = strength[0, slot] * BIG

        dead, card = [], turn_card[0, slot]
        for flop_card in (first_card, second_card, third_card):
            dead.append(jnp.minimum(flop_card, card))
            card = jnp.maximum(flop_card, card)
        dead.append(card)
        low, high = index[0], index[1]
        for card in dead:
            low = low + (low >= card).astype(jnp.int32)
            high = high + (high >= card).astype(jnp.int32)
        lane[0] = ((low * (2 * CARDS - 1 - low)) >> 1) + high - low - 1
        rank = []
        for r in range(RIV):
            river = river_cards[0, r, slot]
            struck[r] = jnp.where((low == river) | (high == river), 1.0, 0.0)
            rank.append(river - sum((card < river).astype(jnp.int32) for card in dead))
        low, high = index[2], index[3]
        lost = (low == dead[0]) | (high == dead[0])
        for card in dead[1:]:
            lost = lost | (low == card) | (high == card)
        less_low, less_high = jnp.zeros_like(low), jnp.zeros_like(high)
        for card in dead:
            less_low = less_low + (low > card).astype(jnp.int32)
            less_high = less_high + (high > card).astype(jnp.int32)
        low, high = low - less_low, high - less_high
        place = ((low * (2 * LEFT - 1 - low)) >> 1) + high - low - 1
        lane[1] = jnp.where(lost, -1, place)

        packed = [[], []]
        for k in range(CP // 128):
            offset = jnp.broadcast_to(lane[0, k : k + 1, :], (8, 128)) - 128 * k
            spot = offset & 127
            for group in range(2):
                parts = [
                    jnp.take_along_axis(
                        wide[group, :, 128 * (k + m) : 128 * (k + m + 1)], spot, axis=1
                    )
                    for m in range(3)
                ]
                packed[group].append(
                    jnp.where(offset < 128, parts[0], jnp.where(offset < 256, parts[1], parts[2]))
                )
        reach, rows, given = [], [], []
        for k in range(CP // 128):
            blocked = [struck[r, k : k + 1, :] > 0.0 for r in range(RIV)]
            force = [packed[1][k][4 + r : 5 + r, :] for r in range(RIV)]
            rows.append([jnp.where(blocked[r], -FAR, force[r]) for r in range(RIV)])
            columns[128 * k : 128 * (k + 1), :] = jnp.concatenate(
                [jnp.where(blocked[r], FAR, force[r]) for r in range(RIV)]
                + [jnp.zeros((8 - RIV, 128), jnp.float32)],
                axis=0,
            ).T
            both = packed[0][k] + swap_halves(packed[0][k])
            zero = jnp.where(upper, packed[1][k], swap_halves(packed[1][k]))
            reach.append(jnp.where(upper, both, zero))
            given.append(jnp.concatenate([packed[0][k], zero], axis=0).astype(jnp.bfloat16))
        given = jnp.concatenate(given, axis=1)

        held = jnp.dot(given, holds[...], preferred_element_type=jnp.float32)
        held = jnp.where(upper, held[0:8] + swap_halves(held[0:8]), held[8:16])
        card = lax.broadcasted_iota(jnp.int32, (8, 128), 1)
        paired, with_river = jnp.zeros((8, 128), jnp.float32), []
        for r in range(RIV):
            lower, upper_card = jnp.minimum(card, rank[r]), jnp.maximum(card, rank[r])
            place = ((lower * (2 * LEFT - 1 - lower)) >> 1) + upper_card - lower - 1
            place = jnp.where((card == rank[r]) | (card >= LEFT), -1, place)
            spot = place & 127
            for k in range(CP // 128):
                part = jnp.take_along_axis(reach[k], spot, axis=1)
                paired = paired + jnp.where((place >> 7) == k, part, 0.0)
            with_river.append(
                jnp.take_along_axis(held, jnp.broadcast_to(rank[r], (8, 128)), axis=1)
            )
        everything = jnp.take_along_axis(held, jnp.full((8, 128), LEFT, jnp.int32), axis=1)
        for k in range(CP // 128):
            ends = [jnp.broadcast_to(index[n, k : k + 1, :], (8, 128)) for n in range(2)]
            excess = with_river[0] + with_river[1]
            rest = everything + 2.0 * reach[k]
            for end in ends:
                excess = excess - jnp.take_along_axis(paired, end, axis=1)
                rest = rest - jnp.take_along_axis(held, end, axis=1)
            for r in range(RIV):
                excess = excess + struck[r, k : k + 1, :] * (rest - with_river[r])
            surplus[:, 128 * k : 128 * (k + 1)] = excess
        return rows, given

    def multiply(side, others, given):
        columns, found = columnses[side], founds[side]
        for start, rows in BLOCKS:
            own = [
                jnp.broadcast_to(columns[start : start + rows, r : r + 1], (rows, 128))
                for r in range(RIV)
            ]
            for other in range(0, CP, BLOCK):
                stop = min(other + BLOCK, CP)
                most = keep[start : start + rows, other:stop]
                least = -most
                outcome = None
                for r in range(RIV):
                    gap = jnp.concatenate(
                        [own[r] - others[k][r] for k in range(other // 128, stop // 128)], axis=1
                    ).astype(jnp.bfloat16)
                    sign = jnp.maximum(jnp.minimum(gap, most), least)
                    outcome = sign if outcome is None else outcome + sign
                gave = jnp.dot(
                    given[:, start : start + rows], outcome, preferred_element_type=jnp.float32
                )
                if start == 0:
                    found[:, other:stop] = gave
                else:
                    found[:, other:stop] += gave

    def finish(slot, side, live):
        lane, found, surplus = lanes[side], founds[side], surpluses[side]
        back, spread = backs[side], spreads[side]
        merged = []
        for k in range(CP // 128):
            values = found[:, 128 * k : 128 * (k + 1)]
            values = jnp.where(upper, values[0:8] + swap_halves(values[0:8]), values[8:16])
            merged.append(surplus[:, 128 * k : 128 * (k + 1)] - values)
        for k in range(HP // 128):
            place = jnp.broadcast_to(lane[1, k : k + 1, :], (8, 128))
            spot = place & 127
            result = jnp.zeros((8, 128), jnp.float32)
            for m in range(max(0, k - 2), min(k + 1, CP // 128)):
                part = jnp.take_along_axis(merged[m], spot, axis=1)
                result = jnp.where((place >> 7) == m, part, result)
            if live is not None:
                result = result * live
            total[:, 128 * k : 128 * (k + 1)] += result
            back[:, 128 * k : 128 * (k + 1)] = jnp.where(upper, swap_halves(result), result)
        against = back[:, :H]
        spreading = spread[...]
        one_total[...] += against * spreading
        for k in range(2):
            updated = jnp.maximum(regrets[slot, k] + against * (pots[k] - spreading), 0.0)
            regrets[slot, k] = updated if live is None else updated * live
        for b in range(A):
            result_copy(slot, b).start()


    def pair_step(pair, carry):
        slots = (2 * pair, 2 * pair + 1)
        live = (None, (slots[1] < count).astype(jnp.float32))
        ready = [prepare(slots[side], side) for side in range(2)]
        for side in range(2):
            multiply(side, *ready[side])
            finish(slots[side], side, live[side])
        return carry

    lax.fori_loop(0, pairs, pair_step, 0)
    whole = total[0:4, :H]
    sums[...] = whole
    scale = 1.0 / (TURNS * FLOPS)
    parts = jnp.concatenate(
        [
            jnp.sum(sigma_flop * whole, axis=0, keepdims=True) * scale,
            jnp.sum(one_total[0:4, :], axis=0, keepdims=True) * scale,
        ],
        axis=0,
    )
    for n in range(NEAR):
        copies[n] = parts
    root[...] = sigma_flop

    def settle(slot, carry):
        for b in range(A):
            result_copy(slot, b).wait()
        return carry

    lax.fori_loop(0, used, settle, 0)

    def settle_blank(slot, carry):
        blank_copy(slot).wait()
        return carry

    lax.fori_loop(used, TS, settle_blank, 0)


def group_sum(copies, axis, groups):
    return jnp.sum(
        lax.all_to_all(copies, axis, 0, 0, axis_index_groups=groups, tiled=True), axis=0
    )


def flip_sum(x, axis, flip):
    size = lax.axis_size(axis)
    return x + lax.ppermute(x, axis, [(n, n ^ flip) for n in range(size)])


def on_device(
    ranges, flop_regret, flop_cards, live_turns, turn_card, river_cards, strength, turn_regret
):
    index, disjoint, holds = tables()
    smem = pl.BlockSpec(memory_space=pltpu.SMEM)
    vmem = pl.BlockSpec(memory_space=pltpu.VMEM)
    hbm = pl.BlockSpec(memory_space=pltpu.HBM)
    new_turn, sums, copies, sigma_flop = pl.pallas_call(
        kernel,
        out_shape=(
            jax.ShapeDtypeStruct(turn_regret.shape, jnp.float32),
            jax.ShapeDtypeStruct((A, H), jnp.float32),
            jax.ShapeDtypeStruct((NEAR, 2, H), jnp.float32),
            jax.ShapeDtypeStruct((A, H), jnp.float32),
        ),
        in_specs=[smem] * 4 + [hbm] * 7,
        out_specs=(hbm, vmem, vmem, vmem),
        scratch_shapes=[
            pltpu.VMEM((2, H), jnp.float32),
            pltpu.VMEM((1, A, H), jnp.float32),
            pltpu.VMEM((1, TS, RIV, H), jnp.float32),
            pltpu.VMEM((4, 16, 128), jnp.int32),
            pltpu.VMEM((CP, CP), jnp.bfloat16),
            pltpu.VMEM((CP, 128), jnp.bfloat16),
            pltpu.VMEM((TS, 2, 8, H), jnp.float32),
            *[pltpu.VMEM((2, 8, HP), jnp.float32)] * 2,
            *[pltpu.VMEM((2, 16, 128), jnp.int32)] * 2,
            *[pltpu.VMEM((RIV, 16, 128), jnp.float32)] * 2,
            *[pltpu.VMEM((CP, 8), jnp.float32)] * 2,
            *[pltpu.VMEM((8, CP), jnp.float32)] * 2,
            *[pltpu.VMEM((16, CP), jnp.float32)] * 2,
            *[pltpu.VMEM((8, HP), jnp.float32)] * 2,
            *[pltpu.VMEM((8, H), jnp.float32)] * 2,
            pltpu.VMEM((8, HP), jnp.float32),
            pltpu.VMEM((8, H), jnp.float32),
            pltpu.VMEM((A, A, H), jnp.float32),
            pltpu.SemaphoreType.DMA((5,)),
            pltpu.SemaphoreType.DMA((len(BLOCKS),)),
            pltpu.SemaphoreType.DMA((TS, A)),
            pltpu.SemaphoreType.DMA((TS, A)),
        ],
        compiler_params=pltpu.CompilerParams(vmem_limit_bytes=60 * 1024 * 1024),
        name="subtrees",
    )(
        flop_cards, live_turns, turn_card, jnp.swapaxes(river_cards, 1, 2),
        ranges, flop_regret, strength, turn_regret, jnp.asarray(index), jnp.asarray(disjoint), jnp.asarray(holds),
    )
    regrets_flop = flop_regret[0]
    turns = flip_sum(sums, "turn", 1)
    if lax.axis_size("flop") == FLOPS:
        near = np.arange(4 * FLOPS).reshape(8, 4, 2, 4).transpose(0, 2, 1, 3).reshape(16, NEAR)
        far = np.arange(FLOPS).reshape(8, 8).T
        root_value = group_sum(copies, ("flop", "turn"), near.tolist())
        root_value = flip_sum(root_value, "flop", 1)
        root_value, turns = lax.optimization_barrier((root_value, turns))
        root_value = group_sum(
            jnp.broadcast_to(root_value, (8, *root_value.shape)), "flop", far.tolist()
        )
    else:
        root_value = lax.psum(copies[0], "turn")
    turns = flip_sum(turns, "turn", 2)
    action_value = turns / TURNS
    node_zero = jnp.sum(sigma_flop * action_value, axis=0)
    new_flop = jnp.maximum(regrets_flop + action_value - node_zero[None, :], 0.0)
    return (new_flop[None], new_turn, root_value)


def solution(mesh):
    placed = (
        P(),
        P("flop", None, None),
        P("flop", None),
        P("flop", None),
        P("flop", "turn"),
        P("flop", "turn", None),
        P("flop", "turn", None, None),
        P("flop", "turn", None, None, None),
    )
    return jax.shard_map(
        on_device,
        mesh=mesh,
        in_specs=placed,
        out_specs=(P("flop", None, None), P("flop", "turn", None, None, None), P()),
        check_vma=False,
    )
```

```python
import jax
import jax.numpy as jnp
import numpy as np
from jax import lax
from jax.experimental import pallas as pl
from jax.experimental.pallas import tpu as pltpu
from jax.sharding import PartitionSpec as P

CARDS = 52
H = 1326
HP = 1408
LEFT = 48
C = 1128
CP = 1152
A = 4
TURNS = 49
TS = 24
RIV = 2
FLOPS = 64
NEAR = 16
BLOCK = 256
BIG = 2.0**126

bet_sizes = (0.25, 0.5, 1.0, 2.0)
card_low, card_high = np.triu_indices(CARDS, 1)
growth = 1.0 + 2.0 * np.asarray(bet_sizes)
pot = (np.outer(growth, growth) / (2.0 * H * RIV)).astype(np.float32)


def spread_rows(values, rows, fill):
    out = np.full((rows * 128,), fill, np.int32)
    out[: len(values)] = values
    return out.reshape(rows, 128)


def tables():
    low, high = np.triu_indices(LEFT, 1)
    index = np.stack(
        [
            spread_rows(low, 16, 0),
            spread_rows(high, 16, 1),
            spread_rows(card_low, 16, 0),
            spread_rows(card_high, 16, 1),
        ]
    )
    disjoint = np.zeros((CP, CP), np.float32)
    disjoint[:C, :C] = (
        (low[:, None] != low[None, :])
        & (low[:, None] != high[None, :])
        & (high[:, None] != low[None, :])
        & (high[:, None] != high[None, :])
    )
    return index, disjoint.astype(jnp.bfloat16)


BLOCKS = [(start, min(BLOCK, 1136 - start)) for start in range(0, CP, BLOCK)]


def swap_halves(x):
    return jnp.concatenate([x[4:8], x[0:4]], axis=0)


def rounded(x):
    return x.astype(jnp.bfloat16).astype(jnp.float32)


def kernel(
    flop_cards, live_turns, turn_card, river_cards,
    ranges_in, flop_regret_in, strength_in, turn_regret, index_in, keep_in,
    new_turn, sums, copies, root,
    ranges, flop_regret, strength, index, keep,
    regrets, wide_a, wide_b, lane_a, lane_b, alive_a, alive_b, columns_a, columns_b,
    found_a, found_b, back_a, back_b, spread_a, spread_b, total, one_total, blank,
    small_sems, keep_sems, in_sems, out_sems,
):
    wides, lanes, alives = (wide_a, wide_b), (lane_a, lane_b), (alive_a, alive_b)
    columnses, founds, backs = (columns_a, columns_b), (found_a, found_b), (back_a, back_b)
    spreads = (spread_a, spread_b)
    me = lax.axis_index("turn")
    count = live_turns[0, me]
    pairs = (count + 1) // 2
    used = 2 * pairs

    def regret_copy(slot, b):
        return pltpu.make_async_copy(
            turn_regret.at[0, slot, :, b],
            regrets.at[slot, b // 2, pl.ds((b % 2) * 4, 4)],
            in_sems.at[slot, b],
        )

    def result_copy(slot, b):
        return pltpu.make_async_copy(
            regrets.at[slot, b // 2, pl.ds((b % 2) * 4, 4)],
            new_turn.at[0, slot, :, b],
            out_sems.at[slot, b],
        )

    def blank_copy(slot):
        return pltpu.make_async_copy(blank, new_turn.at[0, slot], out_sems.at[slot, 0])

    small = [
        pltpu.make_async_copy(source, target, small_sems.at[n])
        for n, (source, target) in enumerate(
            [
                (ranges_in, ranges),
                (flop_regret_in, flop_regret),
                (index_in, index),
                (strength_in, strength),
            ]
        )
    ]
    masks = [
        pltpu.make_async_copy(
            keep_in.at[pl.ds(start, BLOCK if start + BLOCK <= CP else 128)],
            keep.at[pl.ds(start, BLOCK if start + BLOCK <= CP else 128)],
            keep_sems.at[n],
        )
        for n, (start, rows) in enumerate(BLOCKS)
    ]
    for copy in small:
        copy.start()
    for b in range(A):
        regret_copy(0, b).start()
    for copy in masks:
        copy.start()

    def fetch(slot, carry):
        for b in range(A):
            regret_copy(slot, b).start()
        return carry

    lax.fori_loop(1, used, fetch, 0)
    blank[...] = jnp.zeros_like(blank)

    def clear(slot, carry):
        blank_copy(slot).start()
        return carry

    lax.fori_loop(used, TS, clear, 0)
    for ref in wides + backs:
        ref[...] = jnp.zeros_like(ref)
    total[...] = jnp.zeros_like(total)
    one_total[...] = jnp.zeros_like(one_total)
    for copy in small:
        copy.wait()

    regrets_flop = flop_regret[0]
    sigma_flop = regrets_flop / jnp.sum(regrets_flop, axis=0, keepdims=True)
    reach_zero = rounded(ranges[0:1, :] * sigma_flop)
    for wide in wides:
        wide[1, 0:4, :H] = reach_zero
    first_card, second_card, third_card = (flop_cards[0, n] for n in range(3))
    first_card, second_card = jnp.minimum(first_card, second_card), jnp.maximum(first_card, second_card)
    second_card, third_card = jnp.minimum(second_card, third_card), jnp.maximum(second_card, third_card)
    first_card, second_card = jnp.minimum(first_card, second_card), jnp.maximum(first_card, second_card)
    row = lax.broadcasted_iota(jnp.int32, (8, 1), 0)
    upper = row < 4
    pots = []
    for k in range(2):
        column = jnp.zeros((8, 1), jnp.float32)
        for n in range(8):
            column = jnp.where(row == n, float(pot[n % 4, 2 * k + n // 4]), column)
        pots.append(column)
    for copy in masks:
        copy.wait()

    def prepare(slot, side):
        wide, lane, alive, columns, spread = wides[side], lanes[side], alives[side], columnses[side], spreads[side]
        for b in range(A):
            regret_copy(slot, b).wait()
        first, second = regrets[slot, 0], regrets[slot, 1]
        summed = first + second
        inverse = 1.0 / (summed + swap_halves(summed))
        sigma_first, sigma_second = first * inverse, second * inverse
        second_range = ranges[1:2, :]
        weight = (
            rounded(second_range * sigma_first) * pots[0]
            + rounded(second_range * sigma_second) * pots[1]
        )
        weight = weight + swap_halves(weight)
        wide[0, :, :H] = jnp.where(upper, weight, weight - rounded(weight))
        spreading = sigma_first * pots[0] + sigma_second * pots[1]
        spread[...] = spreading + swap_halves(spreading)
        wide[1, 4:6, :H] = strength[0, slot] * BIG

        dead, card = [], turn_card[0, slot]
        for flop_card in (first_card, second_card, third_card):
            dead.append(jnp.minimum(flop_card, card))
            card = jnp.maximum(flop_card, card)
        dead.append(card)
        low, high = index[0], index[1]
        for card in dead:
            low = low + (low >= card).astype(jnp.int32)
            high = high + (high >= card).astype(jnp.int32)
        lane[0] = ((low * (2 * CARDS - 1 - low)) >> 1) + high - low - 1
        for r in range(RIV):
            river = river_cards[0, r, slot]
            alive[r] = jnp.where((low == river) | (high == river), 0.0, -1.0)
        low, high = index[2], index[3]
        lost = (low == dead[0]) | (high == dead[0])
        for card in dead[1:]:
            lost = lost | (low == card) | (high == card)
        less_low, less_high = jnp.zeros_like(low), jnp.zeros_like(high)
        for card in dead:
            less_low = less_low + (low > card).astype(jnp.int32)
            less_high = less_high + (high > card).astype(jnp.int32)
        low, high = low - less_low, high - less_high
        place = ((low * (2 * LEFT - 1 - low)) >> 1) + high - low - 1
        lane[1] = jnp.where(lost, -1, place)

        packed = [[], []]
        for k in range(CP // 128):
            offset = jnp.broadcast_to(lane[0, k : k + 1, :], (8, 128)) - 128 * k
            spot = offset & 127
            for group in range(2):
                parts = [
                    jnp.take_along_axis(
                        wide[group, :, 128 * (k + m) : 128 * (k + m + 1)], spot, axis=1
                    )
                    for m in range(3)
                ]
                packed[group].append(
                    jnp.where(offset < 128, parts[0], jnp.where(offset < 256, parts[1], parts[2]))
                )
        columns[...] = jnp.concatenate(packed[1], axis=1).T
        given = []
        for r in range(RIV):
            pieces = []
            for k in range(CP // 128):
                mask = -alive[r, k : k + 1, :]
                zeros = jnp.where(upper, packed[1][k], swap_halves(packed[1][k]))
                pieces.append(
                    jnp.concatenate([packed[0][k] * mask, zeros * mask], axis=0).astype(jnp.bfloat16)
                )
            given.append(jnp.concatenate(pieces, axis=1))
        return packed, given

    def multiply(side, packed, given):
        columns, found = columnses[side], founds[side]
        for start, rows in BLOCKS:
            own = [
                jnp.broadcast_to(columns[start : start + rows, 4 + r : 5 + r], (rows, 128))
                for r in range(RIV)
            ]
            most = keep[start : start + rows, :]
            least = -most
            for r in range(RIV):
                gap = jnp.concatenate(
                    [own[r] - packed[1][k][4 + r : 5 + r, :] for k in range(CP // 128)], axis=1
                ).astype(jnp.bfloat16)
                outcome = jnp.maximum(jnp.minimum(gap, most), least)
                gave = jnp.dot(
                    given[r][:, start : start + rows], outcome, preferred_element_type=jnp.float32
                )
                if start == 0:
                    found[r] = gave
                else:
                    found[r] += gave

    def finish(slot, side, live):
        lane, alive, found = lanes[side], alives[side], founds[side]
        back, spread = backs[side], spreads[side]
        merged = []
        for k in range(CP // 128):
            values = [
                found[r, :, 128 * k : 128 * (k + 1)] * alive[r, k : k + 1, :] for r in range(RIV)
            ]
            values = values[0] + values[1]
            merged.append(
                jnp.where(upper, values[0:8] + swap_halves(values[0:8]), values[8:16])
            )
        for k in range(HP // 128):
            place = jnp.broadcast_to(lane[1, k : k + 1, :], (8, 128))
            spot = place & 127
            result = jnp.zeros((8, 128), jnp.float32)
            for m in range(max(0, k - 2), min(k + 1, CP // 128)):
                part = jnp.take_along_axis(merged[m], spot, axis=1)
                result = jnp.where((place >> 7) == m, part, result)
            if live is not None:
                result = result * live
            total[:, 128 * k : 128 * (k + 1)] += result
            back[:, 128 * k : 128 * (k + 1)] = jnp.where(upper, swap_halves(result), result)
        against = back[:, :H]
        spreading = spread[...]
        one_total[...] += against * spreading
        for k in range(2):
            updated = jnp.maximum(regrets[slot, k] + against * (pots[k] - spreading), 0.0)
            regrets[slot, k] = updated if live is None else updated * live
        for b in range(A):
            result_copy(slot, b).start()


    def pair_step(pair, carry):
        slots = (2 * pair, 2 * pair + 1)
        live = (None, (slots[1] < count).astype(jnp.float32))
        ready = [prepare(slots[side], side) for side in range(2)]
        for side in range(2):
            multiply(side, *ready[side])
            finish(slots[side], side, live[side])
        return carry

    lax.fori_loop(0, pairs, pair_step, 0)
    whole = total[0:4, :H]
    sums[...] = whole
    scale = 1.0 / (TURNS * FLOPS)
    parts = jnp.concatenate(
        [
            jnp.sum(sigma_flop * whole, axis=0, keepdims=True) * scale,
            jnp.sum(one_total[0:4, :], axis=0, keepdims=True) * scale,
        ],
        axis=0,
    )
    for n in range(NEAR):
        copies[n] = parts
    root[...] = sigma_flop

    def settle(slot, carry):
        for b in range(A):
            result_copy(slot, b).wait()
        return carry

    lax.fori_loop(0, used, settle, 0)

    def settle_blank(slot, carry):
        blank_copy(slot).wait()
        return carry

    lax.fori_loop(used, TS, settle_blank, 0)


def group_sum(copies, axis, groups):
    return jnp.sum(
        lax.all_to_all(copies, axis, 0, 0, axis_index_groups=groups, tiled=True), axis=0
    )


def flip_sum(x, axis, flip):
    size = lax.axis_size(axis)
    return x + lax.ppermute(x, axis, [(n, n ^ flip) for n in range(size)])


def on_device(
    ranges, flop_regret, flop_cards, live_turns, turn_card, river_cards, strength, turn_regret
):
    index, disjoint = tables()
    smem = pl.BlockSpec(memory_space=pltpu.SMEM)
    vmem = pl.BlockSpec(memory_space=pltpu.VMEM)
    hbm = pl.BlockSpec(memory_space=pltpu.HBM)
    new_turn, sums, copies, sigma_flop = pl.pallas_call(
        kernel,
        out_shape=(
            jax.ShapeDtypeStruct(turn_regret.shape, jnp.float32),
            jax.ShapeDtypeStruct((A, H), jnp.float32),
            jax.ShapeDtypeStruct((NEAR, 2, H), jnp.float32),
            jax.ShapeDtypeStruct((A, H), jnp.float32),
        ),
        in_specs=[smem] * 4 + [hbm] * 6,
        out_specs=(hbm, vmem, vmem, vmem),
        scratch_shapes=[
            pltpu.VMEM((2, H), jnp.float32),
            pltpu.VMEM((1, A, H), jnp.float32),
            pltpu.VMEM((1, TS, RIV, H), jnp.float32),
            pltpu.VMEM((4, 16, 128), jnp.int32),
            pltpu.VMEM((CP, CP), jnp.bfloat16),
            pltpu.VMEM((TS, 2, 8, H), jnp.float32),
            *[pltpu.VMEM((2, 8, HP), jnp.float32)] * 2,
            *[pltpu.VMEM((2, 16, 128), jnp.int32)] * 2,
            *[pltpu.VMEM((RIV, 16, 128), jnp.float32)] * 2,
            *[pltpu.VMEM((CP, 8), jnp.float32)] * 2,
            *[pltpu.VMEM((RIV, 16, CP), jnp.float32)] * 2,
            *[pltpu.VMEM((8, HP), jnp.float32)] * 2,
            *[pltpu.VMEM((8, H), jnp.float32)] * 2,
            pltpu.VMEM((8, HP), jnp.float32),
            pltpu.VMEM((8, H), jnp.float32),
            pltpu.VMEM((A, A, H), jnp.float32),
            pltpu.SemaphoreType.DMA((4,)),
            pltpu.SemaphoreType.DMA((len(BLOCKS),)),
            pltpu.SemaphoreType.DMA((TS, A)),
            pltpu.SemaphoreType.DMA((TS, A)),
        ],
        compiler_params=pltpu.CompilerParams(vmem_limit_bytes=60 * 1024 * 1024),
        name="subtrees",
    )(
        flop_cards, live_turns, turn_card, jnp.swapaxes(river_cards, 1, 2),
        ranges, flop_regret, strength, turn_regret, jnp.asarray(index), jnp.asarray(disjoint),
    )
    regrets_flop = flop_regret[0]
    others = [lax.ppermute(sums, "turn", [(n, n ^ flip) for n in range(4)]) for flip in (1, 2, 3)]
    if lax.axis_size("flop") == FLOPS:
        near = np.arange(4 * FLOPS).reshape(8, 4, 2, 4).transpose(0, 2, 1, 3).reshape(16, NEAR)
        far = np.arange(FLOPS).reshape(8, 8).T
        root_value = group_sum(copies, ("flop", "turn"), near.tolist())
        root_value = flip_sum(root_value, "flop", 1)
        root_value, others = lax.optimization_barrier((root_value, others))
        root_value = group_sum(
            jnp.broadcast_to(root_value, (8, *root_value.shape)), "flop", far.tolist()
        )
    else:
        root_value = lax.psum(copies[0], "turn")
    action_value = ((sums + others[0]) + (others[1] + others[2])) / TURNS
    node_zero = jnp.sum(sigma_flop * action_value, axis=0)
    new_flop = jnp.maximum(regrets_flop + action_value - node_zero[None, :], 0.0)
    return (new_flop[None], new_turn, root_value)


def solution(mesh):
    placed = (
        P(),
        P("flop", None, None),
        P("flop", None),
        P("flop", None),
        P("flop", "turn"),
        P("flop", "turn", None),
        P("flop", "turn", None, None),
        P("flop", "turn", None, None, None),
    )
    return jax.shard_map(
        on_device,
        mesh=mesh,
        in_specs=placed,
        out_specs=(P("flop", None, None), P("flop", "turn", None, None, None), P()),
        check_vma=False,
    )
```

```python
import jax
import jax.numpy as jnp
import numpy as np
from jax import lax
from jax.experimental import pallas as pl
from jax.experimental.pallas import tpu as pltpu
from jax.sharding import PartitionSpec as P

CARDS = 52
H = 1326
HP = 1408
LEFT = 48
C = 1128
CP = 1152
A = 4
TURNS = 49
TS = 24
RIV = 2
FLOPS = 64
NEAR = 16
BLOCK = 256
BIG = 2.0**126

bet_sizes = (0.25, 0.5, 1.0, 2.0)
card_low, card_high = np.triu_indices(CARDS, 1)
growth = 1.0 + 2.0 * np.asarray(bet_sizes)
pot = (np.outer(growth, growth) / (2.0 * H * RIV)).astype(np.float32)


def spread_rows(values, rows, fill):
    out = np.full((rows * 128,), fill, np.int32)
    out[: len(values)] = values
    return out.reshape(rows, 128)


def tables():
    low, high = np.triu_indices(LEFT, 1)
    index = np.stack(
        [
            spread_rows(low, 16, 0),
            spread_rows(high, 16, 1),
            spread_rows(card_low, 16, 0),
            spread_rows(card_high, 16, 1),
        ]
    )
    disjoint = np.zeros((CP, CP), np.float32)
    disjoint[:C, :C] = (
        (low[:, None] != low[None, :])
        & (low[:, None] != high[None, :])
        & (high[:, None] != low[None, :])
        & (high[:, None] != high[None, :])
    )
    return index, disjoint.astype(jnp.bfloat16)


BLOCKS = [(start, min(BLOCK, 1136 - start)) for start in range(0, CP, BLOCK)]


def swap_halves(x):
    return jnp.concatenate([x[4:8], x[0:4]], axis=0)


def rounded(x):
    return x.astype(jnp.bfloat16).astype(jnp.float32)


def kernel(
    flop_cards, live_turns, turn_card, river_cards,
    ranges_in, flop_regret_in, strength_in, turn_regret, index_in, keep_in,
    new_turn, sums, copies, root,
    ranges, flop_regret, strength, index, keep,
    regrets, wide_a, wide_b, lane_a, lane_b, alive_a, alive_b, columns_a, columns_b,
    found_a, found_b, back_a, back_b, spread_a, spread_b, total, one_total, blank, selector,
    small_sems, keep_sems, in_sems, out_sems,
):
    wides, lanes, alives = (wide_a, wide_b), (lane_a, lane_b), (alive_a, alive_b)
    columnses, founds, backs = (columns_a, columns_b), (found_a, found_b), (back_a, back_b)
    spreads = (spread_a, spread_b)
    me = lax.axis_index("turn")
    count = live_turns[0, me]
    pairs = (count + 1) // 2
    used = 2 * pairs

    def regret_copy(slot, b):
        return pltpu.make_async_copy(
            turn_regret.at[0, slot, :, b],
            regrets.at[slot, b // 2, pl.ds((b % 2) * 4, 4)],
            in_sems.at[slot, b],
        )

    def result_copy(slot, b):
        return pltpu.make_async_copy(
            regrets.at[slot, b // 2, pl.ds((b % 2) * 4, 4)],
            new_turn.at[0, slot, :, b],
            out_sems.at[slot, b],
        )

    def blank_copy(slot):
        return pltpu.make_async_copy(blank, new_turn.at[0, slot], out_sems.at[slot, 0])

    small = [
        pltpu.make_async_copy(source, target, small_sems.at[n])
        for n, (source, target) in enumerate(
            [
                (ranges_in, ranges),
                (flop_regret_in, flop_regret),
                (index_in, index),
                (strength_in, strength),
            ]
        )
    ]
    masks = [
        pltpu.make_async_copy(
            keep_in.at[pl.ds(start, BLOCK if start + BLOCK <= CP else 128)],
            keep.at[pl.ds(start, BLOCK if start + BLOCK <= CP else 128)],
            keep_sems.at[n],
        )
        for n, (start, rows) in enumerate(BLOCKS)
    ]
    for copy in small:
        copy.start()
    for b in range(A):
        regret_copy(0, b).start()
    for copy in masks:
        copy.start()

    def fetch(slot, carry):
        for b in range(A):
            regret_copy(slot, b).start()
        return carry

    lax.fori_loop(1, used, fetch, 0)
    blank[...] = jnp.zeros_like(blank)

    def clear(slot, carry):
        blank_copy(slot).start()
        return carry

    lax.fori_loop(used, TS, clear, 0)
    part = lax.broadcasted_iota(jnp.int32, (128, 128 * RIV), 0)
    side_of = lax.broadcasted_iota(jnp.int32, (128, 128 * RIV), 1) >> 7
    selector[...] = jnp.where((part < 3 * RIV) & ((part & 1) == side_of), 1.0, 0.0).astype(
        jnp.bfloat16
    )
    for ref in columnses:
        ref[...] = jnp.zeros_like(ref)
    for ref in wides + backs:
        ref[...] = jnp.zeros_like(ref)
    total[...] = jnp.zeros_like(total)
    one_total[...] = jnp.zeros_like(one_total)
    for copy in small:
        copy.wait()

    regrets_flop = flop_regret[0]
    sigma_flop = regrets_flop / jnp.sum(regrets_flop, axis=0, keepdims=True)
    reach_zero = rounded(ranges[0:1, :] * sigma_flop)
    for wide in wides:
        wide[1, 0:4, :H] = reach_zero
    first_card, second_card, third_card = (flop_cards[0, n] for n in range(3))
    first_card, second_card = jnp.minimum(first_card, second_card), jnp.maximum(first_card, second_card)
    second_card, third_card = jnp.minimum(second_card, third_card), jnp.maximum(second_card, third_card)
    first_card, second_card = jnp.minimum(first_card, second_card), jnp.maximum(first_card, second_card)
    row = lax.broadcasted_iota(jnp.int32, (8, 1), 0)
    upper = row < 4
    pots = []
    for k in range(2):
        column = jnp.zeros((8, 1), jnp.float32)
        for n in range(8):
            column = jnp.where(row == n, float(pot[n % 4, 2 * k + n // 4]), column)
        pots.append(column)
    for copy in masks:
        copy.wait()

    def prepare(slot, side):
        wide, lane, alive, columns, spread = wides[side], lanes[side], alives[side], columnses[side], spreads[side]
        for b in range(A):
            regret_copy(slot, b).wait()
        first, second = regrets[slot, 0], regrets[slot, 1]
        summed = first + second
        inverse = 1.0 / (summed + swap_halves(summed))
        sigma_first, sigma_second = first * inverse, second * inverse
        second_range = ranges[1:2, :]
        weight = (
            rounded(second_range * sigma_first) * pots[0]
            + rounded(second_range * sigma_second) * pots[1]
        )
        weight = weight + swap_halves(weight)
        wide[0, :, :H] = jnp.where(upper, weight, weight - rounded(weight))
        spreading = sigma_first * pots[0] + sigma_second * pots[1]
        spread[...] = spreading + swap_halves(spreading)
        wide[1, 4:6, :H] = strength[0, slot] * BIG

        dead, card = [], turn_card[0, slot]
        for flop_card in (first_card, second_card, third_card):
            dead.append(jnp.minimum(flop_card, card))
            card = jnp.maximum(flop_card, card)
        dead.append(card)
        low, high = index[0], index[1]
        for card in dead:
            low = low + (low >= card).astype(jnp.int32)
            high = high + (high >= card).astype(jnp.int32)
        lane[0] = ((low * (2 * CARDS - 1 - low)) >> 1) + high - low - 1
        for r in range(RIV):
            river = river_cards[0, r, slot]
            alive[r] = jnp.where((low == river) | (high == river), 0.0, -1.0)
        low, high = index[2], index[3]
        lost = (low == dead[0]) | (high == dead[0])
        for card in dead[1:]:
            lost = lost | (low == card) | (high == card)
        less_low, less_high = jnp.zeros_like(low), jnp.zeros_like(high)
        for card in dead:
            less_low = less_low + (low > card).astype(jnp.int32)
            less_high = less_high + (high > card).astype(jnp.int32)
        low, high = low - less_low, high - less_high
        place = ((low * (2 * LEFT - 1 - low)) >> 1) + high - low - 1
        lane[1] = jnp.where(lost, -1, place)

        packed = [[], []]
        for k in range(CP // 128):
            offset = jnp.broadcast_to(lane[0, k : k + 1, :], (8, 128)) - 128 * k
            spot = offset & 127
            for group in range(2):
                parts = [
                    jnp.take_along_axis(
                        wide[group, :, 128 * (k + m) : 128 * (k + m + 1)], spot, axis=1
                    )
                    for m in range(3)
                ]
                packed[group].append(
                    jnp.where(offset < 128, parts[0], jnp.where(offset < 256, parts[1], parts[2]))
                )
        for k in range(CP // 128):
            force = packed[1][k][4 : 4 + RIV, :]
            parts = []
            for _ in range(3):
                parts.append(rounded(force))
                force = force - parts[-1]
            parts.append(jnp.zeros((8 - 3 * RIV, 128), jnp.float32))
            columns[128 * k : 128 * (k + 1), 0:8] = jnp.concatenate(parts, axis=0).T.astype(
                jnp.bfloat16
            )
        given = []
        for r in range(RIV):
            pieces = []
            for k in range(CP // 128):
                mask = -alive[r, k : k + 1, :]
                zeros = jnp.where(upper, packed[1][k], swap_halves(packed[1][k]))
                pieces.append(
                    jnp.concatenate([packed[0][k] * mask, zeros * mask], axis=0).astype(jnp.bfloat16)
                )
            given.append(jnp.concatenate(pieces, axis=1))
        return packed, given

    def multiply(side, packed, given):
        columns, found = columnses[side], founds[side]
        for start, rows in BLOCKS:
            band = jnp.dot(
                columns[start : start + rows, :], selector[...], preferred_element_type=jnp.float32
            )
            own = [band[:, 128 * r : 128 * (r + 1)] for r in range(RIV)]
            for other in range(0, CP, BLOCK):
                stop = min(other + BLOCK, CP)
                most = keep[start : start + rows, other:stop]
                least = -most
                for r in range(RIV):
                    gap = jnp.concatenate(
                        [
                            own[r] - packed[1][k][4 + r : 5 + r, :]
                            for k in range(other // 128, stop // 128)
                        ],
                        axis=1,
                    ).astype(jnp.bfloat16)
                    outcome = jnp.maximum(jnp.minimum(gap, most), least)
                    gave = jnp.dot(
                        given[r][:, start : start + rows], outcome,
                        preferred_element_type=jnp.float32,
                    )
                    if start == 0:
                        found[r, :, other:stop] = gave
                    else:
                        found[r, :, other:stop] += gave

    def finish(slot, side, live):
        lane, alive, found = lanes[side], alives[side], founds[side]
        back, spread = backs[side], spreads[side]
        merged = []
        for k in range(CP // 128):
            values = [
                found[r, :, 128 * k : 128 * (k + 1)] * alive[r, k : k + 1, :] for r in range(RIV)
            ]
            values = values[0] + values[1]
            merged.append(
                jnp.where(upper, values[0:8] + swap_halves(values[0:8]), values[8:16])
            )
        for k in range(HP // 128):
            place = jnp.broadcast_to(lane[1, k : k + 1, :], (8, 128))
            spot = place & 127
            result = jnp.zeros((8, 128), jnp.float32)
            for m in range(max(0, k - 2), min(k + 1, CP // 128)):
                part = jnp.take_along_axis(merged[m], spot, axis=1)
                result = jnp.where((place >> 7) == m, part, result)
            if live is not None:
                result = result * live
            total[:, 128 * k : 128 * (k + 1)] += result
            back[:, 128 * k : 128 * (k + 1)] = jnp.where(upper, swap_halves(result), result)
        against = back[:, :H]
        spreading = spread[...]
        one_total[...] += against * spreading
        for k in range(2):
            updated = jnp.maximum(regrets[slot, k] + against * (pots[k] - spreading), 0.0)
            regrets[slot, k] = updated if live is None else updated * live
        for b in range(A):
            result_copy(slot, b).start()


    def pair_step(pair, carry):
        slots = (2 * pair, 2 * pair + 1)
        live = (None, (slots[1] < count).astype(jnp.float32))
        ready = [prepare(slots[side], side) for side in range(2)]
        for side in range(2):
            multiply(side, *ready[side])
            finish(slots[side], side, live[side])
        return carry

    lax.fori_loop(0, pairs, pair_step, 0)
    whole = total[0:4, :H]
    sums[...] = whole
    scale = 1.0 / (TURNS * FLOPS)
    parts = jnp.concatenate(
        [
            jnp.sum(sigma_flop * whole, axis=0, keepdims=True) * scale,
            jnp.sum(one_total[0:4, :], axis=0, keepdims=True) * scale,
        ],
        axis=0,
    )
    for n in range(NEAR):
        copies[n] = parts
    root[...] = sigma_flop

    def settle(slot, carry):
        for b in range(A):
            result_copy(slot, b).wait()
        return carry

    lax.fori_loop(0, used, settle, 0)

    def settle_blank(slot, carry):
        blank_copy(slot).wait()
        return carry

    lax.fori_loop(used, TS, settle_blank, 0)


def group_sum(copies, axis, groups):
    return jnp.sum(
        lax.all_to_all(copies, axis, 0, 0, axis_index_groups=groups, tiled=True), axis=0
    )


def flip_sum(x, axis, flip):
    size = lax.axis_size(axis)
    return x + lax.ppermute(x, axis, [(n, n ^ flip) for n in range(size)])


def on_device(
    ranges, flop_regret, flop_cards, live_turns, turn_card, river_cards, strength, turn_regret
):
    index, disjoint = tables()
    smem = pl.BlockSpec(memory_space=pltpu.SMEM)
    vmem = pl.BlockSpec(memory_space=pltpu.VMEM)
    hbm = pl.BlockSpec(memory_space=pltpu.HBM)
    new_turn, sums, copies, sigma_flop = pl.pallas_call(
        kernel,
        out_shape=(
            jax.ShapeDtypeStruct(turn_regret.shape, jnp.float32),
            jax.ShapeDtypeStruct((A, H), jnp.float32),
            jax.ShapeDtypeStruct((NEAR, 2, H), jnp.float32),
            jax.ShapeDtypeStruct((A, H), jnp.float32),
        ),
        in_specs=[smem] * 4 + [hbm] * 6,
        out_specs=(hbm, vmem, vmem, vmem),
        scratch_shapes=[
            pltpu.VMEM((2, H), jnp.float32),
            pltpu.VMEM((1, A, H), jnp.float32),
            pltpu.VMEM((1, TS, RIV, H), jnp.float32),
            pltpu.VMEM((4, 16, 128), jnp.int32),
            pltpu.VMEM((CP, CP), jnp.bfloat16),
            pltpu.VMEM((TS, 2, 8, H), jnp.float32),
            *[pltpu.VMEM((2, 8, HP), jnp.float32)] * 2,
            *[pltpu.VMEM((2, 16, 128), jnp.int32)] * 2,
            *[pltpu.VMEM((RIV, 16, 128), jnp.float32)] * 2,
            *[pltpu.VMEM((CP, 128), jnp.bfloat16)] * 2,
            *[pltpu.VMEM((RIV, 16, CP), jnp.float32)] * 2,
            *[pltpu.VMEM((8, HP), jnp.float32)] * 2,
            *[pltpu.VMEM((8, H), jnp.float32)] * 2,
            pltpu.VMEM((8, HP), jnp.float32),
            pltpu.VMEM((8, H), jnp.float32),
            pltpu.VMEM((A, A, H), jnp.float32),
            pltpu.VMEM((128, 128 * RIV), jnp.bfloat16),
            pltpu.SemaphoreType.DMA((4,)),
            pltpu.SemaphoreType.DMA((len(BLOCKS),)),
            pltpu.SemaphoreType.DMA((TS, A)),
            pltpu.SemaphoreType.DMA((TS, A)),
        ],
        compiler_params=pltpu.CompilerParams(vmem_limit_bytes=60 * 1024 * 1024),
        name="subtrees",
    )(
        flop_cards, live_turns, turn_card, jnp.swapaxes(river_cards, 1, 2),
        ranges, flop_regret, strength, turn_regret, jnp.asarray(index), jnp.asarray(disjoint),
    )
    regrets_flop = flop_regret[0]
    others = [lax.ppermute(sums, "turn", [(n, n ^ flip) for n in range(4)]) for flip in (1, 2, 3)]
    if lax.axis_size("flop") == FLOPS:
        near = np.arange(4 * FLOPS).reshape(8, 4, 2, 4).transpose(0, 2, 1, 3).reshape(16, NEAR)
        far = np.arange(FLOPS).reshape(8, 8).T
        root_value = group_sum(copies, ("flop", "turn"), near.tolist())
        root_value = flip_sum(root_value, "flop", 1)
        root_value, others = lax.optimization_barrier((root_value, others))
        root_value = group_sum(
            jnp.broadcast_to(root_value, (8, *root_value.shape)), "flop", far.tolist()
        )
    else:
        root_value = lax.psum(copies[0], "turn")
    action_value = ((sums + others[0]) + (others[1] + others[2])) / TURNS
    node_zero = jnp.sum(sigma_flop * action_value, axis=0)
    new_flop = jnp.maximum(regrets_flop + action_value - node_zero[None, :], 0.0)
    return (new_flop[None], new_turn, root_value)


def solution(mesh):
    placed = (
        P(),
        P("flop", None, None),
        P("flop", None),
        P("flop", None),
        P("flop", "turn"),
        P("flop", "turn", None),
        P("flop", "turn", None, None),
        P("flop", "turn", None, None, None),
    )
    return jax.shard_map(
        on_device,
        mesh=mesh,
        in_specs=placed,
        out_specs=(P("flop", None, None), P("flop", "turn", None, None, None), P()),
        check_vma=False,
    )
```

```python
import jax
import jax.numpy as jnp
import numpy as np
from jax import lax
from jax.experimental import pallas as pl
from jax.experimental.pallas import tpu as pltpu
from jax.sharding import PartitionSpec as P

CARDS = 52
H = 1326
HP = 1408
LEFT = 48
C = 1128
CP = 1152
A = 4
TURNS = 49
TS = 24
RIV = 2
FLOPS = 64
NEAR = 16
BLOCK = 256
BIG = 2.0**126

bet_sizes = (0.25, 0.5, 1.0, 2.0)
card_low, card_high = np.triu_indices(CARDS, 1)
growth = 1.0 + 2.0 * np.asarray(bet_sizes)
pot = (np.outer(growth, growth) / (2.0 * H * RIV)).astype(np.float32)


def spread_rows(values, rows, fill):
    out = np.full((rows * 128,), fill, np.int32)
    out[: len(values)] = values
    return out.reshape(rows, 128)


def tables():
    low, high = np.triu_indices(LEFT, 1)
    index = np.stack(
        [
            spread_rows(low, 16, 0),
            spread_rows(high, 16, 1),
            spread_rows(card_low, 16, 0),
            spread_rows(card_high, 16, 1),
        ]
    )
    disjoint = np.zeros((CP, CP), np.float32)
    disjoint[:C, :C] = (
        (low[:, None] != low[None, :])
        & (low[:, None] != high[None, :])
        & (high[:, None] != low[None, :])
        & (high[:, None] != high[None, :])
    )
    return index, disjoint.astype(jnp.bfloat16)


BLOCKS = [(start, min(BLOCK, 1136 - start)) for start in range(0, CP, BLOCK)]


def swap_halves(x):
    return pltpu.roll(x, 4, 0)


def rounded(x):
    return x.astype(jnp.bfloat16).astype(jnp.float32)


def kernel(
    flop_cards, live_turns, turn_card, river_cards,
    ranges_in, flop_regret_in, strength_in, turn_regret, index_in, keep_in,
    new_turn, sums, copies, root,
    ranges, flop_regret, strength, index, keep,
    regrets, wide_a, wide_b, lane_a, lane_b, alive_a, alive_b, columns_a, columns_b,
    found_a, found_b, back_a, back_b, spread_a, spread_b, force_a, force_b, given_a, given_b, total, one_total, blank,
    small_sems, keep_sems, in_sems, out_sems,
):
    wides, lanes, alives = (wide_a, wide_b), (lane_a, lane_b), (alive_a, alive_b)
    columnses, founds, backs = (columns_a, columns_b), (found_a, found_b), (back_a, back_b)
    spreads, forces, givens = (spread_a, spread_b), (force_a, force_b), (given_a, given_b)
    me = lax.axis_index("turn")
    count = live_turns[0, me]
    pairs = (count + 1) // 2
    used = 2 * pairs

    def regret_copy(slot, b):
        return pltpu.make_async_copy(
            turn_regret.at[0, slot, :, b],
            regrets.at[slot, b // 2, pl.ds((b % 2) * 4, 4)],
            in_sems.at[slot, b],
        )

    def result_copy(slot, b):
        return pltpu.make_async_copy(
            regrets.at[slot, b // 2, pl.ds((b % 2) * 4, 4)],
            new_turn.at[0, slot, :, b],
            out_sems.at[slot, b],
        )

    def blank_copy(slot):
        return pltpu.make_async_copy(blank, new_turn.at[0, slot], out_sems.at[slot, 0])

    small = [
        pltpu.make_async_copy(source, target, small_sems.at[n])
        for n, (source, target) in enumerate(
            [
                (ranges_in, ranges),
                (flop_regret_in, flop_regret),
                (index_in, index),
                (strength_in, strength),
            ]
        )
    ]
    masks = [
        pltpu.make_async_copy(
            keep_in.at[pl.ds(start, BLOCK if start + BLOCK <= CP else 128)],
            keep.at[pl.ds(start, BLOCK if start + BLOCK <= CP else 128)],
            keep_sems.at[n],
        )
        for n, (start, rows) in enumerate(BLOCKS)
    ]
    for copy in small:
        copy.start()
    for b in range(A):
        regret_copy(0, b).start()
    for copy in masks:
        copy.start()

    def fetch(slot, carry):
        for b in range(A):
            regret_copy(slot, b).start()
        return carry

    lax.fori_loop(1, used, fetch, 0)
    blank[...] = jnp.zeros_like(blank)

    def clear(slot, carry):
        blank_copy(slot).start()
        return carry

    lax.fori_loop(used, TS, clear, 0)
    for ref in wides + backs:
        ref[...] = jnp.zeros_like(ref)
    total[...] = jnp.zeros_like(total)
    one_total[...] = jnp.zeros_like(one_total)
    for copy in small:
        copy.wait()

    regrets_flop = flop_regret[0]
    sigma_flop = regrets_flop / jnp.sum(regrets_flop, axis=0, keepdims=True)
    reach_zero = rounded(ranges[0:1, :] * sigma_flop)
    for wide in wides:
        wide[1, 0:4, :H] = reach_zero
    first_card, second_card, third_card = (flop_cards[0, n] for n in range(3))
    first_card, second_card = jnp.minimum(first_card, second_card), jnp.maximum(first_card, second_card)
    second_card, third_card = jnp.minimum(second_card, third_card), jnp.maximum(second_card, third_card)
    first_card, second_card = jnp.minimum(first_card, second_card), jnp.maximum(first_card, second_card)
    row = lax.broadcasted_iota(jnp.int32, (8, 1), 0)
    upper = row < 4
    pots = []
    for k in range(2):
        column = jnp.zeros((8, 1), jnp.float32)
        for n in range(8):
            column = jnp.where(row == n, float(pot[n % 4, 2 * k + n // 4]), column)
        pots.append(column)
    for copy in masks:
        copy.wait()

    def prepare(slot, side):
        wide, lane, alive, columns, spread = wides[side], lanes[side], alives[side], columnses[side], spreads[side]
        force, given = forces[side], givens[side]
        for b in range(A):
            regret_copy(slot, b).wait()
        first, second = regrets[slot, 0], regrets[slot, 1]
        summed = first + second
        inverse = 1.0 / (summed + swap_halves(summed))
        sigma_first, sigma_second = first * inverse, second * inverse
        second_range = ranges[1:2, :]
        weight = (
            rounded(second_range * sigma_first) * pots[0]
            + rounded(second_range * sigma_second) * pots[1]
        )
        weight = weight + swap_halves(weight)
        wide[0, :, :H] = jnp.where(upper, weight, weight - rounded(weight))
        spreading = sigma_first * pots[0] + sigma_second * pots[1]
        spread[...] = spreading + swap_halves(spreading)
        wide[1, 4:6, :H] = strength[0, slot] * BIG

        dead, card = [], turn_card[0, slot]
        for flop_card in (first_card, second_card, third_card):
            dead.append(jnp.minimum(flop_card, card))
            card = jnp.maximum(flop_card, card)
        dead.append(card)
        low, high = index[0], index[1]
        for card in dead:
            low = low + (low >= card).astype(jnp.int32)
            high = high + (high >= card).astype(jnp.int32)
        lane[0] = ((low * (2 * CARDS - 1 - low)) >> 1) + high - low - 1
        for r in range(RIV):
            river = river_cards[0, r, slot]
            alive[r] = jnp.where((low == river) | (high == river), 0.0, -1.0)
        low, high = index[2], index[3]
        lost = (low == dead[0]) | (high == dead[0])
        for card in dead[1:]:
            lost = lost | (low == card) | (high == card)
        less_low, less_high = jnp.zeros_like(low), jnp.zeros_like(high)
        for card in dead:
            less_low = less_low + (low > card).astype(jnp.int32)
            less_high = less_high + (high > card).astype(jnp.int32)
        low, high = low - less_low, high - less_high
        place = ((low * (2 * LEFT - 1 - low)) >> 1) + high - low - 1
        lane[1] = jnp.where(lost, -1, place)

        packed = [[], []]
        for k in range(CP // 128):
            offset = jnp.broadcast_to(lane[0, k : k + 1, :], (8, 128)) - 128 * k
            spot = offset & 127
            for group in range(2):
                parts = [
                    jnp.take_along_axis(
                        wide[group, :, 128 * (k + m) : 128 * (k + m + 1)], spot, axis=1
                    )
                    for m in range(3)
                ]
                packed[group].append(
                    jnp.where(offset < 128, parts[0], jnp.where(offset < 256, parts[1], parts[2]))
                )
        columns[...] = jnp.concatenate(packed[1], axis=1).T
        for k in range(CP // 128):
            force[:, 128 * k : 128 * (k + 1)] = packed[1][k]
            zeros = jnp.where(upper, packed[1][k], swap_halves(packed[1][k]))
            for r in range(RIV):
                mask = -alive[r, k : k + 1, :]
                given[r, :, 128 * k : 128 * (k + 1)] = jnp.concatenate(
                    [packed[0][k] * mask, zeros * mask], axis=0
                ).astype(jnp.bfloat16)

    def multiply(side):
        columns, found = columnses[side], founds[side]
        force, given = forces[side], givens[side]
        for start, rows in BLOCKS:
            own = [
                jnp.broadcast_to(columns[start : start + rows, 4 + r : 5 + r], (rows, 128))
                for r in range(RIV)
            ]
            for other in range(0, CP, BLOCK):
                stop = min(other + BLOCK, CP)
                most = keep[start : start + rows, other:stop]
                least = -most
                for r in range(RIV):
                    gap = jnp.concatenate(
                        [
                            own[r] - force[4 + r : 5 + r, 128 * k : 128 * (k + 1)]
                            for k in range(other // 128, stop // 128)
                        ],
                        axis=1,
                    ).astype(jnp.bfloat16)
                    outcome = jnp.maximum(jnp.minimum(gap, most), least)
                    gave = jnp.dot(
                        given[r, :, start : start + rows], outcome,
                        preferred_element_type=jnp.float32,
                    )
                    if start == 0:
                        found[r, :, other:stop] = gave
                    else:
                        found[r, :, other:stop] += gave

    def finish(slot, side, live):
        lane, alive, found = lanes[side], alives[side], founds[side]
        back, spread = backs[side], spreads[side]
        merged = []
        for k in range(CP // 128):
            values = [
                found[r, :, 128 * k : 128 * (k + 1)] * alive[r, k : k + 1, :] for r in range(RIV)
            ]
            values = values[0] + values[1]
            merged.append(
                jnp.where(upper, values[0:8] + swap_halves(values[0:8]), values[8:16])
            )
        for k in range(HP // 128):
            place = jnp.broadcast_to(lane[1, k : k + 1, :], (8, 128))
            spot = place & 127
            result = jnp.zeros((8, 128), jnp.float32)
            for m in range(max(0, k - 2), min(k + 1, CP // 128)):
                part = jnp.take_along_axis(merged[m], spot, axis=1)
                result = jnp.where((place >> 7) == m, part, result)
            if live is not None:
                result = result * live
            total[:, 128 * k : 128 * (k + 1)] += result
            back[:, 128 * k : 128 * (k + 1)] = jnp.where(upper, swap_halves(result), result)
        against = back[:, :H]
        spreading = spread[...]
        one_total[...] += against * spreading
        for k in range(2):
            updated = jnp.maximum(regrets[slot, k] + against * (pots[k] - spreading), 0.0)
            regrets[slot, k] = updated if live is None else updated * live
        for b in range(A):
            result_copy(slot, b).start()


    def pair_step(pair, carry):
        slots = (2 * pair, 2 * pair + 1)
        live = (None, (slots[1] < count).astype(jnp.float32))
        for side in range(2):
            prepare(slots[side], side)
        for side in range(2):
            multiply(side)
            finish(slots[side], side, live[side])
        return carry

    lax.fori_loop(0, pairs, pair_step, 0)
    whole = total[0:4, :H]
    sums[...] = whole
    scale = 1.0 / (TURNS * FLOPS)
    parts = jnp.concatenate(
        [
            jnp.sum(sigma_flop * whole, axis=0, keepdims=True) * scale,
            jnp.sum(one_total[0:4, :], axis=0, keepdims=True) * scale,
        ],
        axis=0,
    )
    for n in range(NEAR):
        copies[n] = parts
    root[...] = sigma_flop

    def settle(slot, carry):
        for b in range(A):
            result_copy(slot, b).wait()
        return carry

    lax.fori_loop(0, used, settle, 0)

    def settle_blank(slot, carry):
        blank_copy(slot).wait()
        return carry

    lax.fori_loop(used, TS, settle_blank, 0)


def group_sum(copies, axis, groups):
    return jnp.sum(
        lax.all_to_all(copies, axis, 0, 0, axis_index_groups=groups, tiled=True), axis=0
    )


def flip_sum(x, axis, flip):
    size = lax.axis_size(axis)
    return x + lax.ppermute(x, axis, [(n, n ^ flip) for n in range(size)])


def on_device(
    ranges, flop_regret, flop_cards, live_turns, turn_card, river_cards, strength, turn_regret
):
    index, disjoint = tables()
    smem = pl.BlockSpec(memory_space=pltpu.SMEM)
    vmem = pl.BlockSpec(memory_space=pltpu.VMEM)
    hbm = pl.BlockSpec(memory_space=pltpu.HBM)
    new_turn, sums, copies, sigma_flop = pl.pallas_call(
        kernel,
        out_shape=(
            jax.ShapeDtypeStruct(turn_regret.shape, jnp.float32),
            jax.ShapeDtypeStruct((A, H), jnp.float32),
            jax.ShapeDtypeStruct((NEAR, 2, H), jnp.float32),
            jax.ShapeDtypeStruct((A, H), jnp.float32),
        ),
        in_specs=[smem] * 4 + [hbm] * 6,
        out_specs=(hbm, vmem, vmem, vmem),
        scratch_shapes=[
            pltpu.VMEM((2, H), jnp.float32),
            pltpu.VMEM((1, A, H), jnp.float32),
            pltpu.VMEM((1, TS, RIV, H), jnp.float32),
            pltpu.VMEM((4, 16, 128), jnp.int32),
            pltpu.VMEM((CP, CP), jnp.bfloat16),
            pltpu.VMEM((TS, 2, 8, H), jnp.float32),
            *[pltpu.VMEM((2, 8, HP), jnp.float32)] * 2,
            *[pltpu.VMEM((2, 16, 128), jnp.int32)] * 2,
            *[pltpu.VMEM((RIV, 16, 128), jnp.float32)] * 2,
            *[pltpu.VMEM((CP, 8), jnp.float32)] * 2,
            *[pltpu.VMEM((RIV, 16, CP), jnp.float32)] * 2,
            *[pltpu.VMEM((8, HP), jnp.float32)] * 2,
            *[pltpu.VMEM((8, H), jnp.float32)] * 2,
            *[pltpu.VMEM((8, CP), jnp.float32)] * 2,
            *[pltpu.VMEM((RIV, 16, CP), jnp.bfloat16)] * 2,
            pltpu.VMEM((8, HP), jnp.float32),
            pltpu.VMEM((8, H), jnp.float32),
            pltpu.VMEM((A, A, H), jnp.float32),
            pltpu.SemaphoreType.DMA((4,)),
            pltpu.SemaphoreType.DMA((len(BLOCKS),)),
            pltpu.SemaphoreType.DMA((TS, A)),
            pltpu.SemaphoreType.DMA((TS, A)),
        ],
        compiler_params=pltpu.CompilerParams(vmem_limit_bytes=60 * 1024 * 1024),
        name="subtrees",
    )(
        flop_cards, live_turns, turn_card, jnp.swapaxes(river_cards, 1, 2),
        ranges, flop_regret, strength, turn_regret, jnp.asarray(index), jnp.asarray(disjoint),
    )
    regrets_flop = flop_regret[0]
    others = [lax.ppermute(sums, "turn", [(n, n ^ flip) for n in range(4)]) for flip in (1, 2, 3)]
    if lax.axis_size("flop") == FLOPS:
        near = np.arange(4 * FLOPS).reshape(8, 4, 2, 4).transpose(0, 2, 1, 3).reshape(16, NEAR)
        far = np.arange(FLOPS).reshape(8, 8).T
        root_value = group_sum(copies, ("flop", "turn"), near.tolist())
        root_value = flip_sum(root_value, "flop", 1)
        root_value, others = lax.optimization_barrier((root_value, others))
        root_value = group_sum(
            jnp.broadcast_to(root_value, (8, *root_value.shape)), "flop", far.tolist()
        )
    else:
        root_value = lax.psum(copies[0], "turn")
    action_value = ((sums + others[0]) + (others[1] + others[2])) / TURNS
    node_zero = jnp.sum(sigma_flop * action_value, axis=0)
    new_flop = jnp.maximum(regrets_flop + action_value - node_zero[None, :], 0.0)
    return (new_flop[None], new_turn, root_value)


def solution(mesh):
    placed = (
        P(),
        P("flop", None, None),
        P("flop", None),
        P("flop", None),
        P("flop", "turn"),
        P("flop", "turn", None),
        P("flop", "turn", None, None),
        P("flop", "turn", None, None, None),
    )
    return jax.shard_map(
        on_device,
        mesh=mesh,
        in_specs=placed,
        out_specs=(P("flop", None, None), P("flop", "turn", None, None, None), P()),
        check_vma=False,
    )
```

```python
import jax
import jax.numpy as jnp
import numpy as np
from jax import lax
from jax.experimental import pallas as pl
from jax.experimental.pallas import tpu as pltpu
from jax.sharding import PartitionSpec as P

CARDS = 52
H = 1326
HP = 1408
LEFT = 48
C = 1128
CP = 1152
A = 4
TURNS = 49
TS = 24
RIV = 2
FLOPS = 64
NEAR = 16
BLOCK = 256
ROWS = 128
BIG = 2.0**126

bet_sizes = (0.25, 0.5, 1.0, 2.0)
card_low, card_high = np.triu_indices(CARDS, 1)
growth = 1.0 + 2.0 * np.asarray(bet_sizes)
pot = (np.outer(growth, growth) / (2.0 * H * RIV)).astype(np.float32)


def spread_rows(values, rows, fill):
    out = np.full((rows * 128,), fill, np.int32)
    out[: len(values)] = values
    return out.reshape(rows, 128)


def tables():
    low, high = np.triu_indices(LEFT, 1)
    index = np.stack(
        [
            spread_rows(low, 16, 0),
            spread_rows(high, 16, 1),
            spread_rows(card_low, 16, 0),
            spread_rows(card_high, 16, 1),
        ]
    )
    disjoint = np.zeros((CP, CP), np.float32)
    disjoint[:C, :C] = (
        (low[:, None] != low[None, :])
        & (low[:, None] != high[None, :])
        & (high[:, None] != low[None, :])
        & (high[:, None] != high[None, :])
    )
    return index, disjoint.astype(jnp.bfloat16)


BLOCKS = [(start, min(ROWS, 1136 - start)) for start in range(0, CP, ROWS)]


def swap_halves(x):
    return jnp.concatenate([x[4:8], x[0:4]], axis=0)


def rounded(x):
    return x.astype(jnp.bfloat16).astype(jnp.float32)


def kernel(
    flop_cards, live_turns, turn_card, river_cards,
    ranges_in, flop_regret_in, strength_in, turn_regret, index_in, keep_in,
    new_turn, sums, copies, root,
    ranges, flop_regret, strength, index, keep,
    regrets, wide_a, wide_b, lane_a, lane_b, alive_a, alive_b, columns_a, columns_b,
    found_a, found_b, back_a, back_b, spread_a, spread_b, total, one_total, blank,
    small_sems, keep_sems, in_sems, out_sems,
):
    wides, lanes, alives = (wide_a, wide_b), (lane_a, lane_b), (alive_a, alive_b)
    columnses, founds, backs = (columns_a, columns_b), (found_a, found_b), (back_a, back_b)
    spreads = (spread_a, spread_b)
    me = lax.axis_index("turn")
    count = live_turns[0, me]
    pairs = (count + 1) // 2
    used = 2 * pairs

    def regret_copy(slot, b):
        return pltpu.make_async_copy(
            turn_regret.at[0, slot, :, b],
            regrets.at[slot, b // 2, pl.ds((b % 2) * 4, 4)],
            in_sems.at[slot, b],
        )

    def result_copy(slot, b):
        return pltpu.make_async_copy(
            regrets.at[slot, b // 2, pl.ds((b % 2) * 4, 4)],
            new_turn.at[0, slot, :, b],
            out_sems.at[slot, b],
        )

    def blank_copy(slot):
        return pltpu.make_async_copy(blank, new_turn.at[0, slot], out_sems.at[slot, 0])

    small = [
        pltpu.make_async_copy(source, target, small_sems.at[n])
        for n, (source, target) in enumerate(
            [
                (ranges_in, ranges),
                (flop_regret_in, flop_regret),
                (index_in, index),
                (strength_in, strength),
            ]
        )
    ]
    masks = [
        pltpu.make_async_copy(
            keep_in.at[pl.ds(start, ROWS)],
            keep.at[pl.ds(start, ROWS)],
            keep_sems.at[n],
        )
        for n, (start, rows) in enumerate(BLOCKS)
    ]
    for copy in small:
        copy.start()
    for b in range(A):
        regret_copy(0, b).start()
    for copy in masks:
        copy.start()

    def fetch(slot, carry):
        for b in range(A):
            regret_copy(slot, b).start()
        return carry

    lax.fori_loop(1, used, fetch, 0)
    blank[...] = jnp.zeros_like(blank)

    def clear(slot, carry):
        blank_copy(slot).start()
        return carry

    lax.fori_loop(used, TS, clear, 0)
    for ref in wides + backs:
        ref[...] = jnp.zeros_like(ref)
    total[...] = jnp.zeros_like(total)
    one_total[...] = jnp.zeros_like(one_total)
    for copy in small:
        copy.wait()

    regrets_flop = flop_regret[0]
    sigma_flop = regrets_flop / jnp.sum(regrets_flop, axis=0, keepdims=True)
    reach_zero = rounded(ranges[0:1, :] * sigma_flop)
    for wide in wides:
        wide[1, 0:4, :H] = reach_zero
    first_card, second_card, third_card = (flop_cards[0, n] for n in range(3))
    first_card, second_card = jnp.minimum(first_card, second_card), jnp.maximum(first_card, second_card)
    second_card, third_card = jnp.minimum(second_card, third_card), jnp.maximum(second_card, third_card)
    first_card, second_card = jnp.minimum(first_card, second_card), jnp.maximum(first_card, second_card)
    row = lax.broadcasted_iota(jnp.int32, (8, 1), 0)
    upper = row < 4
    pots = []
    for k in range(2):
        column = jnp.zeros((8, 1), jnp.float32)
        for n in range(8):
            column = jnp.where(row == n, float(pot[n % 4, 2 * k + n // 4]), column)
        pots.append(column)
    for copy in masks:
        copy.wait()

    def prepare(slot, side):
        wide, lane, alive, columns, spread = wides[side], lanes[side], alives[side], columnses[side], spreads[side]
        for b in range(A):
            regret_copy(slot, b).wait()
        first, second = regrets[slot, 0], regrets[slot, 1]
        summed = first + second
        inverse = 1.0 / (summed + swap_halves(summed))
        sigma_first, sigma_second = first * inverse, second * inverse
        second_range = ranges[1:2, :]
        weight = (
            rounded(second_range * sigma_first) * pots[0]
            + rounded(second_range * sigma_second) * pots[1]
        )
        weight = weight + swap_halves(weight)
        wide[0, :, :H] = jnp.where(upper, weight, weight - rounded(weight))
        spreading = sigma_first * pots[0] + sigma_second * pots[1]
        spread[...] = spreading + swap_halves(spreading)
        wide[1, 4:6, :H] = strength[0, slot] * BIG

        dead, card = [], turn_card[0, slot]
        for flop_card in (first_card, second_card, third_card):
            dead.append(jnp.minimum(flop_card, card))
            card = jnp.maximum(flop_card, card)
        dead.append(card)
        low, high = index[0], index[1]
        for card in dead:
            low = low + (low >= card).astype(jnp.int32)
            high = high + (high >= card).astype(jnp.int32)
        lane[0] = ((low * (2 * CARDS - 1 - low)) >> 1) + high - low - 1
        for r in range(RIV):
            river = river_cards[0, r, slot]
            alive[r] = jnp.where((low == river) | (high == river), 0.0, -1.0)
        low, high = index[2], index[3]
        lost = (low == dead[0]) | (high == dead[0])
        for card in dead[1:]:
            lost = lost | (low == card) | (high == card)
        less_low, less_high = jnp.zeros_like(low), jnp.zeros_like(high)
        for card in dead:
            less_low = less_low + (low > card).astype(jnp.int32)
            less_high = less_high + (high > card).astype(jnp.int32)
        low, high = low - less_low, high - less_high
        place = ((low * (2 * LEFT - 1 - low)) >> 1) + high - low - 1
        lane[1] = jnp.where(lost, -1, place)

        packed = [[], []]
        for k in range(CP // 128):
            offset = jnp.broadcast_to(lane[0, k : k + 1, :], (8, 128)) - 128 * k
            spot = offset & 127
            for group in range(2):
                parts = [
                    jnp.take_along_axis(
                        wide[group, :, 128 * (k + m) : 128 * (k + m + 1)], spot, axis=1
                    )
                    for m in range(3)
                ]
                packed[group].append(
                    jnp.where(offset < 128, parts[0], jnp.where(offset < 256, parts[1], parts[2]))
                )
        columns[...] = jnp.concatenate(packed[1], axis=1).T
        given = []
        for r in range(RIV):
            pieces = []
            for k in range(CP // 128):
                mask = -alive[r, k : k + 1, :]
                zeros = jnp.where(upper, packed[1][k], swap_halves(packed[1][k]))
                pieces.append(
                    jnp.concatenate([packed[0][k] * mask, zeros * mask], axis=0).astype(jnp.bfloat16)
                )
            given.append(jnp.concatenate(pieces, axis=1))
        return packed, given

    def multiply(side, packed, given):
        columns, found = columnses[side], founds[side]
        for start, rows in BLOCKS:
            own = [
                jnp.broadcast_to(columns[start : start + rows, 4 + r : 5 + r], (rows, 128))
                for r in range(RIV)
            ]
            for other in range(0, CP, BLOCK):
                stop = min(other + BLOCK, CP)
                most = keep[start : start + rows, other:stop]
                least = -most
                for r in range(RIV):
                    gap = jnp.concatenate(
                        [
                            own[r] - packed[1][k][4 + r : 5 + r, :]
                            for k in range(other // 128, stop // 128)
                        ],
                        axis=1,
                    ).astype(jnp.bfloat16)
                    outcome = jnp.maximum(jnp.minimum(gap, most), least)
                    gave = jnp.dot(
                        given[r][:, start : start + rows], outcome,
                        preferred_element_type=jnp.float32,
                    )
                    if start == 0:
                        found[r, :, other:stop] = gave
                    else:
                        found[r, :, other:stop] += gave

    def finish(slot, side, live):
        lane, alive, found = lanes[side], alives[side], founds[side]
        back, spread = backs[side], spreads[side]
        merged = []
        for k in range(CP // 128):
            values = [
                found[r, :, 128 * k : 128 * (k + 1)] * alive[r, k : k + 1, :] for r in range(RIV)
            ]
            values = values[0] + values[1]
            merged.append(
                jnp.where(upper, values[0:8] + swap_halves(values[0:8]), values[8:16])
            )
        for k in range(HP // 128):
            place = jnp.broadcast_to(lane[1, k : k + 1, :], (8, 128))
            spot = place & 127
            result = jnp.zeros((8, 128), jnp.float32)
            for m in range(max(0, k - 2), min(k + 1, CP // 128)):
                part = jnp.take_along_axis(merged[m], spot, axis=1)
                result = jnp.where((place >> 7) == m, part, result)
            if live is not None:
                result = result * live
            total[:, 128 * k : 128 * (k + 1)] += result
            back[:, 128 * k : 128 * (k + 1)] = jnp.where(upper, swap_halves(result), result)
        against = back[:, :H]
        spreading = spread[...]
        one_total[...] += against * spreading
        for k in range(2):
            updated = jnp.maximum(regrets[slot, k] + against * (pots[k] - spreading), 0.0)
            regrets[slot, k] = updated if live is None else updated * live
        for b in range(A):
            result_copy(slot, b).start()


    def pair_step(pair, carry):
        slots = (2 * pair, 2 * pair + 1)
        live = (None, (slots[1] < count).astype(jnp.float32))
        ready = [prepare(slots[side], side) for side in range(2)]
        for side in range(2):
            multiply(side, *ready[side])
            finish(slots[side], side, live[side])
        return carry

    lax.fori_loop(0, pairs, pair_step, 0)
    whole = total[0:4, :H]
    sums[...] = whole
    scale = 1.0 / (TURNS * FLOPS)
    parts = jnp.concatenate(
        [
            jnp.sum(sigma_flop * whole, axis=0, keepdims=True) * scale,
            jnp.sum(one_total[0:4, :], axis=0, keepdims=True) * scale,
        ],
        axis=0,
    )
    for n in range(NEAR):
        copies[n] = parts
    root[...] = sigma_flop

    def settle(slot, carry):
        for b in range(A):
            result_copy(slot, b).wait()
        return carry

    lax.fori_loop(0, used, settle, 0)

    def settle_blank(slot, carry):
        blank_copy(slot).wait()
        return carry

    lax.fori_loop(used, TS, settle_blank, 0)


def group_sum(copies, axis, groups):
    return jnp.sum(
        lax.all_to_all(copies, axis, 0, 0, axis_index_groups=groups, tiled=True), axis=0
    )


def flip_sum(x, axis, flip):
    size = lax.axis_size(axis)
    return x + lax.ppermute(x, axis, [(n, n ^ flip) for n in range(size)])


def on_device(
    ranges, flop_regret, flop_cards, live_turns, turn_card, river_cards, strength, turn_regret
):
    index, disjoint = tables()
    smem = pl.BlockSpec(memory_space=pltpu.SMEM)
    vmem = pl.BlockSpec(memory_space=pltpu.VMEM)
    hbm = pl.BlockSpec(memory_space=pltpu.HBM)
    new_turn, sums, copies, sigma_flop = pl.pallas_call(
        kernel,
        out_shape=(
            jax.ShapeDtypeStruct(turn_regret.shape, jnp.float32),
            jax.ShapeDtypeStruct((A, H), jnp.float32),
            jax.ShapeDtypeStruct((NEAR, 2, H), jnp.float32),
            jax.ShapeDtypeStruct((A, H), jnp.float32),
        ),
        in_specs=[smem] * 4 + [hbm] * 6,
        out_specs=(hbm, vmem, vmem, vmem),
        scratch_shapes=[
            pltpu.VMEM((2, H), jnp.float32),
            pltpu.VMEM((1, A, H), jnp.float32),
            pltpu.VMEM((1, TS, RIV, H), jnp.float32),
            pltpu.VMEM((4, 16, 128), jnp.int32),
            pltpu.VMEM((CP, CP), jnp.bfloat16),
            pltpu.VMEM((TS, 2, 8, H), jnp.float32),
            *[pltpu.VMEM((2, 8, HP), jnp.float32)] * 2,
            *[pltpu.VMEM((2, 16, 128), jnp.int32)] * 2,
            *[pltpu.VMEM((RIV, 16, 128), jnp.float32)] * 2,
            *[pltpu.VMEM((CP, 8), jnp.float32)] * 2,
            *[pltpu.VMEM((RIV, 16, CP), jnp.float32)] * 2,
            *[pltpu.VMEM((8, HP), jnp.float32)] * 2,
            *[pltpu.VMEM((8, H), jnp.float32)] * 2,
            pltpu.VMEM((8, HP), jnp.float32),
            pltpu.VMEM((8, H), jnp.float32),
            pltpu.VMEM((A, A, H), jnp.float32),
            pltpu.SemaphoreType.DMA((4,)),
            pltpu.SemaphoreType.DMA((len(BLOCKS),)),
            pltpu.SemaphoreType.DMA((TS, A)),
            pltpu.SemaphoreType.DMA((TS, A)),
        ],
        compiler_params=pltpu.CompilerParams(vmem_limit_bytes=60 * 1024 * 1024),
        name="subtrees",
    )(
        flop_cards, live_turns, turn_card, jnp.swapaxes(river_cards, 1, 2),
        ranges, flop_regret, strength, turn_regret, jnp.asarray(index), jnp.asarray(disjoint),
    )
    regrets_flop = flop_regret[0]
    others = [lax.ppermute(sums, "turn", [(n, n ^ flip) for n in range(4)]) for flip in (1, 2, 3)]
    if lax.axis_size("flop") == FLOPS:
        near = np.arange(4 * FLOPS).reshape(8, 4, 2, 4).transpose(0, 2, 1, 3).reshape(16, NEAR)
        far = np.arange(FLOPS).reshape(8, 8).T
        root_value = group_sum(copies, ("flop", "turn"), near.tolist())
        root_value = flip_sum(root_value, "flop", 1)
        root_value, others = lax.optimization_barrier((root_value, others))
        root_value = group_sum(
            jnp.broadcast_to(root_value, (8, *root_value.shape)), "flop", far.tolist()
        )
    else:
        root_value = lax.psum(copies[0], "turn")
    action_value = ((sums + others[0]) + (others[1] + others[2])) / TURNS
    node_zero = jnp.sum(sigma_flop * action_value, axis=0)
    new_flop = jnp.maximum(regrets_flop + action_value - node_zero[None, :], 0.0)
    return (new_flop[None], new_turn, root_value)


def solution(mesh):
    placed = (
        P(),
        P("flop", None, None),
        P("flop", None),
        P("flop", None),
        P("flop", "turn"),
        P("flop", "turn", None),
        P("flop", "turn", None, None),
        P("flop", "turn", None, None, None),
    )
    return jax.shard_map(
        on_device,
        mesh=mesh,
        in_specs=placed,
        out_specs=(P("flop", None, None), P("flop", "turn", None, None, None), P()),
        check_vma=False,
    )
```

```python
import jax
import jax.numpy as jnp
import numpy as np
from jax import lax
from jax.experimental import pallas as pl
from jax.experimental.pallas import tpu as pltpu
from jax.sharding import PartitionSpec as P

CARDS = 52
H = 1326
HP = 1408
LEFT = 48
C = 1128
CP = 1152
A = 4
TURNS = 49
TS = 24
SIDES = 4
RIV = 2
FLOPS = 64
NEAR = 16
BLOCK = 256
ROWS = 128
BIG = 2.0**126

bet_sizes = (0.25, 0.5, 1.0, 2.0)
card_low, card_high = np.triu_indices(CARDS, 1)
growth = 1.0 + 2.0 * np.asarray(bet_sizes)
pot = (np.outer(growth, growth) / (2.0 * H * RIV)).astype(np.float32)


def spread_rows(values, rows, fill):
    out = np.full((rows * 128,), fill, np.int32)
    out[: len(values)] = values
    return out.reshape(rows, 128)


def tables():
    low, high = np.triu_indices(LEFT, 1)
    index = np.stack(
        [
            spread_rows(low, 16, 0),
            spread_rows(high, 16, 1),
            spread_rows(card_low, 16, 0),
            spread_rows(card_high, 16, 1),
        ]
    )
    disjoint = np.zeros((CP, CP), np.float32)
    disjoint[:C, :C] = (
        (low[:, None] != low[None, :])
        & (low[:, None] != high[None, :])
        & (high[:, None] != low[None, :])
        & (high[:, None] != high[None, :])
    )
    return index, disjoint.astype(jnp.bfloat16)


BLOCKS = [(start, min(ROWS, 1136 - start)) for start in range(0, CP, ROWS)]


def swap_halves(x):
    return jnp.concatenate([x[4:8], x[0:4]], axis=0)


def rounded(x):
    return x.astype(jnp.bfloat16).astype(jnp.float32)


def kernel(
    flop_cards, live_turns, turn_card, river_cards,
    ranges_in, flop_regret_in, strength_in, turn_regret, index_in, keep_in,
    new_turn, sums, copies, root,
    ranges, flop_regret, strength, index, keep,
    regrets, wides, lanes, alives, columnses, founds, backs, spreads, total, one_total, blank,
    small_sems, keep_sems, in_sems, out_sems,
):
    me = lax.axis_index("turn")
    count = live_turns[0, me]
    steps = (count + SIDES - 1) // SIDES
    used = SIDES * steps

    def regret_copy(slot, b):
        return pltpu.make_async_copy(
            turn_regret.at[0, slot, :, b],
            regrets.at[slot, b // 2, pl.ds((b % 2) * 4, 4)],
            in_sems.at[slot, b],
        )

    def result_copy(slot, b):
        return pltpu.make_async_copy(
            regrets.at[slot, b // 2, pl.ds((b % 2) * 4, 4)],
            new_turn.at[0, slot, :, b],
            out_sems.at[slot, b],
        )

    def blank_copy(slot):
        return pltpu.make_async_copy(blank, new_turn.at[0, slot], out_sems.at[slot, 0])

    small = [
        pltpu.make_async_copy(source, target, small_sems.at[n])
        for n, (source, target) in enumerate(
            [
                (ranges_in, ranges),
                (flop_regret_in, flop_regret),
                (index_in, index),
                (strength_in, strength),
            ]
        )
    ]
    masks = [
        pltpu.make_async_copy(
            keep_in.at[pl.ds(start, ROWS)],
            keep.at[pl.ds(start, ROWS)],
            keep_sems.at[n],
        )
        for n, (start, rows) in enumerate(BLOCKS)
    ]
    for copy in small:
        copy.start()
    for b in range(A):
        regret_copy(0, b).start()
    for copy in masks:
        copy.start()

    def fetch(slot, carry):
        for b in range(A):
            regret_copy(slot, b).start()
        return carry

    lax.fori_loop(1, used, fetch, 0)
    blank[...] = jnp.zeros_like(blank)

    def clear(slot, carry):
        blank_copy(slot).start()
        return carry

    lax.fori_loop(used, TS, clear, 0)
    for ref in wides + backs:
        ref[...] = jnp.zeros_like(ref)
    total[...] = jnp.zeros_like(total)
    one_total[...] = jnp.zeros_like(one_total)
    for copy in small:
        copy.wait()

    regrets_flop = flop_regret[0]
    sigma_flop = regrets_flop / jnp.sum(regrets_flop, axis=0, keepdims=True)
    reach_zero = rounded(ranges[0:1, :] * sigma_flop)
    for wide in wides:
        wide[1, 0:4, :H] = reach_zero
    first_card, second_card, third_card = (flop_cards[0, n] for n in range(3))
    first_card, second_card = jnp.minimum(first_card, second_card), jnp.maximum(first_card, second_card)
    second_card, third_card = jnp.minimum(second_card, third_card), jnp.maximum(second_card, third_card)
    first_card, second_card = jnp.minimum(first_card, second_card), jnp.maximum(first_card, second_card)
    row = lax.broadcasted_iota(jnp.int32, (8, 1), 0)
    upper = row < 4
    pots = []
    for k in range(2):
        column = jnp.zeros((8, 1), jnp.float32)
        for n in range(8):
            column = jnp.where(row == n, float(pot[n % 4, 2 * k + n // 4]), column)
        pots.append(column)
    for copy in masks:
        copy.wait()

    def prepare(slot, side):
        wide, lane, alive, columns, spread = wides[side], lanes[side], alives[side], columnses[side], spreads[side]
        for b in range(A):
            regret_copy(slot, b).wait()
        first, second = regrets[slot, 0], regrets[slot, 1]
        summed = first + second
        inverse = 1.0 / (summed + swap_halves(summed))
        sigma_first, sigma_second = first * inverse, second * inverse
        second_range = ranges[1:2, :]
        weight = (
            rounded(second_range * sigma_first) * pots[0]
            + rounded(second_range * sigma_second) * pots[1]
        )
        weight = weight + swap_halves(weight)
        wide[0, :, :H] = jnp.where(upper, weight, weight - rounded(weight))
        spreading = sigma_first * pots[0] + sigma_second * pots[1]
        spread[...] = spreading + swap_halves(spreading)
        wide[1, 4:6, :H] = strength[0, slot] * BIG

        dead, card = [], turn_card[0, slot]
        for flop_card in (first_card, second_card, third_card):
            dead.append(jnp.minimum(flop_card, card))
            card = jnp.maximum(flop_card, card)
        dead.append(card)
        low, high = index[0], index[1]
        for card in dead:
            low = low + (low >= card).astype(jnp.int32)
            high = high + (high >= card).astype(jnp.int32)
        lane[0] = ((low * (2 * CARDS - 1 - low)) >> 1) + high - low - 1
        for r in range(RIV):
            river = river_cards[0, r, slot]
            alive[r] = jnp.where((low == river) | (high == river), 0.0, -1.0)
        low, high = index[2], index[3]
        lost = (low == dead[0]) | (high == dead[0])
        for card in dead[1:]:
            lost = lost | (low == card) | (high == card)
        less_low, less_high = jnp.zeros_like(low), jnp.zeros_like(high)
        for card in dead:
            less_low = less_low + (low > card).astype(jnp.int32)
            less_high = less_high + (high > card).astype(jnp.int32)
        low, high = low - less_low, high - less_high
        place = ((low * (2 * LEFT - 1 - low)) >> 1) + high - low - 1
        lane[1] = jnp.where(lost, -1, place)

        packed = [[], []]
        for k in range(CP // 128):
            offset = jnp.broadcast_to(lane[0, k : k + 1, :], (8, 128)) - 128 * k
            spot = offset & 127
            for group in range(2):
                parts = [
                    jnp.take_along_axis(
                        wide[group, :, 128 * (k + m) : 128 * (k + m + 1)], spot, axis=1
                    )
                    for m in range(3)
                ]
                packed[group].append(
                    jnp.where(offset < 128, parts[0], jnp.where(offset < 256, parts[1], parts[2]))
                )
        columns[...] = jnp.concatenate(packed[1], axis=1).T
        given = []
        for r in range(RIV):
            pieces = []
            for k in range(CP // 128):
                mask = -alive[r, k : k + 1, :]
                zeros = jnp.where(upper, packed[1][k], swap_halves(packed[1][k]))
                pieces.append(
                    jnp.concatenate([packed[0][k] * mask, zeros * mask], axis=0).astype(jnp.bfloat16)
                )
            given.append(jnp.concatenate(pieces, axis=1))
        return packed, given

    def multiply(side, packed, given):
        columns, found = columnses[side], founds[side]
        for start, rows in BLOCKS:
            own = [
                jnp.broadcast_to(columns[start : start + rows, 4 + r : 5 + r], (rows, 128))
                for r in range(RIV)
            ]
            for other in range(0, CP, BLOCK):
                stop = min(other + BLOCK, CP)
                most = keep[start : start + rows, other:stop]
                least = -most
                for r in range(RIV):
                    gap = jnp.concatenate(
                        [
                            own[r] - packed[1][k][4 + r : 5 + r, :]
                            for k in range(other // 128, stop // 128)
                        ],
                        axis=1,
                    ).astype(jnp.bfloat16)
                    outcome = jnp.maximum(jnp.minimum(gap, most), least)
                    gave = jnp.dot(
                        given[r][:, start : start + rows], outcome,
                        preferred_element_type=jnp.float32,
                    )
                    if start == 0:
                        found[r, :, other:stop] = gave
                    else:
                        found[r, :, other:stop] += gave

    def finish(slot, side, live):
        lane, alive, found = lanes[side], alives[side], founds[side]
        back, spread = backs[side], spreads[side]
        merged = []
        for k in range(CP // 128):
            values = [
                found[r, :, 128 * k : 128 * (k + 1)] * alive[r, k : k + 1, :] for r in range(RIV)
            ]
            values = values[0] + values[1]
            merged.append(
                jnp.where(upper, values[0:8] + swap_halves(values[0:8]), values[8:16])
            )
        for k in range(HP // 128):
            place = jnp.broadcast_to(lane[1, k : k + 1, :], (8, 128))
            spot = place & 127
            result = jnp.zeros((8, 128), jnp.float32)
            for m in range(max(0, k - 2), min(k + 1, CP // 128)):
                part = jnp.take_along_axis(merged[m], spot, axis=1)
                result = jnp.where((place >> 7) == m, part, result)
            if live is not None:
                result = result * live
            total[:, 128 * k : 128 * (k + 1)] += result
            back[:, 128 * k : 128 * (k + 1)] = jnp.where(upper, swap_halves(result), result)
        against = back[:, :H]
        spreading = spread[...]
        one_total[...] += against * spreading
        for k in range(2):
            updated = jnp.maximum(regrets[slot, k] + against * (pots[k] - spreading), 0.0)
            regrets[slot, k] = updated if live is None else updated * live
        for b in range(A):
            result_copy(slot, b).start()


    def group_step(group, carry):
        slots = [SIDES * group + side for side in range(SIDES)]
        ready = [prepare(slots[0], 0)]
        for side in range(SIDES):
            if side + 1 < SIDES:
                ready.append(prepare(slots[side + 1], side + 1))
            multiply(side, *ready[side])
            live = (slots[side] < count).astype(jnp.float32) if side else None
            finish(slots[side], side, live)
        return carry

    lax.fori_loop(0, steps, group_step, 0)
    whole = total[0:4, :H]
    sums[...] = whole
    scale = 1.0 / (TURNS * FLOPS)
    parts = jnp.concatenate(
        [
            jnp.sum(sigma_flop * whole, axis=0, keepdims=True) * scale,
            jnp.sum(one_total[0:4, :], axis=0, keepdims=True) * scale,
        ],
        axis=0,
    )
    for n in range(NEAR):
        copies[n] = parts
    root[...] = sigma_flop

    def settle(slot, carry):
        for b in range(A):
            result_copy(slot, b).wait()
        return carry

    lax.fori_loop(0, used, settle, 0)

    def settle_blank(slot, carry):
        blank_copy(slot).wait()
        return carry

    lax.fori_loop(used, TS, settle_blank, 0)


def group_sum(copies, axis, groups):
    return jnp.sum(
        lax.all_to_all(copies, axis, 0, 0, axis_index_groups=groups, tiled=True), axis=0
    )


def flip_sum(x, axis, flip):
    size = lax.axis_size(axis)
    return x + lax.ppermute(x, axis, [(n, n ^ flip) for n in range(size)])


def on_device(
    ranges, flop_regret, flop_cards, live_turns, turn_card, river_cards, strength, turn_regret
):
    index, disjoint = tables()
    smem = pl.BlockSpec(memory_space=pltpu.SMEM)
    vmem = pl.BlockSpec(memory_space=pltpu.VMEM)
    hbm = pl.BlockSpec(memory_space=pltpu.HBM)
    new_turn, sums, copies, sigma_flop = pl.pallas_call(
        kernel,
        out_shape=(
            jax.ShapeDtypeStruct(turn_regret.shape, jnp.float32),
            jax.ShapeDtypeStruct((A, H), jnp.float32),
            jax.ShapeDtypeStruct((NEAR, 2, H), jnp.float32),
            jax.ShapeDtypeStruct((A, H), jnp.float32),
        ),
        in_specs=[smem] * 4 + [hbm] * 6,
        out_specs=(hbm, vmem, vmem, vmem),
        scratch_shapes=[
            pltpu.VMEM((2, H), jnp.float32),
            pltpu.VMEM((1, A, H), jnp.float32),
            pltpu.VMEM((1, TS, RIV, H), jnp.float32),
            pltpu.VMEM((4, 16, 128), jnp.int32),
            pltpu.VMEM((CP, CP), jnp.bfloat16),
            pltpu.VMEM((TS, 2, 8, H), jnp.float32),
            [pltpu.VMEM((2, 8, HP), jnp.float32)] * SIDES,
            [pltpu.VMEM((2, 16, 128), jnp.int32)] * SIDES,
            [pltpu.VMEM((RIV, 16, 128), jnp.float32)] * SIDES,
            [pltpu.VMEM((CP, 8), jnp.float32)] * SIDES,
            [pltpu.VMEM((RIV, 16, CP), jnp.float32)] * SIDES,
            [pltpu.VMEM((8, HP), jnp.float32)] * SIDES,
            [pltpu.VMEM((8, H), jnp.float32)] * SIDES,
            pltpu.VMEM((8, HP), jnp.float32),
            pltpu.VMEM((8, H), jnp.float32),
            pltpu.VMEM((A, A, H), jnp.float32),
            pltpu.SemaphoreType.DMA((4,)),
            pltpu.SemaphoreType.DMA((len(BLOCKS),)),
            pltpu.SemaphoreType.DMA((TS, A)),
            pltpu.SemaphoreType.DMA((TS, A)),
        ],
        compiler_params=pltpu.CompilerParams(vmem_limit_bytes=60 * 1024 * 1024),
        name="subtrees",
    )(
        flop_cards, live_turns, turn_card, jnp.swapaxes(river_cards, 1, 2),
        ranges, flop_regret, strength, turn_regret, jnp.asarray(index), jnp.asarray(disjoint),
    )
    regrets_flop = flop_regret[0]
    others = [lax.ppermute(sums, "turn", [(n, n ^ flip) for n in range(4)]) for flip in (1, 2, 3)]
    if lax.axis_size("flop") == FLOPS:
        near = np.arange(4 * FLOPS).reshape(8, 4, 2, 4).transpose(0, 2, 1, 3).reshape(16, NEAR)
        far = np.arange(FLOPS).reshape(8, 8).T
        root_value = group_sum(copies, ("flop", "turn"), near.tolist())
        root_value = flip_sum(root_value, "flop", 1)
        root_value, others = lax.optimization_barrier((root_value, others))
        root_value = group_sum(
            jnp.broadcast_to(root_value, (8, *root_value.shape)), "flop", far.tolist()
        )
    else:
        root_value = lax.psum(copies[0], "turn")
    action_value = ((sums + others[0]) + (others[1] + others[2])) / TURNS
    node_zero = jnp.sum(sigma_flop * action_value, axis=0)
    new_flop = jnp.maximum(regrets_flop + action_value - node_zero[None, :], 0.0)
    return (new_flop[None], new_turn, root_value)


def solution(mesh):
    placed = (
        P(),
        P("flop", None, None),
        P("flop", None),
        P("flop", None),
        P("flop", "turn"),
        P("flop", "turn", None),
        P("flop", "turn", None, None),
        P("flop", "turn", None, None, None),
    )
    return jax.shard_map(
        on_device,
        mesh=mesh,
        in_specs=placed,
        out_specs=(P("flop", None, None), P("flop", "turn", None, None, None), P()),
        check_vma=False,
    )
```

```python
import jax
import jax.numpy as jnp
import numpy as np
from jax import lax
from jax.experimental import pallas as pl
from jax.experimental.pallas import tpu as pltpu
from jax.sharding import PartitionSpec as P

CARDS = 52
H = 1326
HP = 1408
LEFT = 48
C = 1128
CP = 1152
A = 4
TURNS = 49
TS = 24
SIDES = 4
RIV = 2
FLOPS = 64
NEAR = 16
BLOCK = 256
ROWS = 128
BIG = 2.0**126

bet_sizes = (0.25, 0.5, 1.0, 2.0)
card_low, card_high = np.triu_indices(CARDS, 1)
growth = 1.0 + 2.0 * np.asarray(bet_sizes)
pot = (np.outer(growth, growth) / (2.0 * H * RIV)).astype(np.float32)


def spread_rows(values, rows, fill):
    out = np.full((rows * 128,), fill, np.int32)
    out[: len(values)] = values
    return out.reshape(rows, 128)


def tables():
    low, high = np.triu_indices(LEFT, 1)
    index = np.stack(
        [
            spread_rows(low, 16, 0),
            spread_rows(high, 16, 1),
            spread_rows(card_low, 16, 0),
            spread_rows(card_high, 16, 1),
        ]
    )
    disjoint = np.zeros((CP, CP), np.float32)
    disjoint[:C, :C] = (
        (low[:, None] != low[None, :])
        & (low[:, None] != high[None, :])
        & (high[:, None] != low[None, :])
        & (high[:, None] != high[None, :])
    )
    return index, disjoint.astype(jnp.bfloat16)


BLOCKS = [(start, min(ROWS, 1136 - start)) for start in range(0, CP, ROWS)]


def swap_halves(x):
    return jnp.concatenate([x[4:8], x[0:4]], axis=0)


def rounded(x):
    return x.astype(jnp.bfloat16).astype(jnp.float32)


def kernel(
    flop_cards, live_turns, turn_card, river_cards,
    ranges_in, flop_regret_in, strength_in, turn_regret, index_in, keep_in,
    new_turn, sums, copies, root,
    ranges, flop_regret, strength, index, keep,
    regrets, wides, lanes, alives, columnses, founds, backs, spreads, total, one_total, blank,
    small_sems, keep_sems, in_sems, out_sems,
):
    me = lax.axis_index("turn")
    count = live_turns[0, me]
    steps = (count + SIDES - 1) // SIDES
    used = SIDES * steps

    def regret_copy(slot, b):
        return pltpu.make_async_copy(
            turn_regret.at[0, jnp.minimum(slot, TS - 1), :, b],
            regrets.at[slot, b // 2, pl.ds((b % 2) * 4, 4)],
            in_sems.at[slot, b],
        )

    def result_copy(slot, b):
        return pltpu.make_async_copy(
            regrets.at[slot, b // 2, pl.ds((b % 2) * 4, 4)],
            new_turn.at[0, slot, :, b],
            out_sems.at[slot, b],
        )

    def blank_copy(slot):
        return pltpu.make_async_copy(blank, new_turn.at[0, slot], out_sems.at[slot, 0])

    small = [
        pltpu.make_async_copy(source, target, small_sems.at[n])
        for n, (source, target) in enumerate(
            [
                (ranges_in, ranges),
                (flop_regret_in, flop_regret),
                (index_in, index),
                (strength_in, strength),
            ]
        )
    ]
    masks = [
        pltpu.make_async_copy(
            keep_in.at[pl.ds(start, ROWS)],
            keep.at[pl.ds(start, ROWS)],
            keep_sems.at[n],
        )
        for n, (start, rows) in enumerate(BLOCKS)
    ]
    for copy in small:
        copy.start()
    for b in range(A):
        regret_copy(0, b).start()
    for copy in masks:
        copy.start()

    def fetch(slot, carry):
        for b in range(A):
            regret_copy(slot, b).start()
        return carry

    lax.fori_loop(1, used + 1, fetch, 0)
    blank[...] = jnp.zeros_like(blank)

    def clear(slot, carry):
        blank_copy(slot).start()
        return carry

    lax.fori_loop(used, TS, clear, 0)
    for ref in wides + backs:
        ref[...] = jnp.zeros_like(ref)
    total[...] = jnp.zeros_like(total)
    one_total[...] = jnp.zeros_like(one_total)
    for copy in small:
        copy.wait()

    regrets_flop = flop_regret[0]
    sigma_flop = regrets_flop / jnp.sum(regrets_flop, axis=0, keepdims=True)
    reach_zero = rounded(ranges[0:1, :] * sigma_flop)
    for wide in wides:
        wide[1, 0:4, :H] = reach_zero
    first_card, second_card, third_card = (flop_cards[0, n] for n in range(3))
    first_card, second_card = jnp.minimum(first_card, second_card), jnp.maximum(first_card, second_card)
    second_card, third_card = jnp.minimum(second_card, third_card), jnp.maximum(second_card, third_card)
    first_card, second_card = jnp.minimum(first_card, second_card), jnp.maximum(first_card, second_card)
    row = lax.broadcasted_iota(jnp.int32, (8, 1), 0)
    upper = row < 4
    pots = []
    for k in range(2):
        column = jnp.zeros((8, 1), jnp.float32)
        for n in range(8):
            column = jnp.where(row == n, float(pot[n % 4, 2 * k + n // 4]), column)
        pots.append(column)
    def prepare(slot, side):
        source = jnp.minimum(slot, TS - 1)
        wide, lane, alive, columns, spread = wides[side], lanes[side], alives[side], columnses[side], spreads[side]
        for b in range(A):
            regret_copy(slot, b).wait()
        first, second = regrets[slot, 0], regrets[slot, 1]
        summed = first + second
        inverse = 1.0 / (summed + swap_halves(summed))
        sigma_first, sigma_second = first * inverse, second * inverse
        second_range = ranges[1:2, :]
        weight = (
            rounded(second_range * sigma_first) * pots[0]
            + rounded(second_range * sigma_second) * pots[1]
        )
        weight = weight + swap_halves(weight)
        wide[0, :, :H] = jnp.where(upper, weight, weight - rounded(weight))
        spreading = sigma_first * pots[0] + sigma_second * pots[1]
        spread[...] = spreading + swap_halves(spreading)
        wide[1, 4:6, :H] = strength[0, source] * BIG

        dead, card = [], turn_card[0, source]
        for flop_card in (first_card, second_card, third_card):
            dead.append(jnp.minimum(flop_card, card))
            card = jnp.maximum(flop_card, card)
        dead.append(card)
        low, high = index[0], index[1]
        for card in dead:
            low = low + (low >= card).astype(jnp.int32)
            high = high + (high >= card).astype(jnp.int32)
        lane[0] = ((low * (2 * CARDS - 1 - low)) >> 1) + high - low - 1
        for r in range(RIV):
            river = river_cards[0, r, source]
            alive[r] = jnp.where((low == river) | (high == river), 0.0, -1.0)
        low, high = index[2], index[3]
        lost = (low == dead[0]) | (high == dead[0])
        for card in dead[1:]:
            lost = lost | (low == card) | (high == card)
        less_low, less_high = jnp.zeros_like(low), jnp.zeros_like(high)
        for card in dead:
            less_low = less_low + (low > card).astype(jnp.int32)
            less_high = less_high + (high > card).astype(jnp.int32)
        low, high = low - less_low, high - less_high
        place = ((low * (2 * LEFT - 1 - low)) >> 1) + high - low - 1
        lane[1] = jnp.where(lost, -1, place)

        packed = [[], []]
        for k in range(CP // 128):
            offset = jnp.broadcast_to(lane[0, k : k + 1, :], (8, 128)) - 128 * k
            spot = offset & 127
            for group in range(2):
                parts = [
                    jnp.take_along_axis(
                        wide[group, :, 128 * (k + m) : 128 * (k + m + 1)], spot, axis=1
                    )
                    for m in range(3)
                ]
                packed[group].append(
                    jnp.where(offset < 128, parts[0], jnp.where(offset < 256, parts[1], parts[2]))
                )
        columns[...] = jnp.concatenate(packed[1], axis=1).T
        given = []
        for r in range(RIV):
            pieces = []
            for k in range(CP // 128):
                mask = -alive[r, k : k + 1, :]
                zeros = jnp.where(upper, packed[1][k], swap_halves(packed[1][k]))
                pieces.append(
                    jnp.concatenate([packed[0][k] * mask, zeros * mask], axis=0).astype(jnp.bfloat16)
                )
            given.append(jnp.concatenate(pieces, axis=1))
        return packed, given

    def multiply(side, packed, given):
        columns, found = columnses[side], founds[side]
        for start, rows in BLOCKS:
            own = [
                jnp.broadcast_to(columns[start : start + rows, 4 + r : 5 + r], (rows, 128))
                for r in range(RIV)
            ]
            for other in range(0, CP, BLOCK):
                stop = min(other + BLOCK, CP)
                most = keep[start : start + rows, other:stop]
                least = -most
                for r in range(RIV):
                    gap = jnp.concatenate(
                        [
                            own[r] - packed[1][k][4 + r : 5 + r, :]
                            for k in range(other // 128, stop // 128)
                        ],
                        axis=1,
                    ).astype(jnp.bfloat16)
                    outcome = jnp.maximum(jnp.minimum(gap, most), least)
                    gave = jnp.dot(
                        given[r][:, start : start + rows], outcome,
                        preferred_element_type=jnp.float32,
                    )
                    if start == 0:
                        found[r, :, other:stop] = gave
                    else:
                        found[r, :, other:stop] += gave

    def finish(slot, side, live):
        lane, alive, found = lanes[side], alives[side], founds[side]
        back, spread = backs[side], spreads[side]
        merged = []
        for k in range(CP // 128):
            values = [
                found[r, :, 128 * k : 128 * (k + 1)] * alive[r, k : k + 1, :] for r in range(RIV)
            ]
            values = values[0] + values[1]
            merged.append(
                jnp.where(upper, values[0:8] + swap_halves(values[0:8]), values[8:16])
            )
        for k in range(HP // 128):
            place = jnp.broadcast_to(lane[1, k : k + 1, :], (8, 128))
            spot = place & 127
            result = jnp.zeros((8, 128), jnp.float32)
            for m in range(max(0, k - 2), min(k + 1, CP // 128)):
                part = jnp.take_along_axis(merged[m], spot, axis=1)
                result = jnp.where((place >> 7) == m, part, result)
            if live is not None:
                result = result * live
            total[:, 128 * k : 128 * (k + 1)] += result
            back[:, 128 * k : 128 * (k + 1)] = jnp.where(upper, swap_halves(result), result)
        against = back[:, :H]
        spreading = spread[...]
        one_total[...] += against * spreading
        for k in range(2):
            updated = jnp.maximum(regrets[slot, k] + against * (pots[k] - spreading), 0.0)
            regrets[slot, k] = updated if live is None else updated * live
        for b in range(A):
            result_copy(slot, b).start()


    def group_step(group, carry):
        slots = [SIDES * group + side for side in range(SIDES)]
        ready = carry
        for side in range(SIDES):
            following = prepare(slots[side] + 1, (side + 1) % SIDES)
            multiply(side, *ready)
            ready = following
            live = (slots[side] < count).astype(jnp.float32) if side else None
            finish(slots[side], side, live)
        return ready

    first = prepare(0, 0)
    for copy in masks:
        copy.wait()
    lax.fori_loop(0, steps, group_step, first)
    whole = total[0:4, :H]
    sums[...] = whole
    scale = 1.0 / (TURNS * FLOPS)
    parts = jnp.concatenate(
        [
            jnp.sum(sigma_flop * whole, axis=0, keepdims=True) * scale,
            jnp.sum(one_total[0:4, :], axis=0, keepdims=True) * scale,
        ],
        axis=0,
    )
    for n in range(NEAR):
        copies[n] = parts
    root[...] = sigma_flop

    def settle(slot, carry):
        for b in range(A):
            result_copy(slot, b).wait()
        return carry

    lax.fori_loop(0, used, settle, 0)

    def settle_blank(slot, carry):
        blank_copy(slot).wait()
        return carry

    lax.fori_loop(used, TS, settle_blank, 0)


def group_sum(copies, axis, groups):
    return jnp.sum(
        lax.all_to_all(copies, axis, 0, 0, axis_index_groups=groups, tiled=True), axis=0
    )


def flip_sum(x, axis, flip):
    size = lax.axis_size(axis)
    return x + lax.ppermute(x, axis, [(n, n ^ flip) for n in range(size)])


def on_device(
    ranges, flop_regret, flop_cards, live_turns, turn_card, river_cards, strength, turn_regret
):
    index, disjoint = tables()
    smem = pl.BlockSpec(memory_space=pltpu.SMEM)
    vmem = pl.BlockSpec(memory_space=pltpu.VMEM)
    hbm = pl.BlockSpec(memory_space=pltpu.HBM)
    new_turn, sums, copies, sigma_flop = pl.pallas_call(
        kernel,
        out_shape=(
            jax.ShapeDtypeStruct(turn_regret.shape, jnp.float32),
            jax.ShapeDtypeStruct((A, H), jnp.float32),
            jax.ShapeDtypeStruct((NEAR, 2, H), jnp.float32),
            jax.ShapeDtypeStruct((A, H), jnp.float32),
        ),
        in_specs=[smem] * 4 + [hbm] * 6,
        out_specs=(hbm, vmem, vmem, vmem),
        scratch_shapes=[
            pltpu.VMEM((2, H), jnp.float32),
            pltpu.VMEM((1, A, H), jnp.float32),
            pltpu.VMEM((1, TS, RIV, H), jnp.float32),
            pltpu.VMEM((4, 16, 128), jnp.int32),
            pltpu.VMEM((CP, CP), jnp.bfloat16),
            pltpu.VMEM((TS + 1, 2, 8, H), jnp.float32),
            [pltpu.VMEM((2, 8, HP), jnp.float32)] * SIDES,
            [pltpu.VMEM((2, 16, 128), jnp.int32)] * SIDES,
            [pltpu.VMEM((RIV, 16, 128), jnp.float32)] * SIDES,
            [pltpu.VMEM((CP, 8), jnp.float32)] * SIDES,
            [pltpu.VMEM((RIV, 16, CP), jnp.float32)] * SIDES,
            [pltpu.VMEM((8, HP), jnp.float32)] * SIDES,
            [pltpu.VMEM((8, H), jnp.float32)] * SIDES,
            pltpu.VMEM((8, HP), jnp.float32),
            pltpu.VMEM((8, H), jnp.float32),
            pltpu.VMEM((A, A, H), jnp.float32),
            pltpu.SemaphoreType.DMA((4,)),
            pltpu.SemaphoreType.DMA((len(BLOCKS),)),
            pltpu.SemaphoreType.DMA((TS + 1, A)),
            pltpu.SemaphoreType.DMA((TS, A)),
        ],
        compiler_params=pltpu.CompilerParams(vmem_limit_bytes=60 * 1024 * 1024),
        name="subtrees",
    )(
        flop_cards, live_turns, turn_card, jnp.swapaxes(river_cards, 1, 2),
        ranges, flop_regret, strength, turn_regret, jnp.asarray(index), jnp.asarray(disjoint),
    )
    regrets_flop = flop_regret[0]
    others = [lax.ppermute(sums, "turn", [(n, n ^ flip) for n in range(4)]) for flip in (1, 2, 3)]
    if lax.axis_size("flop") == FLOPS:
        near = np.arange(4 * FLOPS).reshape(8, 4, 2, 4).transpose(0, 2, 1, 3).reshape(16, NEAR)
        far = np.arange(FLOPS).reshape(8, 8).T
        root_value = group_sum(copies, ("flop", "turn"), near.tolist())
        root_value = flip_sum(root_value, "flop", 1)
        root_value, others = lax.optimization_barrier((root_value, others))
        root_value = group_sum(
            jnp.broadcast_to(root_value, (8, *root_value.shape)), "flop", far.tolist()
        )
    else:
        root_value = lax.psum(copies[0], "turn")
    action_value = ((sums + others[0]) + (others[1] + others[2])) / TURNS
    node_zero = jnp.sum(sigma_flop * action_value, axis=0)
    new_flop = jnp.maximum(regrets_flop + action_value - node_zero[None, :], 0.0)
    return (new_flop[None], new_turn, root_value)


def solution(mesh):
    placed = (
        P(),
        P("flop", None, None),
        P("flop", None),
        P("flop", None),
        P("flop", "turn"),
        P("flop", "turn", None),
        P("flop", "turn", None, None),
        P("flop", "turn", None, None, None),
    )
    return jax.shard_map(
        on_device,
        mesh=mesh,
        in_specs=placed,
        out_specs=(P("flop", None, None), P("flop", "turn", None, None, None), P()),
        check_vma=False,
    )
```

```python
import jax
import jax.numpy as jnp
import numpy as np
from jax import lax
from jax.experimental import pallas as pl
from jax.experimental.pallas import tpu as pltpu
from jax.sharding import PartitionSpec as P

CARDS = 52
H = 1326
HP = 1408
LEFT = 48
C = 1128
CP = 1152
A = 4
TURNS = 49
TS = 24
SIDES = 4
RIV = 2
FLOPS = 64
NEAR = 16
BLOCK = 256
ROWS = 64
BIG = 2.0**126

bet_sizes = (0.25, 0.5, 1.0, 2.0)
card_low, card_high = np.triu_indices(CARDS, 1)
growth = 1.0 + 2.0 * np.asarray(bet_sizes)
pot = (np.outer(growth, growth) / (2.0 * H * RIV)).astype(np.float32)


def spread_rows(values, rows, fill):
    out = np.full((rows * 128,), fill, np.int32)
    out[: len(values)] = values
    return out.reshape(rows, 128)


def tables():
    low, high = np.triu_indices(LEFT, 1)
    index = np.stack(
        [
            spread_rows(low, 16, 0),
            spread_rows(high, 16, 1),
            spread_rows(card_low, 16, 0),
            spread_rows(card_high, 16, 1),
        ]
    )
    disjoint = np.zeros((CP, CP), np.float32)
    disjoint[:C, :C] = (
        (low[:, None] != low[None, :])
        & (low[:, None] != high[None, :])
        & (high[:, None] != low[None, :])
        & (high[:, None] != high[None, :])
    )
    return index, disjoint.astype(jnp.bfloat16)


BLOCKS = [(start, min(ROWS, 1136 - start)) for start in range(0, CP, ROWS)]


def swap_halves(x):
    return jnp.concatenate([x[4:8], x[0:4]], axis=0)


def rounded(x):
    return x.astype(jnp.bfloat16).astype(jnp.float32)


def kernel(
    flop_cards, live_turns, turn_card, river_cards,
    ranges_in, flop_regret_in, strength_in, turn_regret, index_in, keep_in,
    new_turn, sums, copies, root,
    ranges, flop_regret, strength, index, keep,
    regrets, wides, lanes, alives, columnses, founds, backs, spreads, total, one_total, blank,
    small_sems, keep_sems, in_sems, out_sems,
):
    me = lax.axis_index("turn")
    count = live_turns[0, me]
    steps = (count + SIDES - 1) // SIDES
    used = SIDES * steps

    def regret_copy(slot, b):
        return pltpu.make_async_copy(
            turn_regret.at[0, jnp.minimum(slot, TS - 1), :, b],
            regrets.at[slot, b // 2, pl.ds((b % 2) * 4, 4)],
            in_sems.at[slot, b],
        )

    def result_copy(slot, b):
        return pltpu.make_async_copy(
            regrets.at[slot, b // 2, pl.ds((b % 2) * 4, 4)],
            new_turn.at[0, slot, :, b],
            out_sems.at[slot, b],
        )

    def blank_copy(slot):
        return pltpu.make_async_copy(blank, new_turn.at[0, slot], out_sems.at[slot, 0])

    small = [
        pltpu.make_async_copy(source, target, small_sems.at[n])
        for n, (source, target) in enumerate(
            [
                (ranges_in, ranges),
                (flop_regret_in, flop_regret),
                (index_in, index),
                (strength_in, strength),
            ]
        )
    ]
    masks = [
        pltpu.make_async_copy(
            keep_in.at[pl.ds(start, ROWS)],
            keep.at[pl.ds(start, ROWS)],
            keep_sems.at[n],
        )
        for n, (start, rows) in enumerate(BLOCKS)
    ]
    for copy in small:
        copy.start()
    for b in range(A):
        regret_copy(0, b).start()
    for copy in masks:
        copy.start()

    def fetch(slot, carry):
        for b in range(A):
            regret_copy(slot, b).start()
        return carry

    lax.fori_loop(1, used + 1, fetch, 0)
    blank[...] = jnp.zeros_like(blank)

    def clear(slot, carry):
        blank_copy(slot).start()
        return carry

    lax.fori_loop(used, TS, clear, 0)
    for ref in wides + backs:
        ref[...] = jnp.zeros_like(ref)
    total[...] = jnp.zeros_like(total)
    one_total[...] = jnp.zeros_like(one_total)
    for copy in small:
        copy.wait()

    regrets_flop = flop_regret[0]
    sigma_flop = regrets_flop / jnp.sum(regrets_flop, axis=0, keepdims=True)
    reach_zero = rounded(ranges[0:1, :] * sigma_flop)
    for wide in wides:
        wide[1, 0:4, :H] = reach_zero
    first_card, second_card, third_card = (flop_cards[0, n] for n in range(3))
    first_card, second_card = jnp.minimum(first_card, second_card), jnp.maximum(first_card, second_card)
    second_card, third_card = jnp.minimum(second_card, third_card), jnp.maximum(second_card, third_card)
    first_card, second_card = jnp.minimum(first_card, second_card), jnp.maximum(first_card, second_card)
    row = lax.broadcasted_iota(jnp.int32, (8, 1), 0)
    upper = row < 4
    pots = []
    for k in range(2):
        column = jnp.zeros((8, 1), jnp.float32)
        for n in range(8):
            column = jnp.where(row == n, float(pot[n % 4, 2 * k + n // 4]), column)
        pots.append(column)
    def prepare(slot, side):
        source = jnp.minimum(slot, TS - 1)
        wide, lane, alive, columns, spread = wides[side], lanes[side], alives[side], columnses[side], spreads[side]
        for b in range(A):
            regret_copy(slot, b).wait()
        first, second = regrets[slot, 0], regrets[slot, 1]
        summed = first + second
        inverse = 1.0 / (summed + swap_halves(summed))
        sigma_first, sigma_second = first * inverse, second * inverse
        second_range = ranges[1:2, :]
        weight = (
            rounded(second_range * sigma_first) * pots[0]
            + rounded(second_range * sigma_second) * pots[1]
        )
        weight = weight + swap_halves(weight)
        wide[0, :, :H] = jnp.where(upper, weight, weight - rounded(weight))
        spreading = sigma_first * pots[0] + sigma_second * pots[1]
        spread[...] = spreading + swap_halves(spreading)
        wide[1, 4:6, :H] = strength[0, source] * BIG

        dead, card = [], turn_card[0, source]
        for flop_card in (first_card, second_card, third_card):
            dead.append(jnp.minimum(flop_card, card))
            card = jnp.maximum(flop_card, card)
        dead.append(card)
        low, high = index[0], index[1]
        for card in dead:
            low = low + (low >= card).astype(jnp.int32)
            high = high + (high >= card).astype(jnp.int32)
        lane[0] = ((low * (2 * CARDS - 1 - low)) >> 1) + high - low - 1
        for r in range(RIV):
            river = river_cards[0, r, source]
            alive[r] = jnp.where((low == river) | (high == river), 0.0, -1.0)
        low, high = index[2], index[3]
        lost = (low == dead[0]) | (high == dead[0])
        for card in dead[1:]:
            lost = lost | (low == card) | (high == card)
        less_low, less_high = jnp.zeros_like(low), jnp.zeros_like(high)
        for card in dead:
            less_low = less_low + (low > card).astype(jnp.int32)
            less_high = less_high + (high > card).astype(jnp.int32)
        low, high = low - less_low, high - less_high
        place = ((low * (2 * LEFT - 1 - low)) >> 1) + high - low - 1
        lane[1] = jnp.where(lost, -1, place)

        packed = [[], []]
        for k in range(CP // 128):
            offset = jnp.broadcast_to(lane[0, k : k + 1, :], (8, 128)) - 128 * k
            spot = offset & 127
            for group in range(2):
                parts = [
                    jnp.take_along_axis(
                        wide[group, :, 128 * (k + m) : 128 * (k + m + 1)], spot, axis=1
                    )
                    for m in range(3)
                ]
                packed[group].append(
                    jnp.where(offset < 128, parts[0], jnp.where(offset < 256, parts[1], parts[2]))
                )
        columns[...] = jnp.concatenate(packed[1], axis=1).T
        given = []
        for r in range(RIV):
            pieces = []
            for k in range(CP // 128):
                mask = -alive[r, k : k + 1, :]
                zeros = jnp.where(upper, packed[1][k], swap_halves(packed[1][k]))
                pieces.append(
                    jnp.concatenate([packed[0][k] * mask, zeros * mask], axis=0).astype(jnp.bfloat16)
                )
            given.append(jnp.concatenate(pieces, axis=1))
        return packed, given

    def multiply(side, packed, given):
        columns, found = columnses[side], founds[side]
        for start, rows in BLOCKS:
            own = [
                jnp.broadcast_to(columns[start : start + rows, 4 + r : 5 + r], (rows, 128))
                for r in range(RIV)
            ]
            for other in range(0, CP, BLOCK):
                stop = min(other + BLOCK, CP)
                most = keep[start : start + rows, other:stop]
                least = -most
                for r in range(RIV):
                    gap = jnp.concatenate(
                        [
                            own[r] - packed[1][k][4 + r : 5 + r, :]
                            for k in range(other // 128, stop // 128)
                        ],
                        axis=1,
                    ).astype(jnp.bfloat16)
                    outcome = jnp.maximum(jnp.minimum(gap, most), least)
                    gave = jnp.dot(
                        given[r][:, start : start + rows], outcome,
                        preferred_element_type=jnp.float32,
                    )
                    if start == 0:
                        found[r, :, other:stop] = gave
                    else:
                        found[r, :, other:stop] += gave

    def finish(slot, side, live):
        lane, alive, found = lanes[side], alives[side], founds[side]
        back, spread = backs[side], spreads[side]
        merged = []
        for k in range(CP // 128):
            values = [
                found[r, :, 128 * k : 128 * (k + 1)] * alive[r, k : k + 1, :] for r in range(RIV)
            ]
            values = values[0] + values[1]
            merged.append(
                jnp.where(upper, values[0:8] + swap_halves(values[0:8]), values[8:16])
            )
        for k in range(HP // 128):
            place = jnp.broadcast_to(lane[1, k : k + 1, :], (8, 128))
            spot = place & 127
            result = jnp.zeros((8, 128), jnp.float32)
            for m in range(max(0, k - 2), min(k + 1, CP // 128)):
                part = jnp.take_along_axis(merged[m], spot, axis=1)
                result = jnp.where((place >> 7) == m, part, result)
            if live is not None:
                result = result * live
            total[:, 128 * k : 128 * (k + 1)] += result
            back[:, 128 * k : 128 * (k + 1)] = jnp.where(upper, swap_halves(result), result)
        against = back[:, :H]
        spreading = spread[...]
        one_total[...] += against * spreading
        for k in range(2):
            updated = jnp.maximum(regrets[slot, k] + against * (pots[k] - spreading), 0.0)
            regrets[slot, k] = updated if live is None else updated * live
        for b in range(A):
            result_copy(slot, b).start()


    def group_step(group, carry):
        slots = [SIDES * group + side for side in range(SIDES)]
        ready = carry
        for side in range(SIDES):
            following = prepare(slots[side] + 1, (side + 1) % SIDES)
            multiply(side, *ready)
            ready = following
            live = (slots[side] < count).astype(jnp.float32) if side else None
            finish(slots[side], side, live)
        return ready

    first = prepare(0, 0)
    for copy in masks:
        copy.wait()
    lax.fori_loop(0, steps, group_step, first)
    whole = total[0:4, :H]
    sums[...] = whole
    scale = 1.0 / (TURNS * FLOPS)
    parts = jnp.concatenate(
        [
            jnp.sum(sigma_flop * whole, axis=0, keepdims=True) * scale,
            jnp.sum(one_total[0:4, :], axis=0, keepdims=True) * scale,
        ],
        axis=0,
    )
    for n in range(NEAR):
        copies[n] = parts
    root[...] = sigma_flop

    def settle(slot, carry):
        for b in range(A):
            result_copy(slot, b).wait()
        return carry

    lax.fori_loop(0, used, settle, 0)

    def settle_blank(slot, carry):
        blank_copy(slot).wait()
        return carry

    lax.fori_loop(used, TS, settle_blank, 0)


def group_sum(copies, axis, groups):
    return jnp.sum(
        lax.all_to_all(copies, axis, 0, 0, axis_index_groups=groups, tiled=True), axis=0
    )


def flip_sum(x, axis, flip):
    size = lax.axis_size(axis)
    return x + lax.ppermute(x, axis, [(n, n ^ flip) for n in range(size)])


def on_device(
    ranges, flop_regret, flop_cards, live_turns, turn_card, river_cards, strength, turn_regret
):
    index, disjoint = tables()
    smem = pl.BlockSpec(memory_space=pltpu.SMEM)
    vmem = pl.BlockSpec(memory_space=pltpu.VMEM)
    hbm = pl.BlockSpec(memory_space=pltpu.HBM)
    new_turn, sums, copies, sigma_flop = pl.pallas_call(
        kernel,
        out_shape=(
            jax.ShapeDtypeStruct(turn_regret.shape, jnp.float32),
            jax.ShapeDtypeStruct((A, H), jnp.float32),
            jax.ShapeDtypeStruct((NEAR, 2, H), jnp.float32),
            jax.ShapeDtypeStruct((A, H), jnp.float32),
        ),
        in_specs=[smem] * 4 + [hbm] * 6,
        out_specs=(hbm, vmem, vmem, vmem),
        scratch_shapes=[
            pltpu.VMEM((2, H), jnp.float32),
            pltpu.VMEM((1, A, H), jnp.float32),
            pltpu.VMEM((1, TS, RIV, H), jnp.float32),
            pltpu.VMEM((4, 16, 128), jnp.int32),
            pltpu.VMEM((CP, CP), jnp.bfloat16),
            pltpu.VMEM((TS + 1, 2, 8, H), jnp.float32),
            [pltpu.VMEM((2, 8, HP), jnp.float32)] * SIDES,
            [pltpu.VMEM((2, 16, 128), jnp.int32)] * SIDES,
            [pltpu.VMEM((RIV, 16, 128), jnp.float32)] * SIDES,
            [pltpu.VMEM((CP, 8), jnp.float32)] * SIDES,
            [pltpu.VMEM((RIV, 16, CP), jnp.float32)] * SIDES,
            [pltpu.VMEM((8, HP), jnp.float32)] * SIDES,
            [pltpu.VMEM((8, H), jnp.float32)] * SIDES,
            pltpu.VMEM((8, HP), jnp.float32),
            pltpu.VMEM((8, H), jnp.float32),
            pltpu.VMEM((A, A, H), jnp.float32),
            pltpu.SemaphoreType.DMA((4,)),
            pltpu.SemaphoreType.DMA((len(BLOCKS),)),
            pltpu.SemaphoreType.DMA((TS + 1, A)),
            pltpu.SemaphoreType.DMA((TS, A)),
        ],
        compiler_params=pltpu.CompilerParams(vmem_limit_bytes=60 * 1024 * 1024),
        name="subtrees",
    )(
        flop_cards, live_turns, turn_card, jnp.swapaxes(river_cards, 1, 2),
        ranges, flop_regret, strength, turn_regret, jnp.asarray(index), jnp.asarray(disjoint),
    )
    regrets_flop = flop_regret[0]
    others = [lax.ppermute(sums, "turn", [(n, n ^ flip) for n in range(4)]) for flip in (1, 2, 3)]
    if lax.axis_size("flop") == FLOPS:
        near = np.arange(4 * FLOPS).reshape(8, 4, 2, 4).transpose(0, 2, 1, 3).reshape(16, NEAR)
        far = np.arange(FLOPS).reshape(8, 8).T
        root_value = group_sum(copies, ("flop", "turn"), near.tolist())
        root_value = flip_sum(root_value, "flop", 1)
        root_value, others = lax.optimization_barrier((root_value, others))
        root_value = group_sum(
            jnp.broadcast_to(root_value, (8, *root_value.shape)), "flop", far.tolist()
        )
    else:
        root_value = lax.psum(copies[0], "turn")
    action_value = ((sums + others[0]) + (others[1] + others[2])) / TURNS
    node_zero = jnp.sum(sigma_flop * action_value, axis=0)
    new_flop = jnp.maximum(regrets_flop + action_value - node_zero[None, :], 0.0)
    return (new_flop[None], new_turn, root_value)


def solution(mesh):
    placed = (
        P(),
        P("flop", None, None),
        P("flop", None),
        P("flop", None),
        P("flop", "turn"),
        P("flop", "turn", None),
        P("flop", "turn", None, None),
        P("flop", "turn", None, None, None),
    )
    return jax.shard_map(
        on_device,
        mesh=mesh,
        in_specs=placed,
        out_specs=(P("flop", None, None), P("flop", "turn", None, None, None), P()),
        check_vma=False,
    )
```
